32 devices in a mesh: dp: 8 (over z, y), tensor: 4 (over x, core).
Axes of the slice: x: 2, y: 2, z: 4, core: 2. Of those that a mesh axis runs over, the one named last changes fastest.
Arguments:
- tokens: float32 [8192, 768], P(('dp', 'tensor')), may hold values from -6 to 6
- segments: int32 [8192], P('dp'), may hold values from 0 to 4, as said below
- routes: int32 [8192, 1], P('dp'), may hold values from 0 to 3
- cotangent: float32 [8192, 768], P(('dp', 'tensor')), may hold values from -6 to 6
- gain_attn: bfloat16 [768], replicated, may hold values from 0.5 to 1.5
- w_query: bfloat16 [768, 768], P('dp', 'tensor'), may hold values from -0.21875 to 0.21875
- w_key: bfloat16 [768, 768], P('dp', 'tensor'), may hold values from -0.21875 to 0.21875
- w_value: bfloat16 [768, 768], P('dp', 'tensor'), may hold values from -0.21875 to 0.21875
- w_output: bfloat16 [768, 768], P('tensor', 'dp'), may hold values from -0.875 to 0.875
- rel_table: bfloat16 [32, 12], replicated, may hold values from -4 to 4
- gain_ffn: bfloat16 [768], replicated, may hold values from 0.5 to 1.5
- w_router: bfloat16 [768, 4], replicated, may hold values from -0.15625 to 0.15625
- w_inner: bfloat16 [4, 768, 3072], P(None, 'dp', 'tensor'), may hold values from -0.21875 to 0.21875
- w_outer: bfloat16 [4, 3072, 768], P(None, 'tensor', 'dp'), may hold values from -0.3125 to 0.3125
Outputs:
- output: float32 [8192, 768], P(('dp', 'tensor'))
- grad_tokens: float32 [8192, 768], P(('dp', 'tensor'))
- grad_gain_attn: float32 [768], replicated
- grad_query: float32 [768, 768], P('dp', 'tensor')
- grad_key: float32 [768, 768], P('dp', 'tensor')
- grad_value: float32 [768, 768], P('dp', 'tensor')
- grad_output_proj: float32 [768, 768], P('tensor', 'dp')
- grad_table: float32 [32, 12], replicated
- grad_gain_ffn: float32 [768], replicated
- grad_router: float32 [768, 4], replicated
- grad_inner: float32 [4, 768, 3072], P(None, 'dp', 'tensor')
- grad_outer: float32 [4, 3072, 768], P(None, 'tensor', 'dp')
The draws below stay inside these ranges and needn't reach their ends.
Inputs may be any that keep to these rules, and one draw needn't show every extreme that they name: `segments`: segment numbers start at 0 in each sequence of 1024 tokens and never fall within it; each sequence holds five documents.
All inputs are finite; a program needn't handle non-finite values.
Results may differ from the reference program's by a relative error of at most 0.018.
Values may be sent and summed in bfloat16 or wider, within the bound.
A program may use at most 768 MiB of HBM per device.

```python
import math
import jax
import jax.numpy as jnp
import numpy as np
from jax import lax

D = 768
H = 12
HD = 64
FF = 3072
NBKT = 32
MAXD = 128
E = 4
WIN = 1024
QB = 512
BLK = 128
TOK_DEV = 256
SEQ = 1024
TOKENS = 8192
N_DP = 8


def draw_segments(key, part):
    key = jax.random.fold_in(key, 11)
    groups = TOKENS // SEQ
    key_one, key_two, key_three, key_four = jax.random.split(key, 4)
    half = TOK_DEV // 2
    first_cut = jax.random.randint(key_one, (groups, 1), 1, half)
    second_cut = jax.random.randint(key_two, (groups, 1), half + 1, TOK_DEV)
    third_cut = jax.random.randint(key_three, (groups, 1), 3 * TOK_DEV + 1, SEQ - half)
    fourth_cut = jax.random.randint(key_four, (groups, 1), SEQ - half + 1, SEQ)
    position = jnp.arange(SEQ, dtype=jnp.int32)[None, :]
    starts = (position == first_cut) | (position == second_cut) | (position == third_cut) | (position == fourth_cut)
    return jnp.cumsum(starts.astype(jnp.int32), axis=1).reshape(TOKENS).astype(jnp.int32)


def level_of(own_key, dims, cuts, low, top_value):
    loudness = 1.0
    for dim, blocks in cuts:
        heights = jax.random.uniform(jax.random.fold_in(jax.random.fold_in(own_key, 6), dim), (blocks,), jnp.float32, low / len(cuts), top_value / len(cuts))
        loudness = loudness * jnp.repeat(jnp.exp(heights), dims[dim] // blocks).reshape((-1,) + (1,) * (len(dims) - 1 - dim))
    return loudness


def picks_of(stream_key, rows, number_of, top, lift):
    order = jax.random.permutation(jax.random.fold_in(stream_key, 1), number_of)
    pull = order
    for power in range(3):
        pull = pull * pull // number_of
    pull = pull * lift // number_of
    chance = jax.random.randint(jax.random.fold_in(stream_key, 2), (rows, number_of), 0, 4096) + pull
    fixed_rows = jax.random.permutation(jax.random.fold_in(stream_key, 3), rows)[jnp.arange(number_of) % rows]
    chance = jnp.where(jnp.arange(rows)[:, None] == fixed_rows[None, :], 1 << 14, chance)
    priority = chance * number_of + jnp.arange(number_of)
    return lax.top_k(priority.astype(jnp.int32), top)[1].astype(jnp.int32)


def noise(rng, shape, spread, limit, cuts=(), held_as=jnp.bfloat16):
    values = jax.random.normal(rng, shape, jnp.float32) * spread
    if len(cuts) > 0:
        values = level_of(rng, shape, cuts, -0.22, 0.18) * values
    return jnp.clip(values, min=-limit, max=limit).astype(held_as)


def setup_inputs(seed: int = 0) -> dict:
    splits = jax.random.split(jax.random.key(seed), 15)
    tokens = noise(splits[0], (TOKENS, D), 1.0, 6.0, ((0, 32),), jnp.float32)
    segments = draw_segments(jax.random.fold_in(splits[14], 71), 0)
    routes = picks_of(splits[2], TOKENS, E, 1, 2048)
    cotangent = noise(splits[3], (TOKENS, D), 1.0, 6.0, ((0, 32),), jnp.float32)
    gain_attn = jnp.clip(1.0 + 0.1 * jax.random.normal(splits[4], (D,), jnp.float32), 0.5, 1.5).astype(jnp.bfloat16)
    w_query = noise(splits[5], (D, D), D ** -0.5, 0.21875, ((0, 8), (1, 4)))
    w_key = noise(splits[6], (D, D), D ** -0.5, 0.21875, ((0, 8), (1, 4)))
    w_value = noise(splits[7], (D, D), D ** -0.5, 0.21875, ((0, 8), (1, 4)))
    w_output = noise(splits[8], (D, D), (D // 16) ** -0.5, 0.875, ((0, 4), (1, 8)))
    rel_table = noise(splits[9], (NBKT, H), 1.0, 4.0)
    gain_ffn = jnp.clip(1.0 + 0.1 * jax.random.normal(splits[10], (D,), jnp.float32), 0.5, 1.5).astype(jnp.bfloat16)
    w_router = noise(splits[11], (D, E), (2 * D) ** -0.5, 0.15625)
    w_inner = noise(splits[12], (E, D, FF), D ** -0.5, 0.21875, ((1, 8), (2, 4)))
    w_outer = noise(splits[13], (E, FF, D), (FF // 8) ** -0.5, 0.3125, ((1, 4), (2, 8)))
    return {"tokens": tokens, "segments": segments, "routes": routes, "cotangent": cotangent, "gain_attn": gain_attn, "w_query": w_query, "w_key": w_key, "w_value": w_value, "w_output": w_output, "rel_table": rel_table, "gain_ffn": gain_ffn, "w_router": w_router, "w_inner": w_inner, "w_outer": w_outer}


EPSILON = 1e-06
NEG_LARGE = -1e+30

@jax.custom_vjp
def low(v):
    return lax.optimization_barrier(v.astype(jnp.bfloat16)).astype(jnp.float32)

@jax.custom_vjp
def low_back(v):
    return v

def low_keep(v):
    return (low(v), None)

def low_pass(kept, grad):
    return (grad,)

def back_keep(v):
    return (v, None)

def back_low(kept, grad):
    return (low(grad),)
low.defvjp(low_keep, low_pass)
low_back.defvjp(back_keep, back_low)

def bucket_numbers(window, buckets, far_distance):
    distance = np.arange(window)
    exact_part = buckets // 2
    safe_distance = np.maximum(distance, 1) * 1.0
    log_part = exact_part + np.floor(np.log(safe_distance / exact_part) / np.log(far_distance / exact_part) * (buckets - exact_part)).astype(np.int32)
    log_part = np.minimum(log_part, buckets - 1)
    return np.where(distance < exact_part, distance, log_part).astype(np.int32)

def band_tables():
    key_span = QB + WIN
    distance = np.arange(QB)[:, None] + WIN - np.arange(key_span)[None, :]
    in_band = (distance >= 0) & (distance < WIN)
    clipped = np.clip(distance, 0, WIN - 1)
    bucket_list = bucket_numbers(WIN, NBKT, MAXD)
    return (in_band, bucket_list[clipped])

def rms_apply(values, gain_vec):
    inverse = lax.rsqrt(lax.optimization_barrier(jnp.mean(values * values, axis=-1, keepdims=True)) + EPSILON)
    return values * inverse * gain_vec

def gelu_tanh(values):
    return jax.nn.gelu(values, approximate=True)

def exact_dot(left, right):
    return jnp.dot(left, right, precision=lax.Precision.HIGHEST)

def expert_slots(route_ids):
    length = route_ids.shape[0]
    chosen = (route_ids[:, None] == jnp.arange(E, dtype=jnp.int32)[None, :]).astype(jnp.int32)
    before = jnp.cumsum(chosen, axis=0) - chosen
    rank_in = lax.optimization_barrier(jnp.sum(before * chosen, axis=1))
    counts = lax.optimization_barrier(jnp.sum(chosen, axis=0))
    padded = (counts + BLK - 1) // BLK * BLK
    starts = jnp.cumsum(padded) - padded
    slot_of_token = (lax.optimization_barrier(jnp.sum(starts[None, :] * chosen, axis=1)) + rank_in).astype(jnp.int32)
    capacity = length + E * BLK
    token_of_slot = jnp.full((capacity,), length, jnp.int32).at[slot_of_token].set(jnp.arange(length, dtype=jnp.int32))
    block_first = jnp.arange(capacity // BLK, dtype=jnp.int32) * BLK
    ends = (starts + padded).astype(jnp.int32)
    block_expert = jnp.minimum(lax.optimization_barrier(jnp.sum((block_first[:, None] >= ends[None, :]).astype(jnp.int32), axis=1)), E - 1).astype(jnp.int32)
    return (slot_of_token, token_of_slot, block_expert)

def layer(tokens, gain_attn, w_query, w_key, w_value, w_output, rel_table, gain_ffn, w_router, w_inner, w_outer, segments, route_ids):
    seq_len = tokens.shape[0]
    key_span = QB + WIN
    score_scale = 1.0 / math.sqrt(HD)
    normed_attn = low(rms_apply(tokens, gain_attn))
    queries = low_back(low(exact_dot(normed_attn, w_query)))
    key_all = low_back(low(exact_dot(normed_attn, w_key)))
    value_all = low_back(low(exact_dot(normed_attn, w_value)))
    in_band, bucket_ids = band_tables()
    band_mask = jnp.asarray(in_band)
    bias_block = jnp.transpose(rel_table[jnp.asarray(bucket_ids)], (2, 0, 1))
    keys_pad = jnp.pad(key_all, ((WIN, 0), (0, 0)))
    values_pad = jnp.pad(value_all, ((WIN, 0), (0, 0)))
    segs_pad = jnp.pad(segments, (WIN, 0), constant_values=-1)

    def attend_block(block_index):
        row_start = (block_index * QB).astype(jnp.int32)
        query_rows = lax.dynamic_slice_in_dim(queries, row_start, QB, 0).reshape(QB, H, HD)
        key_rows = lax.dynamic_slice_in_dim(keys_pad, row_start, key_span, 0).reshape(key_span, H, HD)
        value_rows = lax.dynamic_slice_in_dim(values_pad, row_start, key_span, 0).reshape(key_span, H, HD)
        seg_query = lax.dynamic_slice_in_dim(segments, row_start, QB, 0)
        seg_key = lax.dynamic_slice_in_dim(segs_pad, row_start, key_span, 0)
        allowed = ((seg_query[:, None] == seg_key[None, :]) & band_mask)[None]
        scores = jnp.einsum('qhd,khd->hqk', query_rows, key_rows, precision=lax.Precision.HIGHEST) * score_scale + bias_block
        scores = low_back(scores)
        masked = jnp.where(allowed, scores, NEG_LARGE)
        row_peak = lax.optimization_barrier(jnp.max(masked, axis=-1, keepdims=True))
        exp_terms = jnp.where(allowed, jnp.exp(masked - row_peak), 0.0)
        probabilities = exp_terms / lax.optimization_barrier(jnp.sum(exp_terms, axis=-1, keepdims=True))
        weights_low = low(probabilities)
        context_rows = jnp.einsum('hqk,khd->qhd', weights_low, value_rows, precision=lax.Precision.HIGHEST)
        return context_rows.reshape(QB, D)
    blocks = lax.map(jax.checkpoint(attend_block), jnp.arange(seq_len // QB, dtype=jnp.int32))
    context = low_back(low(blocks.reshape(seq_len, D)))
    attended = tokens + low_back(exact_dot(context, w_output))
    normed_ffn = low(rms_apply(attended, gain_ffn))
    route_mask = (route_ids[:, None] == jnp.arange(E, dtype=jnp.int32)[None, :]).astype(jnp.float32)
    gate_weight = lax.optimization_barrier(jnp.sum(jax.nn.softmax(exact_dot(normed_ffn, w_router), axis=-1) * route_mask, axis=-1))
    slot_of_token, token_of_slot, block_expert = expert_slots(route_ids)
    padded_rows = jnp.concatenate([normed_ffn, jnp.zeros((1, D), jnp.float32)], axis=0)
    slot_rows = padded_rows[token_of_slot].reshape(-1, BLK, D)

    def expert_block(inputs):
        rows_in, expert_id = inputs
        inner_act = low_back(exact_dot(rows_in, w_inner[expert_id]))
        active = low(gelu_tanh(inner_act))
        return exact_dot(active, w_outer[expert_id])
    slot_out = lax.map(jax.checkpoint(expert_block), (slot_rows, block_expert))
    expert_out = low_back(slot_out.reshape(-1, D)[slot_of_token])
    return attended + gate_weight[:, None] * expert_out

def reference(tokens, segments, routes, cotangent, gain_attn, w_query, w_key, w_value, w_output, rel_table, gain_ffn, w_router, w_inner, w_outer):
    weights_all = tuple((weight_arg.astype(jnp.float32) for weight_arg in (gain_attn, w_query, w_key, w_value, w_output, rel_table, gain_ffn, w_router, w_inner, w_outer)))
    group_tokens = tokens.reshape(N_DP, SEQ, D)
    group_segments = segments.reshape(N_DP, SEQ)
    group_routes = routes.reshape(N_DP, SEQ)
    group_cot = cotangent.reshape(N_DP, SEQ, D)

    def one_sequence(totals, inputs):
        seq_tokens, seq_segments, seq_routes, seq_cot = inputs

        def forward(values, *weights_in):
            return layer(values, *weights_in, seq_segments, seq_routes)
        result, pullback = jax.vjp(forward, seq_tokens, *weights_all)
        gradients = pullback(seq_cot)
        totals = tuple((acc_total + grad_piece for acc_total, grad_piece in zip(totals, gradients[1:])))
        return (totals, (result, gradients[0]))
    zero_totals = tuple((jnp.zeros_like(weight_arg) for weight_arg in weights_all))
    totals, (results, grad_seq) = lax.scan(one_sequence, zero_totals, (group_tokens, group_segments, group_routes, group_cot))
    return (results.reshape(TOKENS, D), grad_seq.reshape(TOKENS, D), totals[0], totals[1], totals[2], totals[3], totals[4], totals[5], totals[6], totals[7], totals[8], totals[9])
```

```python
import functools
import math

import jax
import jax.numpy as jnp
import numpy as np
from jax import lax
from jax.experimental import pallas as pl
from jax.experimental.pallas import tpu as pltpu
from jax.sharding import PartitionSpec as P

HD = 64
NBKT = 32
MAXD = 128
E = 4
WIN = 1024
QT = 256
HALF = 128
ROWS = 256

EPSILON = 1e-06
NEG_LARGE = -1e30
BF = jnp.bfloat16
F32 = jnp.float32
VMEM_MAX = 56 * 1024 * 1024


def bucket_numbers(window, buckets, far_distance):
    distance = np.arange(window)
    exact_part = buckets // 2
    safe_distance = np.maximum(distance, 1) * 1.0
    log_part = exact_part + np.floor(
        np.log(safe_distance / exact_part)
        / np.log(far_distance / exact_part)
        * (buckets - exact_part)
    ).astype(np.int32)
    log_part = np.minimum(log_part, buckets - 1)
    return np.where(distance < exact_part, distance, log_part).astype(np.int32)


BUCKETS = bucket_numbers(WIN, NBKT, MAXD)
FIRST = [int(np.argmax(BUCKETS == b)) for b in range(NBKT)]
NEAR = FIRST[NBKT - 1]


def nn(a, b):
    return lax.dot_general(a, b, (((1,), (0,)), ((), ())), preferred_element_type=F32)


def nt(a, b):
    return lax.dot_general(a, b, (((1,), (1,)), ((), ())), preferred_element_type=F32)


def tn(a, b):
    return lax.dot_general(a, b, (((0,), (0,)), ((), ())), preferred_element_type=F32)


def iota(shape, dim):
    return lax.broadcasted_iota(jnp.int32, shape, dim)


def gather_dp(shard, size):
    rows = shard.shape[0]
    if size != 8:
        return [lax.all_gather(shard, "dp", axis=0, tiled=True)], jnp.zeros((1,), jnp.int32)
    me = lax.axis_index("dp")
    z, y = me // 2, me % 2
    own = [shard] + [lax.ppermute(shard, "dp", z_shift(k)) for k in (1, 2, 3)]
    far = [lax.ppermute(piece, "dp", Y_SWAP) for piece in own]
    ids = [((z + 4 - k) % 4) * 2 + y for k in range(4)]
    ids += [((z + 4 - k) % 4) * 2 + 1 - y for k in range(4)]
    return own + far, (jnp.stack(ids) * rows).astype(jnp.int32)


Y_SWAP = [(d, d ^ 1) for d in range(8)]


def z_shift(k):
    return [(z * 2 + y, ((z + k) % 4) * 2 + y) for z in range(4) for y in range(2)]


def send_offsets(rows, size):
    if size != 8:
        return jnp.zeros((1,), jnp.int32)
    me = lax.axis_index("dp")
    z, y = me // 2, me % 2
    ids = [((z + k) % 4) * 2 + y for k in range(4)] + [((z + k) % 4) * 2 + 1 - y for k in range(4)]
    return (jnp.stack(ids) * rows).astype(jnp.int32)


def reduce_dp(parts, size):
    if size != 8:
        return lax.psum_scatter(parts[0][0], "dp", scatter_dimension=0, tiled=True).astype(F32)
    mine, other = parts
    got = lax.ppermute(other, "dp", Y_SWAP)
    total = mine[0].astype(F32) + got[0].astype(F32)
    arrived = []
    for k in (1, 2, 3):
        pair = (mine[k].astype(F32) + got[k].astype(F32)).astype(BF)
        arrived.append(lax.ppermute(pair, "dp", z_shift(k)))
    for piece in arrived:
        total = total + piece.astype(F32)
    return total


def plan_kernel(route_ref, slot_row_ref, slot_col_ref, plan_ref):
    length = route_ref.shape[1]
    route = route_ref[...]
    chosen = jnp.where(iota((8, length), 0) == route, 1.0, 0.0).astype(F32)
    upper = jnp.where(iota((length, length), 0) < iota((length, length), 1), 1.0, 0.0)
    before = nn(chosen.astype(BF), upper.astype(BF))
    rank = jnp.sum(chosen * before, axis=0, keepdims=True)
    start = jnp.int32(0)
    base = jnp.zeros((1, length), F32)
    for e in range(E):
        here = route == e
        count = jnp.sum(jnp.where(here, 1, 0))
        tiles = (count + (ROWS - 1)) // ROWS
        plan_ref[e] = tiles
        plan_ref[E + e] = start
        base = base + jnp.where(here, start.astype(F32), 0.0)
        start = start + tiles * ROWS
    slots = jnp.broadcast_to(rank + base, (8, length))
    slot_row_ref[...] = slots.astype(jnp.int32)
    slot_col_ref[...] = jnp.transpose(slots).astype(jnp.int32)


def make_plan(route_row):
    length = route_row.shape[1]
    return pl.pallas_call(
        plan_kernel,
        out_shape=(
            jax.ShapeDtypeStruct((8, length), jnp.int32),
            jax.ShapeDtypeStruct((length, 8), jnp.int32),
            jax.ShapeDtypeStruct((2 * E,), jnp.int32),
        ),
        in_specs=[pl.BlockSpec(memory_space=pltpu.VMEM)],
        out_specs=(
            pl.BlockSpec(memory_space=pltpu.VMEM),
            pl.BlockSpec(memory_space=pltpu.VMEM),
            pl.BlockSpec(memory_space=pltpu.SMEM),
        ),
        compiler_params=pltpu.CompilerParams(vmem_limit_bytes=VMEM_MAX),
        name="route_plan",
    )(route_row)


def fill_bias(bias_ref, table_ref, heads):
    step = iota((HALF, HALF), 1) - iota((HALF, HALF), 0)
    for side in range(2):
        distance = step + side * HALF
        tiles = [jnp.full((HALF, HALF), table_ref[h, NBKT - 1], F32) for h in range(heads)]
        for b in reversed(range(NBKT - 1)):
            below = distance < FIRST[b + 1]
            tiles = [jnp.where(below, table_ref[h, b], tiles[h]) for h in range(heads)]
        for h in range(heads):
            bias_ref[h, side] = tiles[h]


def biased_scores(raw, gap, h, bias_ref, table_ref, first_key, key_start, query_block):
    far = table_ref[h, NBKT - 1]
    keys = key_start + iota((QT, QT), 0)
    if gap >= 2:
        return jnp.where(keys >= first_key, raw + far, NEG_LARGE)
    diag, near = bias_ref[h, 0], bias_ref[h, 1]
    const = jnp.full((HALF, HALF), far, F32)
    if gap == 1:
        tile = jnp.concatenate(
            [
                jnp.concatenate([const, const], axis=1),
                jnp.concatenate([near, const], axis=1),
            ],
            axis=0,
        )
        return jnp.where(keys >= first_key, raw + tile, NEG_LARGE)
    tile = jnp.concatenate(
        [jnp.concatenate([diag, near], axis=1), jnp.concatenate([const, diag], axis=1)], axis=0
    )
    causal = iota((QT, QT), 0) <= iota((QT, QT), 1)
    return jnp.where((keys >= first_key) & causal, raw + tile, NEG_LARGE)


def load_rows(pieces, offsets_ref, whole, sem):
    rows = pieces[0].shape[0]
    copies = []
    for k, piece in enumerate(pieces):
        at = pl.ds(pl.multiple_of(offsets_ref[k], rows), rows)
        copies.append(pltpu.make_async_copy(piece, whole.at[at], sem.at[k]))
    for copy in copies:
        copy.start()
    return copies


def attend_kernel(heads, pieces, offsets_ref, table_ref, x_ref, first_ref, *refs):
    piece_refs = refs[:pieces]
    qkv_ref, ctx_ref, lse_ref, branch_ref, w_out_ref = refs[pieces : pieces + 5]
    w_ref, q_t, v_t, kn, bias_ref, s_ref, ctx_t, sem = refs[pieces + 5 :]
    width = heads * HD
    seq = x_ref.shape[0]
    copies = load_rows(piece_refs, offsets_ref, w_ref, sem)
    fill_bias(bias_ref, table_ref, heads)
    for copy in copies:
        copy.wait()
    w_out_ref[...] = w_ref[...]
    qkv = nn(x_ref[...], w_ref[:, : 3 * width]).astype(BF)
    qkv_ref[...] = qkv
    q_t[...] = jnp.transpose(qkv[:, :width]) * jnp.asarray(1.0 / math.sqrt(HD), BF)
    v_t[...] = jnp.transpose(qkv[:, 2 * width :])
    for h in range(heads):
        kn[h] = qkv[:, width + h * HD : width + (h + 1) * HD]
    for i in range(seq // QT):
        cols = slice(i * QT, (i + 1) * QT)
        first_key = first_ref[:, cols]
        for h in range(heads):
            band = slice(h * HD, (h + 1) * HD)
            q_blk = q_t[band, cols]
            peak = None
            for j in range(i + 1):
                raw = nn(kn[h, j * QT : (j + 1) * QT], q_blk)
                s = biased_scores(raw, i - j, h, bias_ref, table_ref, first_key, j * QT, i)
                s_ref[h, j] = s
                top = jnp.max(s, axis=0, keepdims=True)
                peak = top if peak is None else jnp.maximum(peak, top)
            total = jnp.zeros((1, QT), F32)
            acc = jnp.zeros((HD, QT), F32)
            for j in range(i + 1):
                p = jnp.exp(s_ref[h, j] - peak)
                total = total + jnp.sum(p, axis=0, keepdims=True)
                acc = acc + nn(v_t[band, j * QT : (j + 1) * QT], p.astype(BF))
            ctx_t[band, cols] = (acc / total).astype(BF)
            lse_ref[h : h + 1, cols] = peak + jnp.log(total)
    ctx = jnp.transpose(ctx_t[...])
    ctx_ref[...] = ctx
    branch_ref[...] = nt(ctx, w_ref[:, 3 * width :]).astype(BF)


def attend(x, pieces, offsets, table, first_key, heads):
    seq, model = x.shape
    width = heads * HD
    n = len(pieces)
    vmem = pl.BlockSpec(memory_space=pltpu.VMEM)
    smem = pl.BlockSpec(memory_space=pltpu.SMEM)
    return pl.pallas_call(
        functools.partial(attend_kernel, heads, n),
        out_shape=(
            jax.ShapeDtypeStruct((seq, 3 * width), BF),
            jax.ShapeDtypeStruct((seq, width), BF),
            jax.ShapeDtypeStruct((8, seq), F32),
            jax.ShapeDtypeStruct((seq, model), BF),
            jax.ShapeDtypeStruct((model, 4 * width), BF),
        ),
        in_specs=[smem, smem, vmem, vmem] + [pl.BlockSpec(memory_space=pl.ANY)] * n,
        out_specs=(vmem,) * 5,
        scratch_shapes=[
            pltpu.VMEM((model, 4 * width), BF),
            pltpu.VMEM((width, seq), BF),
            pltpu.VMEM((width, seq), BF),
            pltpu.VMEM((heads, seq, HD), BF),
            pltpu.VMEM((heads, 2, HALF, HALF), F32),
            pltpu.VMEM((heads, seq // QT, QT, QT), F32),
            pltpu.VMEM((width, seq), BF),
            pltpu.SemaphoreType.DMA((n,)),
        ],
        compiler_params=pltpu.CompilerParams(vmem_limit_bytes=VMEM_MAX),
        cost_estimate=pl.CostEstimate(flops=4 * 10**9, bytes_accessed=10**7, transcendentals=2 * 10**6),
        name="attend",
    )(offsets, table, x, first_key, *pieces)


def attend_back_kernel(
    heads, blocks, offs_ref, table_ref, d_ref, w_ref, qkv_ref, ctx_ref, lse_ref, first_ref, x_ref,
    rows_ref, diag_ref, *refs
):
    grads = refs[: len(blocks)]
    q_t, k_t, dc_t, kn, vn, qn, dcn, bias_ref, dq_t, dqkv, near_ref, delta_ref, acc_ref = refs[len(blocks) :]
    width = heads * HD
    seq = d_ref.shape[0]
    scale = jnp.asarray(1.0 / math.sqrt(HD), BF)
    fill_bias(bias_ref, table_ref, heads)
    d_rows = d_ref[...]
    ctx = ctx_ref[...]
    dc = nn(d_rows, w_ref[:, 3 * width :]).astype(BF)
    acc_ref[:, 3 * width :] = tn(d_rows, ctx)
    dct = jnp.transpose(dc)
    dc_t[...] = dct
    qkv = qkv_ref[...]
    q_t[...] = jnp.transpose(qkv[:, :width]) * scale
    k_t[...] = jnp.transpose(qkv[:, width : 2 * width])
    product = dct.astype(F32) * jnp.transpose(ctx).astype(F32)
    for h in range(heads):
        band = slice(h * HD, (h + 1) * HD)
        qn[h] = qkv[:, band] * scale
        kn[h] = qkv[:, width + h * HD : width + (h + 1) * HD]
        vn[h] = qkv[:, 2 * width + h * HD : 2 * width + (h + 1) * HD]
        dcn[h] = dc[:, band]
        delta_ref[h : h + 1] = jnp.sum(product[band], axis=0, keepdims=True)
    dq_t[...] = jnp.zeros_like(dq_t)
    near_ref[...] = jnp.zeros_like(near_ref)
    for j in range(seq // QT):
        keys = slice(j * QT, (j + 1) * QT)
        for h in range(heads):
            band = slice(h * HD, (h + 1) * HD)
            dk = jnp.zeros((QT, HD), F32)
            dv = jnp.zeros((QT, HD), F32)
            for i in range(j, seq // QT):
                cols = slice(i * QT, (i + 1) * QT)
                raw = nn(kn[h, keys], q_t[band, cols])
                s = biased_scores(raw, i - j, h, bias_ref, table_ref, first_ref[:, cols], j * QT, i)
                p = jnp.exp(s - lse_ref[h : h + 1, cols])
                dp = nn(vn[h, keys], dc_t[band, cols])
                ds = p * (dp - delta_ref[h : h + 1, cols])
                if i == j:
                    near_ref[h, 0] += ds[:HALF, :HALF] + ds[HALF:, HALF:]
                    near_ref[h, 1] += ds[:HALF, HALF:]
                elif i == j + 1:
                    near_ref[h, 1] += ds[HALF:, :HALF]
                ds = ds.astype(BF)
                dv = dv + nn(p.astype(BF), dcn[h, cols])
                dk = dk + nn(ds, qn[h, cols])
                dq_t[band, cols] += nn(k_t[band, keys], ds)
            dqkv[keys, width + h * HD : width + (h + 1) * HD] = dk.astype(BF)
            dqkv[keys, 2 * width + h * HD : 2 * width + (h + 1) * HD] = dv.astype(BF)
    dqkv[:, :width] = jnp.transpose((dq_t[...] * (1.0 / math.sqrt(HD))).astype(BF))
    d_qkv = dqkv[...]
    rows_ref[...] = nt(d_qkv, w_ref[:, : 3 * width]).astype(BF)
    acc_ref[:, : 3 * width] = tn(x_ref[...], d_qkv)
    scatter_rows(acc_ref, offs_ref, grads, blocks)
    key, query = iota((HALF, HALF), 0), iota((HALF, HALF), 1)
    lines = []
    for h in range(heads):
        both = near_ref[h, 0] + jnp.where(query < key, near_ref[h, 1], 0.0)
        for bit in range(7):
            turned = pltpu.roll(both, HALF - (1 << bit), 1)
            both = jnp.where((key >> bit) & 1 == 1, turned, both)
        lines.append(jnp.sum(both, axis=0, keepdims=True))
    lines += [jnp.zeros((8 - heads, HALF), F32)]
    diag_ref[...] = jnp.concatenate(lines, axis=0)


def scatter_rows(acc_ref, offs_ref, outs, blocks):
    k = 0
    for out, count in zip(outs, blocks):
        rows = out.shape[1]
        for b in range(count):
            at = pl.ds(pl.multiple_of(offs_ref[k], rows), rows)
            out[b] = acc_ref[at, :].astype(BF)
            k += 1


def attend_back(d_rows, w, qkv, ctx, lse, first_key, x, table, offs, heads, size):
    seq, model = x.shape
    width = heads * HD
    vmem = pl.BlockSpec(memory_space=pltpu.VMEM)
    smem = pl.BlockSpec(memory_space=pltpu.SMEM)
    blocks = (4, 4) if size == 8 else (1,)
    rows = model // sum(blocks)
    out = pl.pallas_call(
        functools.partial(attend_back_kernel, heads, blocks),
        out_shape=(
            jax.ShapeDtypeStruct((seq, model), BF),
            jax.ShapeDtypeStruct((8, HALF), F32),
            *[jax.ShapeDtypeStruct((b, rows, 4 * width), BF) for b in blocks],
        ),
        in_specs=[smem, smem] + [vmem] * 7,
        out_specs=(vmem,) * (2 + len(blocks)),
        scratch_shapes=[
            pltpu.VMEM((width, seq), BF),
            pltpu.VMEM((width, seq), BF),
            pltpu.VMEM((width, seq), BF),
            pltpu.VMEM((heads, seq, HD), BF),
            pltpu.VMEM((heads, seq, HD), BF),
            pltpu.VMEM((heads, seq, HD), BF),
            pltpu.VMEM((heads, seq, HD), BF),
            pltpu.VMEM((heads, 2, HALF, HALF), F32),
            pltpu.VMEM((width, seq), F32),
            pltpu.VMEM((seq, 3 * width), BF),
            pltpu.VMEM((heads, 2, HALF, HALF), F32),
            pltpu.VMEM((8, seq), F32),
            pltpu.VMEM((model, 4 * width), F32),
        ],
        compiler_params=pltpu.CompilerParams(vmem_limit_bytes=VMEM_MAX),
        cost_estimate=pl.CostEstimate(flops=10**10, bytes_accessed=10**7, transcendentals=2 * 10**6),
        name="attend_back",
    )(offs, table, d_rows, w, qkv, ctx, lse, first_key, x)
    return out[0], out[1], out[2:]


def expert_kernel(e, pieces, blocks, plan_ref, offsets_ref, goffs_ref, xd_ref, row_ref, col_ref, *refs):
    model = xd_ref.shape[1] // 2
    has_terms = e > 0
    terms_in = refs[0] if has_terms else None
    refs = refs[1:] if has_terms else refs
    piece_refs = refs[:pieces]
    terms_ref = refs[pieces]
    grads = refs[pieces + 1 : pieces + 1 + len(blocks)]
    w_ref, acc_ref, sem = refs[pieces + 1 + len(blocks) :]
    hidden = w_ref.shape[1] // 2
    length = xd_ref.shape[0]
    copies = load_rows(piece_refs, offsets_ref, w_ref, sem)
    if has_terms:
        terms_ref[...] = terms_in[...]
    else:
        terms_ref[...] = jnp.zeros_like(terms_ref)
    acc_ref[...] = jnp.zeros_like(acc_ref)
    for copy in copies:
        copy.wait()
    tiles = plan_ref[e]
    base = plan_ref[E + e]

    @pl.loop(0, tiles)
    def _(t):
        start = base + t * ROWS
        pick = jnp.where(row_ref[0:1, :] == start + iota((ROWS, length), 0), 1.0, 0.0).astype(BF)
        xd = nn(pick, xd_ref[...]).astype(BF)
        x, d = xd[:, :model], xd[:, model:]
        inner = nn(x, w_ref[:, :hidden])
        cubic = 0.044715 * inner * inner
        tanh = jnp.tanh(math.sqrt(2.0 / math.pi) * inner * (1.0 + cubic))
        half = 0.5 * (1.0 + tanh)
        active = (inner * half).astype(BF)
        slope = half + (0.5 * math.sqrt(2.0 / math.pi)) * inner * (1.0 - tanh * tanh) * (1.0 + 3.0 * cubic)
        out = nt(active, w_ref[:, hidden:]).astype(BF)
        d_inner = (nn(d, w_ref[:, hidden:]) * slope).astype(BF)
        acc_ref[:, :hidden] += tn(x, d_inner)
        acc_ref[:, hidden:] += tn(d, active)
        d_x = nt(d_inner, w_ref[:, :hidden]).astype(BF)
        place = jnp.where(col_ref[:, 0:1] == start + iota((length, ROWS), 1), 1.0, 0.0).astype(BF)
        terms_ref[:, :model] = (terms_ref[:, :model].astype(F32) + nn(place, out)).astype(BF)
        terms_ref[:, model:] = (terms_ref[:, model:].astype(F32) + nn(place, d_x)).astype(BF)

    scatter_rows(acc_ref, goffs_ref, grads, blocks)


def expert(e, plan, offsets, goffs, xd, slot_row, slot_col, terms, pieces, size):
    length, both = xd.shape
    model = both // 2
    hidden2 = pieces[0].shape[1]
    n = len(pieces)
    vmem = pl.BlockSpec(memory_space=pltpu.VMEM)
    smem = pl.BlockSpec(memory_space=pltpu.SMEM)
    blocks = (4, 4) if size == 8 else (1,)
    rows = model // sum(blocks)
    extra = [] if terms is None else [terms]
    out = pl.pallas_call(
        functools.partial(expert_kernel, e, n, blocks),
        out_shape=(
            jax.ShapeDtypeStruct((length, both), BF),
            *[jax.ShapeDtypeStruct((b, rows, hidden2), BF) for b in blocks],
        ),
        in_specs=[smem] * 3 + [vmem] * (3 + len(extra)) + [pl.BlockSpec(memory_space=pl.ANY)] * n,
        out_specs=(vmem,) * (1 + len(blocks)),
        scratch_shapes=[
            pltpu.VMEM((model, hidden2), BF),
            pltpu.VMEM((model, hidden2), F32),
            pltpu.SemaphoreType.DMA((n,)),
        ],
        compiler_params=pltpu.CompilerParams(vmem_limit_bytes=VMEM_MAX),
        cost_estimate=pl.CostEstimate(flops=3 * 10**9, bytes_accessed=10**7, transcendentals=10**6),
        name=f"expert_{e}",
    )(plan, offsets, goffs, xd, slot_row, slot_col, *extra, *pieces)
    return out[0], out[1:]


def rms_apply(values, gain_vec):
    inverse = lax.rsqrt(jnp.mean(values * values, axis=-1, keepdims=True) + EPSILON)
    return values * inverse * gain_vec


def per_device(
    sizes,
    tokens,
    segments,
    routes,
    cotangent,
    gain_attn,
    w_query,
    w_key,
    w_value,
    w_output,
    rel_table,
    gain_ffn,
    w_router,
    w_inner,
    w_outer,
):
    size = sizes["dp"]
    part_index = lax.axis_index("tensor")
    rows_local, model = tokens.shape
    seq_len = segments.shape[0]
    width = w_query.shape[1]
    heads = width // HD
    all_heads = rel_table.shape[1]
    hidden = w_inner.shape[2]
    shard_rows = w_query.shape[0]

    attn_shard = jnp.concatenate([w_query, w_key, w_value, jnp.transpose(w_output)], axis=1)
    attn_pieces, offsets = gather_dp(attn_shard, size)
    both_shard = jnp.concatenate([w_inner, jnp.transpose(w_outer, (0, 2, 1))], axis=2)
    expert_pieces = [gather_dp(both_shard[e], size)[0] for e in range(E)]
    goffs = send_offsets(shard_rows, size)

    route_row = jnp.reshape(routes, (1, seq_len))
    slot_row, slot_col, plan = make_plan(route_row)
    counts = [jnp.sum((segments < s).astype(jnp.int32)) for s in range(1, 5)]
    first_key = jnp.zeros_like(segments)
    for s in range(1, 5):
        first_key = jnp.where(segments >= s, counts[s - 1], first_key)
    first_key = first_key[None, :]
    table = jnp.transpose(
        lax.dynamic_slice_in_dim(rel_table.astype(F32), part_index * heads, heads, 1)
    )

    normed_attn, norm_one_pull = jax.vjp(rms_apply, tokens, gain_attn.astype(F32))
    attn_rows = lax.all_gather(normed_attn.astype(BF), "tensor", axis=0, tiled=True)
    qkv, ctx, lse, branch, w_attn = attend(attn_rows, attn_pieces, offsets, table, first_key, heads)
    attended = tokens + lax.psum_scatter(
        branch, "tensor", scatter_dimension=0, tiled=True
    ).astype(F32)

    normed_ffn, norm_two_pull = jax.vjp(rms_apply, attended, gain_ffn.astype(F32))
    ffn_in = normed_ffn.astype(BF)
    local_routes = lax.dynamic_slice_in_dim(routes[:, 0], part_index * rows_local, rows_local, 0)
    route_mask = (local_routes[:, None] == jnp.arange(E, dtype=jnp.int32)[None, :]).astype(F32)

    def gate_of(normed_values, router_values):
        logits = jnp.dot(normed_values, router_values, precision=lax.Precision.HIGHEST)
        return jnp.sum(jax.nn.softmax(logits, axis=-1) * route_mask, axis=-1)

    gate_weight, gate_pull = jax.vjp(gate_of, ffn_in.astype(F32), w_router.astype(F32))
    d_expert = (cotangent * gate_weight[:, None]).astype(BF)
    xd = lax.all_gather(
        jnp.concatenate([ffn_in, d_expert], axis=1), "tensor", axis=0, tiled=True
    )

    terms = None
    expert_sums = []
    for e in range(E):
        terms, parts = expert(
            e, plan, offsets, goffs, xd, slot_row, slot_col, terms, expert_pieces[e], size
        )
        expert_sums.append(reduce_dp(parts, size))
    sums = lax.psum_scatter(terms, "tensor", scatter_dimension=0, tiled=True).astype(F32)
    expert_out, d_ffn_local = sums[:, :model], sums[:, model:]
    output = attended + gate_weight[:, None] * expert_out
    d_gate = jnp.sum(cotangent * expert_out, axis=-1)

    d_ffn_router, grad_router_local = gate_pull(d_gate)
    d_attended_norm, grad_gain_two = norm_two_pull(d_ffn_local + d_ffn_router)
    d_attended = cotangent + d_attended_norm
    d_branch_rows = lax.all_gather(d_attended.astype(BF), "tensor", axis=0, tiled=True)

    total_rows, diag, attn_parts = attend_back(
        d_branch_rows, w_attn, qkv, ctx, lse, first_key, attn_rows, table, goffs, heads, size
    )
    attn_sum = reduce_dp(attn_parts, size)
    d_attn_local = lax.psum_scatter(
        total_rows, "tensor", scatter_dimension=0, tiled=True
    ).astype(F32)
    d_tokens_norm, grad_gain_one = norm_one_pull(d_attn_local)
    grad_tokens = d_attended + d_tokens_norm

    onehot = jnp.asarray((BUCKETS[:HALF, None] == np.arange(NBKT - 1)[None, :]).astype(np.float32))
    near_sums = jnp.dot(onehot.T, diag[:heads].T, precision=lax.Precision.HIGHEST)
    table_local = jnp.concatenate([near_sums, -jnp.sum(near_sums, axis=0, keepdims=True)], axis=0)
    grad_table_full = lax.dynamic_update_slice_in_dim(
        jnp.zeros((NBKT, all_heads), F32), table_local, part_index * heads, 1
    )
    small_sums = lax.psum(
        (grad_gain_one, grad_gain_two, grad_router_local, grad_table_full), ("dp", "tensor")
    )
    grad_inner = jnp.stack([s[:, :hidden] for s in expert_sums])
    grad_outer = jnp.stack([jnp.transpose(s[:, hidden:]) for s in expert_sums])
    return (
        output,
        grad_tokens,
        small_sums[0],
        attn_sum[:, :width],
        attn_sum[:, width : 2 * width],
        attn_sum[:, 2 * width : 3 * width],
        jnp.transpose(attn_sum[:, 3 * width :]),
        small_sums[3],
        small_sums[1],
        small_sums[2],
        grad_inner,
        grad_outer,
    )


def solution(mesh):
    sizes = dict(mesh.shape)
    in_specs = (
        P(("dp", "tensor"), None),
        P("dp"),
        P("dp", None),
        P(("dp", "tensor"), None),
        P(),
        P("dp", "tensor"),
        P("dp", "tensor"),
        P("dp", "tensor"),
        P("tensor", "dp"),
        P(),
        P(),
        P(),
        P(None, "dp", "tensor"),
        P(None, "tensor", "dp"),
    )
    out_specs = (
        P(("dp", "tensor"), None),
        P(("dp", "tensor"), None),
        P(),
        P("dp", "tensor"),
        P("dp", "tensor"),
        P("dp", "tensor"),
        P("tensor", "dp"),
        P(),
        P(),
        P(),
        P(None, "dp", "tensor"),
        P(None, "tensor", "dp"),
    )
    return jax.shard_map(
        functools.partial(per_device, sizes),
        mesh=mesh,
        in_specs=in_specs,
        out_specs=out_specs,
        check_vma=False,
    )
```

```python
import functools
import math

import jax
import jax.numpy as jnp
import numpy as np
from jax import lax
from jax.experimental import pallas as pl
from jax.experimental.pallas import tpu as pltpu
from jax.sharding import PartitionSpec as P

HD = 64
NBKT = 32
MAXD = 128
E = 4
WIN = 1024
QT = 256
HALF = 128
ROWS = 256

EPSILON = 1e-06
NEG_LARGE = -1e30
BF = jnp.bfloat16
F32 = jnp.float32
VMEM_MAX = 56 * 1024 * 1024


def bucket_numbers(window, buckets, far_distance):
    distance = np.arange(window)
    exact_part = buckets // 2
    safe_distance = np.maximum(distance, 1) * 1.0
    log_part = exact_part + np.floor(
        np.log(safe_distance / exact_part)
        / np.log(far_distance / exact_part)
        * (buckets - exact_part)
    ).astype(np.int32)
    log_part = np.minimum(log_part, buckets - 1)
    return np.where(distance < exact_part, distance, log_part).astype(np.int32)


BUCKETS = bucket_numbers(WIN, NBKT, MAXD)
FIRST = [int(np.argmax(BUCKETS == b)) for b in range(NBKT)]
NEAR = FIRST[NBKT - 1]


def nn(a, b):
    return lax.dot_general(a, b, (((1,), (0,)), ((), ())), preferred_element_type=F32)


def nt(a, b):
    return lax.dot_general(a, b, (((1,), (1,)), ((), ())), preferred_element_type=F32)


def tn(a, b):
    return lax.dot_general(a, b, (((0,), (0,)), ((), ())), preferred_element_type=F32)


def iota(shape, dim):
    return lax.broadcasted_iota(jnp.int32, shape, dim)


def gather_dp(shard, size):
    rows = shard.shape[0]
    if size != 8:
        return [lax.all_gather(shard, "dp", axis=0, tiled=True)], jnp.zeros((1,), jnp.int32)
    me = lax.axis_index("dp")
    z, y = me // 2, me % 2
    own = [shard] + [lax.ppermute(shard, "dp", z_shift(k)) for k in (1, 2, 3)]
    far = [lax.ppermute(piece, "dp", Y_SWAP) for piece in own]
    ids = [((z + 4 - k) % 4) * 2 + y for k in range(4)]
    ids += [((z + 4 - k) % 4) * 2 + 1 - y for k in range(4)]
    return own + far, (jnp.stack(ids) * rows).astype(jnp.int32)


Y_SWAP = [(d, d ^ 1) for d in range(8)]


def z_shift(k):
    return [(z * 2 + y, ((z + k) % 4) * 2 + y) for z in range(4) for y in range(2)]


def send_offsets(rows, size):
    if size != 8:
        return jnp.zeros((1,), jnp.int32)
    me = lax.axis_index("dp")
    z, y = me // 2, me % 2
    ids = [((z + k) % 4) * 2 + y for k in range(4)] + [((z + k) % 4) * 2 + 1 - y for k in range(4)]
    return (jnp.stack(ids) * rows).astype(jnp.int32)


def reduce_dp(parts, size):
    if size != 8:
        return lax.psum_scatter(parts[0][0], "dp", scatter_dimension=0, tiled=True).astype(F32)
    mine, other = parts
    got = lax.ppermute(other, "dp", Y_SWAP)
    total = mine[0].astype(F32) + got[0].astype(F32)
    arrived = []
    for k in (1, 2, 3):
        pair = (mine[k].astype(F32) + got[k].astype(F32)).astype(BF)
        arrived.append(lax.ppermute(pair, "dp", z_shift(k)))
    for piece in arrived:
        total = total + piece.astype(F32)
    return total


def plan_kernel(route_ref, slot_row_ref, slot_col_ref, plan_ref):
    length = route_ref.shape[1]
    route = route_ref[...]
    chosen = jnp.where(iota((8, length), 0) == route, 1.0, 0.0).astype(F32)
    upper = jnp.where(iota((length, length), 0) < iota((length, length), 1), 1.0, 0.0)
    before = nn(chosen.astype(BF), upper.astype(BF))
    rank = jnp.sum(chosen * before, axis=0, keepdims=True)
    start = jnp.int32(0)
    base = jnp.zeros((1, length), F32)
    for e in range(E):
        here = route == e
        count = jnp.sum(jnp.where(here, 1, 0))
        tiles = (count + (ROWS - 1)) // ROWS
        plan_ref[e] = tiles
        plan_ref[E + e] = start
        base = base + jnp.where(here, start.astype(F32), 0.0)
        start = start + tiles * ROWS
    slots = jnp.broadcast_to(rank + base, (8, length))
    slot_row_ref[...] = slots.astype(jnp.int32)
    slot_col_ref[...] = jnp.transpose(slots).astype(jnp.int32)


def make_plan(route_row):
    length = route_row.shape[1]
    return pl.pallas_call(
        plan_kernel,
        out_shape=(
            jax.ShapeDtypeStruct((8, length), jnp.int32),
            jax.ShapeDtypeStruct((length, 8), jnp.int32),
            jax.ShapeDtypeStruct((2 * E,), jnp.int32),
        ),
        in_specs=[pl.BlockSpec(memory_space=pltpu.VMEM)],
        out_specs=(
            pl.BlockSpec(memory_space=pltpu.VMEM),
            pl.BlockSpec(memory_space=pltpu.VMEM),
            pl.BlockSpec(memory_space=pltpu.SMEM),
        ),
        compiler_params=pltpu.CompilerParams(vmem_limit_bytes=VMEM_MAX),
        name="route_plan",
    )(route_row)


def fill_bias(bias_ref, table_ref, heads):
    step = iota((HALF, HALF), 1) - iota((HALF, HALF), 0)
    for side in range(2):
        distance = step + side * HALF
        tiles = [jnp.full((HALF, HALF), table_ref[h, NBKT - 1], F32) for h in range(heads)]
        for b in reversed(range(NBKT - 1)):
            below = distance < FIRST[b + 1]
            tiles = [jnp.where(below, table_ref[h, b], tiles[h]) for h in range(heads)]
        for h in range(heads):
            bias_ref[h, side] = tiles[h]


def biased_scores(raw, gap, h, bias_ref, table_ref, first_key, key_start):
    far = table_ref[h, NBKT - 1]
    keys = key_start + iota((QT, QT), 0)
    if gap >= 2:
        return jnp.where(keys >= first_key, raw + far, NEG_LARGE)
    diag, near = bias_ref[h, 0], bias_ref[h, 1]
    const = jnp.full((HALF, HALF), far, F32)
    if gap == 1:
        tile = jnp.concatenate(
            [
                jnp.concatenate([const, const], axis=1),
                jnp.concatenate([near, const], axis=1),
            ],
            axis=0,
        )
        return jnp.where(keys >= first_key, raw + tile, NEG_LARGE)
    tile = jnp.concatenate(
        [jnp.concatenate([diag, near], axis=1), jnp.concatenate([const, diag], axis=1)], axis=0
    )
    causal = iota((QT, QT), 0) <= iota((QT, QT), 1)
    return jnp.where((keys >= first_key) & causal, raw + tile, NEG_LARGE)


def load_rows(pieces, offsets_ref, whole, sem):
    rows = pieces[0].shape[0]
    copies = []
    for k, piece in enumerate(pieces):
        at = pl.ds(pl.multiple_of(offsets_ref[k], rows), rows)
        copies.append(pltpu.make_async_copy(piece, whole.at[at], sem.at[k]))
    for copy in copies:
        copy.start()
    return copies


def attend_blocks(heads, seq, first_ref, table_ref, q_t, v_t, kn, bias_ref, s_ref, ctx_t, lse_ref, blocks):
    for i in blocks:
        cols = slice(i * QT, (i + 1) * QT)
        first_key = first_ref[0:1, cols]
        for h in range(heads):
            band = slice(h * HD, (h + 1) * HD)
            q_blk = q_t[band, cols]
            peak = None
            for j in range(i + 1):
                raw = nn(kn[h, j * QT : (j + 1) * QT], q_blk)
                s = biased_scores(raw, i - j, h, bias_ref, table_ref, first_key, j * QT)
                s_ref[h, j] = s
                top = jnp.max(s, axis=0, keepdims=True)
                peak = top if peak is None else jnp.maximum(peak, top)
            total = jnp.zeros((1, QT), F32)
            acc = jnp.zeros((HD, QT), F32)
            for j in range(i + 1):
                p = jnp.exp(s_ref[h, j] - peak)
                total = total + jnp.sum(p, axis=0, keepdims=True)
                acc = acc + nn(v_t[band, j * QT : (j + 1) * QT], p.astype(BF))
            ctx_t[band, cols] = (acc / total).astype(BF)
            lse_ref[h : h + 1, cols] = peak + jnp.log(total)


def project(heads, x, w_ref, qkv_ref, q_t, v_t, kn):
    width = heads * HD
    qkv = nn(x, w_ref[:, : 3 * width]).astype(BF)
    qkv_ref[...] = qkv
    q_t[...] = jnp.transpose(qkv[:, :width]) * jnp.asarray(1.0 / math.sqrt(HD), BF)
    v_t[...] = jnp.transpose(qkv[:, 2 * width :])
    for h in range(heads):
        kn[h] = qkv[:, width + h * HD : width + (h + 1) * HD]


def attend_kernel(heads, pieces, offsets_ref, table_ref, x_ref, first_ref, *refs):
    piece_refs = refs[:pieces]
    qkv_ref, ctx_ref, lse_ref, branch_ref, w_out_ref = refs[pieces : pieces + 5]
    w_ref, q_t, v_t, kn, bias_ref, s_ref, ctx_t, sem = refs[pieces + 5 :]
    width = heads * HD
    seq = x_ref.shape[0]
    copies = load_rows(piece_refs, offsets_ref, w_ref, sem)
    fill_bias(bias_ref, table_ref, heads)
    for copy in copies:
        copy.wait()
    w_out_ref[...] = w_ref[...]
    project(heads, x_ref[...], w_ref, qkv_ref, q_t, v_t, kn)
    blocks = range(seq // QT)
    attend_blocks(
        heads, seq, first_ref, table_ref, q_t, v_t, kn, bias_ref, s_ref, ctx_t, lse_ref, blocks
    )
    ctx = jnp.transpose(ctx_t[...])
    ctx_ref[...] = ctx
    branch_ref[...] = nt(ctx, w_ref[:, 3 * width :]).astype(BF)


def attend(x, pieces, offsets, table, first_key, heads):
    seq, model = x.shape
    width = heads * HD
    n = len(pieces)
    vmem = pl.BlockSpec(memory_space=pltpu.VMEM)
    smem = pl.BlockSpec(memory_space=pltpu.SMEM)
    return pl.pallas_call(
        functools.partial(attend_kernel, heads, n),
        out_shape=(
            jax.ShapeDtypeStruct((seq, 3 * width), BF),
            jax.ShapeDtypeStruct((seq, width), BF),
            jax.ShapeDtypeStruct((8, seq), F32),
            jax.ShapeDtypeStruct((seq, model), BF),
            jax.ShapeDtypeStruct((model, 4 * width), BF),
        ),
        in_specs=[smem, smem, vmem, vmem] + [pl.BlockSpec(memory_space=pl.ANY)] * n,
        out_specs=(vmem,) * 5,
        scratch_shapes=[
            pltpu.VMEM((model, 4 * width), BF),
            pltpu.VMEM((width, seq), BF),
            pltpu.VMEM((width, seq), BF),
            pltpu.VMEM((heads, seq, HD), BF),
            pltpu.VMEM((heads, 2, HALF, HALF), F32),
            pltpu.VMEM((heads, seq // QT, QT, QT), F32),
            pltpu.VMEM((width, seq), BF),
            pltpu.SemaphoreType.DMA((n,)),
        ],
        compiler_params=pltpu.CompilerParams(vmem_limit_bytes=VMEM_MAX),
        cost_estimate=pl.CostEstimate(flops=4 * 10**9, bytes_accessed=10**7, transcendentals=2 * 10**6),
        name="attend",
    )(offsets, table, x, first_key, *pieces)


def attend_back_kernel(
    heads, blocks, offs_ref, table_ref, d_ref, w_ref, qkv_ref, ctx_ref, lse_ref, first_ref, x_ref,
    rows_ref, diag_ref, *refs
):
    grads = refs[: len(blocks)]
    q_t, k_t, dc_t, kn, vn, qn, dcn, bias_ref, dq_t, dqkv, near_ref, delta_ref, acc_ref = refs[len(blocks) :]
    width = heads * HD
    seq = d_ref.shape[0]
    scale = jnp.asarray(1.0 / math.sqrt(HD), BF)
    fill_bias(bias_ref, table_ref, heads)
    d_rows = d_ref[...]
    ctx = ctx_ref[...]
    dc = nn(d_rows, w_ref[:, 3 * width :]).astype(BF)
    acc_ref[:, 3 * width :] = tn(d_rows, ctx)
    dct = jnp.transpose(dc)
    dc_t[...] = dct
    qkv = qkv_ref[...]
    q_t[...] = jnp.transpose(qkv[:, :width]) * scale
    k_t[...] = jnp.transpose(qkv[:, width : 2 * width])
    product = dct.astype(F32) * jnp.transpose(ctx).astype(F32)
    for h in range(heads):
        band = slice(h * HD, (h + 1) * HD)
        qn[h] = qkv[:, band] * scale
        kn[h] = qkv[:, width + h * HD : width + (h + 1) * HD]
        vn[h] = qkv[:, 2 * width + h * HD : 2 * width + (h + 1) * HD]
        dcn[h] = dc[:, band]
        delta_ref[h : h + 1] = jnp.sum(product[band], axis=0, keepdims=True)
    dq_t[...] = jnp.zeros_like(dq_t)
    near_ref[...] = jnp.zeros_like(near_ref)
    for j in range(seq // QT):
        keys = slice(j * QT, (j + 1) * QT)
        for h in range(heads):
            band = slice(h * HD, (h + 1) * HD)
            dk = jnp.zeros((QT, HD), F32)
            dv = jnp.zeros((QT, HD), F32)
            for i in range(j, seq // QT):
                cols = slice(i * QT, (i + 1) * QT)
                raw = nn(kn[h, keys], q_t[band, cols])
                s = biased_scores(raw, i - j, h, bias_ref, table_ref, first_ref[0:1, cols], j * QT)
                p = jnp.exp(s - lse_ref[h : h + 1, cols])
                dp = nn(vn[h, keys], dc_t[band, cols])
                ds = p * (dp - delta_ref[h : h + 1, cols])
                if i == j:
                    near_ref[h, 0] += ds[:HALF, :HALF] + ds[HALF:, HALF:]
                    near_ref[h, 1] += ds[:HALF, HALF:]
                elif i == j + 1:
                    near_ref[h, 1] += ds[HALF:, :HALF]
                ds = ds.astype(BF)
                dv = dv + nn(p.astype(BF), dcn[h, cols])
                dk = dk + nn(ds, qn[h, cols])
                dq_t[band, cols] += nn(k_t[band, keys], ds)
            dqkv[keys, width + h * HD : width + (h + 1) * HD] = dk.astype(BF)
            dqkv[keys, 2 * width + h * HD : 2 * width + (h + 1) * HD] = dv.astype(BF)
    dqkv[:, :width] = jnp.transpose((dq_t[...] * (1.0 / math.sqrt(HD))).astype(BF))
    d_qkv = dqkv[...]
    rows_ref[...] = nt(d_qkv, w_ref[:, : 3 * width]).astype(BF)
    acc_ref[:, : 3 * width] = tn(x_ref[...], d_qkv)
    scatter_rows(acc_ref, offs_ref, grads, blocks)
    key, query = iota((HALF, HALF), 0), iota((HALF, HALF), 1)
    lines = []
    for h in range(heads):
        both = near_ref[h, 0] + jnp.where(query < key, near_ref[h, 1], 0.0)
        for bit in range(7):
            turned = pltpu.roll(both, HALF - (1 << bit), 1)
            both = jnp.where((key >> bit) & 1 == 1, turned, both)
        lines.append(jnp.sum(both, axis=0, keepdims=True))
    lines += [jnp.zeros((8 - heads, HALF), F32)]
    diag_ref[...] = jnp.concatenate(lines, axis=0)


def scatter_rows(acc_ref, offs_ref, outs, blocks):
    k = 0
    for out, count in zip(outs, blocks):
        rows = out.shape[1]
        for b in range(count):
            at = pl.ds(pl.multiple_of(offs_ref[k], rows), rows)
            out[b] = acc_ref[at, :].astype(BF)
            k += 1


def attend_back(d_rows, w, qkv, ctx, lse, first_key, x, table, offs, heads, size):
    seq, model = x.shape
    width = heads * HD
    vmem = pl.BlockSpec(memory_space=pltpu.VMEM)
    smem = pl.BlockSpec(memory_space=pltpu.SMEM)
    blocks = (4, 4) if size == 8 else (1,)
    rows = model // sum(blocks)
    out = pl.pallas_call(
        functools.partial(attend_back_kernel, heads, blocks),
        out_shape=(
            jax.ShapeDtypeStruct((seq, model), BF),
            jax.ShapeDtypeStruct((8, HALF), F32),
            *[jax.ShapeDtypeStruct((b, rows, 4 * width), BF) for b in blocks],
        ),
        in_specs=[smem, smem] + [vmem] * 7,
        out_specs=(vmem,) * (2 + len(blocks)),
        scratch_shapes=[
            pltpu.VMEM((width, seq), BF),
            pltpu.VMEM((width, seq), BF),
            pltpu.VMEM((width, seq), BF),
            pltpu.VMEM((heads, seq, HD), BF),
            pltpu.VMEM((heads, seq, HD), BF),
            pltpu.VMEM((heads, seq, HD), BF),
            pltpu.VMEM((heads, seq, HD), BF),
            pltpu.VMEM((heads, 2, HALF, HALF), F32),
            pltpu.VMEM((width, seq), F32),
            pltpu.VMEM((seq, 3 * width), BF),
            pltpu.VMEM((heads, 2, HALF, HALF), F32),
            pltpu.VMEM((8, seq), F32),
            pltpu.VMEM((model, 4 * width), F32),
        ],
        compiler_params=pltpu.CompilerParams(vmem_limit_bytes=VMEM_MAX),
        cost_estimate=pl.CostEstimate(flops=10**10, bytes_accessed=10**7, transcendentals=2 * 10**6),
        name="attend_back",
    )(offs, table, d_rows, w, qkv, ctx, lse, first_key, x)
    return out[0], out[1], out[2:]


def expert_kernel(e, pieces, blocks, plan_ref, offsets_ref, goffs_ref, xd_ref, row_ref, col_ref, *refs):
    model = xd_ref.shape[1] // 2
    has_terms = e > 0
    terms_in = refs[0] if has_terms else None
    refs = refs[1:] if has_terms else refs
    piece_refs = refs[:pieces]
    terms_ref = refs[pieces]
    grads = refs[pieces + 1 : pieces + 1 + len(blocks)]
    w_ref, acc_ref, sem = refs[pieces + 1 + len(blocks) :]
    hidden = w_ref.shape[1] // 2
    length = xd_ref.shape[0]
    if len(piece_refs[0].shape) == 3:
        whole = piece_refs[0]
        copies = [
            pltpu.make_async_copy(whole.at[2 * e], w_ref.at[:, :hidden], sem.at[0]),
            pltpu.make_async_copy(whole.at[2 * e + 1], w_ref.at[:, hidden:], sem.at[1]),
        ]
        for copy in copies:
            copy.start()
    else:
        copies = load_rows(piece_refs, offsets_ref, w_ref, sem)
    if has_terms:
        terms_ref[...] = terms_in[...]
    else:
        terms_ref[...] = jnp.zeros_like(terms_ref)
    acc_ref[...] = jnp.zeros_like(acc_ref)
    for copy in copies:
        copy.wait()
    tiles = plan_ref[e]
    base = plan_ref[E + e]

    @pl.loop(0, tiles)
    def _(t):
        start = base + t * ROWS
        pick = jnp.where(row_ref[0:1, :] == start + iota((ROWS, length), 0), 1.0, 0.0).astype(BF)
        xd = nn(pick, xd_ref[...]).astype(BF)
        x, d = xd[:, :model], xd[:, model:]
        inner = nn(x, w_ref[:, :hidden])
        cubic = 0.044715 * inner * inner
        tanh = jnp.tanh(math.sqrt(2.0 / math.pi) * inner * (1.0 + cubic))
        half = 0.5 * (1.0 + tanh)
        active = (inner * half).astype(BF)
        slope = half + (0.5 * math.sqrt(2.0 / math.pi)) * inner * (1.0 - tanh * tanh) * (1.0 + 3.0 * cubic)
        out = nt(active, w_ref[:, hidden:]).astype(BF)
        d_inner = (nn(d, w_ref[:, hidden:]) * slope).astype(BF)
        acc_ref[:, :hidden] += tn(x, d_inner)
        acc_ref[:, hidden:] += tn(d, active)
        d_x = nt(d_inner, w_ref[:, :hidden]).astype(BF)
        place = jnp.where(col_ref[:, 0:1] == start + iota((length, ROWS), 1), 1.0, 0.0).astype(BF)
        terms_ref[:, :model] = (terms_ref[:, :model].astype(F32) + nn(place, out)).astype(BF)
        terms_ref[:, model:] = (terms_ref[:, model:].astype(F32) + nn(place, d_x)).astype(BF)

    scatter_rows(acc_ref, goffs_ref, grads, blocks)


def expert(e, plan, offsets, goffs, xd, slot_row, slot_col, terms, pieces, size):
    length, both = xd.shape
    model = both // 2
    hidden2 = 2 * pieces[0].shape[2] if pieces[0].ndim == 3 else pieces[0].shape[1]
    n = len(pieces)
    vmem = pl.BlockSpec(memory_space=pltpu.VMEM)
    smem = pl.BlockSpec(memory_space=pltpu.SMEM)
    blocks = (4, 4) if size == 8 else (1,)
    rows = model // sum(blocks)
    extra = [] if terms is None else [terms]
    out = pl.pallas_call(
        functools.partial(expert_kernel, e, n, blocks),
        out_shape=(
            jax.ShapeDtypeStruct((length, both), BF),
            *[jax.ShapeDtypeStruct((b, rows, hidden2), BF) for b in blocks],
        ),
        in_specs=[smem] * 3 + [vmem] * (3 + len(extra)) + [pl.BlockSpec(memory_space=pl.ANY)] * n,
        out_specs=(vmem,) * (1 + len(blocks)),
        scratch_shapes=[
            pltpu.VMEM((model, hidden2), BF),
            pltpu.VMEM((model, hidden2), F32),
            pltpu.SemaphoreType.DMA((max(n, 2),)),
        ],
        compiler_params=pltpu.CompilerParams(vmem_limit_bytes=VMEM_MAX),
        cost_estimate=pl.CostEstimate(flops=3 * 10**9, bytes_accessed=10**7, transcendentals=10**6),
        name=f"expert_{e}",
    )(plan, offsets, goffs, xd, slot_row, slot_col, *extra, *pieces)
    return out[0], out[1:]


MESH = pl.DeviceIdType.MESH
PIECES = 1 + 2 * E
T_SEMS = 32
W_SEMS = 7 * PIECES


class Here:
    def __init__(self):
        self.d = lax.axis_index("dp")
        self.t = lax.axis_index("tensor")
        self.z, self.y = self.d // 2, self.d % 2
        self.x, self.c = self.t // 2, self.t % 2
        self.core = {"dp": self.d, "tensor": 2 * self.x + 1 - self.c}
        self.side = {"dp": self.d, "tensor": 2 * (1 - self.x) + self.c}
        self.over = {"dp": 2 * self.z + 1 - self.y, "tensor": self.t}

    def z_dp(self, k):
        return 2 * ((self.z + 4 + k) % 4) + self.y

    def z_peer(self, k):
        return {"dp": self.z_dp(k), "tensor": self.t}

    def greet(self):
        barrier = pltpu.get_barrier_semaphore()
        peers = [self.core, self.side, self.over] + [self.z_peer(k) for k in (1, 2, 3)]
        for peer in peers:
            pl.semaphore_signal(barrier, inc=1, device_id=peer, device_id_type=MESH)
        pl.semaphore_wait(barrier, len(peers))


class Wire:
    def __init__(self, send, recv):
        self.send, self.recv, self.sent = send, recv, []

    def __call__(self, src, dst, peer):
        k = len(self.sent)
        copy = pltpu.make_async_remote_copy(
            src_ref=src, dst_ref=dst, send_sem=self.send.at[k], recv_sem=self.recv.at[k],
            device_id=peer, device_id_type=MESH,
        )
        copy.start()
        self.sent.append(copy)
        return copy

    def close(self):
        for copy in self.sent:
            copy.wait_send()


class Rows:
    def __init__(self, here, wire, buf, rows, part, parts):
        self.here, self.wire, self.buf = here, wire, buf
        self.rows, self.size = rows, rows // parts
        self.shift = part * self.size

    def at(self, t):
        return self.buf.at[pl.ds(pl.multiple_of(t * self.rows + self.shift, 16), self.size)]

    def start(self):
        mine = self.at(self.here.t)
        self.far = self.wire(mine, mine, self.here.side)
        self.near = self.wire(mine, mine, self.here.core)

    def forward(self):
        self.far.wait_recv()
        theirs = self.at(2 * (1 - self.here.x) + self.here.c)
        self.last = self.wire(theirs, theirs, self.here.core)

    def finish(self):
        self.near.wait_recv()
        self.last.wait_recv()


class Sums:
    def __init__(self, here, wire, src, landed, out, back, rows, part, parts):
        self.here, self.wire, self.src = here, wire, src
        self.landed, self.out, self.back = landed, out, back
        self.rows, self.size = rows, rows // parts
        self.shift = part * self.size
        self.part = part

    def at(self, t):
        return pl.ds(pl.multiple_of(t * self.rows + self.shift, 16), self.size)

    def start(self):
        h = self.here
        self.copies = []
        for slot, x in ((0, 1 - h.x), (1, h.x)):
            src = self.src.at[self.at(2 * x + 1 - h.c)]
            self.copies.append(self.wire(src, self.landed.at[slot, self.part], h.core))

    def cross(self):
        h = self.here
        self.copies[0].wait_recv()
        mine = self.src[self.at(2 * (1 - h.x) + h.c)].astype(F32)
        self.out[self.part] = (mine + self.landed[0, self.part].astype(F32)).astype(BF)
        self.last = self.wire(self.out.at[self.part], self.back.at[self.part], h.side)

    def total(self):
        h = self.here
        self.copies[1].wait_recv()
        near = self.src[self.at(2 * h.x + h.c)].astype(F32) + self.landed[1, self.part].astype(F32)
        self.last.wait_recv()
        return near + self.back[self.part].astype(F32)


class Weights:
    def __init__(self, here, wire, own_sem, sources, target):
        self.here, self.wire, self.own_sem = here, wire, own_sem
        self.sources, self.target = sources, target
        self.z, self.over, self.own = {}, {}, {}

    def at(self, p, dp):
        rows = self.sources[p].shape[0]
        return self.target(p, pl.ds(pl.multiple_of(dp * rows, 16), rows))

    def start(self, p):
        if p >= PIECES:
            return
        h, src = self.here, self.sources[p]
        dst = self.at(p, h.d)
        self.z[p] = [self.wire(src, dst, h.z_peer(k)) for k in (1, 2, 3)]
        self.over[p] = [self.wire(src, dst, h.over)]
        self.own[p] = pltpu.make_async_copy(src, dst, self.own_sem.at[p])
        self.own[p].start()

    def forward(self, p):
        if p >= PIECES:
            return
        h = self.here
        for k, copy in zip((1, 2, 3), self.z[p]):
            copy.wait_recv()
            part = self.at(p, h.z_dp(-k))
            self.over[p].append(self.wire(part, part, h.over))

    def finish(self, p):
        for copy in self.over[p]:
            copy.wait_recv()
        self.own[p].wait()


def normed(values, gain):
    inverse = lax.rsqrt(jnp.mean(values * values, axis=-1, keepdims=True) + EPSILON)
    return values * inverse * gain


def front_kernel(
    heads, table_ref, tokens_ref, cot_ref, seg_ref, route_ref, gain_a_ref, gain_f_ref, router_ref,
    wq_ref, wk_ref, wv_ref, wo_ref, w_in_ref, w_out_ref,
    attn_rows, qkv_ref, ctx_ref, lse_ref, w_attn, first_ref, attended_ref, x_rows, d_rows, experts,
    attn_shard, outer_shard, tab_ref, q_t, v_t, kn, bias_ref, s_ref, ctx_t, cot_rows, branch,
    landed, out, back, t_send, t_recv, w_send, w_recv, own_sem,
):
    h = Here()
    width = heads * HD
    seq = attn_rows.shape[0]
    rows = tokens_ref.shape[0]
    wire = Wire(t_send, t_recv)
    sources = [attn_shard]
    for e in range(E):
        sources += [w_in_ref.at[e], outer_shard.at[e]]

    def target(p, at):
        return w_attn.at[at] if p == 0 else experts.at[p - 1, at]

    weights = Weights(h, Wire(w_send, w_recv), own_sem, sources, target)
    attn_shard[:, :width] = wq_ref[...]
    attn_shard[:, width : 2 * width] = wk_ref[...]
    attn_shard[:, 2 * width : 3 * width] = wv_ref[...]
    attn_shard[:, 3 * width :] = jnp.transpose(wo_ref[...])
    h.greet()
    weights.start(0)

    half = rows // 2
    gathers = [Rows(h, wire, attn_rows, rows, part, 2) for part in range(2)]
    gain_a = gain_a_ref[...].astype(F32)
    for part in range(2):
        at = pl.ds(pl.multiple_of(h.t * rows + part * half, 16), half)
        attn_rows[at] = normed(tokens_ref[part * half : (part + 1) * half], gain_a).astype(BF)
        gathers[part].start()
    own = pl.ds(pl.multiple_of(h.t * rows, 16), rows)
    cot_rows[own] = cot_ref[...].astype(BF)
    for hd in range(heads):
        for b in range(NBKT):
            tab_ref[hd, b] = table_ref[b, h.t * heads + hd]
    fill_bias(bias_ref, tab_ref, heads)
    segments = seg_ref[...]
    first = jnp.zeros(segments.shape, jnp.int32)
    for s in range(1, 5):
        first = jnp.where(segments >= s, jnp.sum(jnp.where(segments < s, 1, 0)), first)
    first_ref[...] = jnp.broadcast_to(first, first_ref.shape)
    for e in range(E):
        outer_shard[e] = jnp.transpose(w_out_ref[e])
    gathers[0].forward()
    gathers[1].forward()
    weights.forward(0)
    weights.start(1)
    weights.start(2)
    gathers[0].finish()
    gathers[1].finish()
    cots = Rows(h, wire, cot_rows, rows, 0, 1)
    cots.start()
    weights.finish(0)

    project(heads, attn_rows[...], w_attn, qkv_ref, q_t, v_t, kn)
    state = (first_ref, tab_ref, q_t, v_t, kn, bias_ref, s_ref, ctx_t, lse_ref)
    attend_blocks(heads, seq, *state, range(0, 3))
    cots.forward()
    weights.forward(1)
    weights.start(3)
    attend_blocks(heads, seq, *state, range(3, seq // QT))
    ctx = jnp.transpose(ctx_t[...])
    ctx_ref[...] = ctx
    branch[...] = nt(ctx, w_attn[:, 3 * width :]).astype(BF)
    sums = [Sums(h, wire, branch, landed, out, back, rows, part, 2) for part in range(2)]
    for part in range(2):
        sums[part].start()
    for part in range(2):
        sums[part].cross()
    weights.forward(2)
    weights.start(4)
    gathers = [Rows(h, wire, x_rows, rows, part, 2) for part in range(2)]
    gain_f = gain_f_ref[...].astype(F32)
    for part in range(2):
        at = slice(part * half, (part + 1) * half)
        attended = tokens_ref[at] + sums[part].total()
        attended_ref[at] = attended
        x_rows[pl.ds(pl.multiple_of(h.t * rows + part * half, 16), half)] = normed(
            attended, gain_f
        ).astype(BF)
        gathers[part].start()
    weights.forward(3)
    weights.start(5)
    for part in range(2):
        gathers[part].forward()
    cots.finish()
    for part in range(2):
        gathers[part].finish()
    logits = nn(x_rows[...], router_ref[...])
    raised = jnp.exp(logits - jnp.max(logits, axis=1, keepdims=True))
    chosen = jnp.where(route_ref[...] == iota(logits.shape, 1), raised, 0.0)
    gate = jnp.sum(chosen, axis=1, keepdims=True) / jnp.sum(raised, axis=1, keepdims=True)
    d_rows[...] = (cot_rows[...].astype(F32) * gate).astype(BF)
    for p in range(4, PIECES):
        weights.forward(p)
        weights.start(p + 2)
    for p in range(1, PIECES):
        weights.finish(p)
    wire.close()
    weights.wire.close()


def front(table, tokens, cot, segments, routes, gain_a, gain_f, router, wq, wk, wv, wo, w_in, w_out):
    rows, model = tokens.shape
    seq = segments.shape[1]
    width = wq.shape[1]
    heads = width // HD
    vmem = pl.BlockSpec(memory_space=pltpu.VMEM)
    smem = pl.BlockSpec(memory_space=pltpu.SMEM)
    hbm = pl.BlockSpec(memory_space=pl.ANY)
    shard = wq.shape[0]
    return pl.pallas_call(
        functools.partial(front_kernel, heads),
        out_shape=(
            jax.ShapeDtypeStruct((seq, model), BF),
            jax.ShapeDtypeStruct((seq, 3 * width), BF),
            jax.ShapeDtypeStruct((seq, width), BF),
            jax.ShapeDtypeStruct((8, seq), F32),
            jax.ShapeDtypeStruct((model, 4 * width), BF),
            jax.ShapeDtypeStruct((8, seq), jnp.int32),
            jax.ShapeDtypeStruct((rows, model), F32),
            jax.ShapeDtypeStruct((seq, model), BF),
            jax.ShapeDtypeStruct((seq, model), BF),
            jax.ShapeDtypeStruct((2 * E, model, w_in.shape[2]), BF),
        ),
        in_specs=[smem] + [vmem] * 11 + [hbm, vmem],
        out_specs=(vmem,) * 9 + (hbm,),
        scratch_shapes=[
            pltpu.VMEM((shard, model), BF),
            pltpu.VMEM((E, shard, w_in.shape[2]), BF),
            pltpu.SMEM((heads, NBKT), F32),
            pltpu.VMEM((width, seq), BF),
            pltpu.VMEM((width, seq), BF),
            pltpu.VMEM((heads, seq, HD), BF),
            pltpu.VMEM((heads, 2, HALF, HALF), F32),
            pltpu.VMEM((heads, seq // QT, QT, QT), F32),
            pltpu.VMEM((width, seq), BF),
            pltpu.VMEM((seq, model), BF),
            pltpu.VMEM((seq, model), BF),
            pltpu.VMEM((2, 2, rows // 2, model), BF),
            pltpu.VMEM((2, rows // 2, model), BF),
            pltpu.VMEM((2, rows // 2, model), BF),
            pltpu.SemaphoreType.DMA((T_SEMS,)),
            pltpu.SemaphoreType.DMA((T_SEMS,)),
            pltpu.SemaphoreType.DMA((W_SEMS,)),
            pltpu.SemaphoreType.DMA((W_SEMS,)),
            pltpu.SemaphoreType.DMA((PIECES,)),
        ],
        compiler_params=pltpu.CompilerParams(
            vmem_limit_bytes=VMEM_MAX, collective_id=1, has_side_effects=True
        ),
        cost_estimate=pl.CostEstimate(flops=4 * 10**9, bytes_accessed=10**8, transcendentals=2 * 10**6),
        name="front",
    )(table, tokens, cot, segments, routes, gain_a, gain_f, router, wq, wk, wv, wo, w_in, w_out)


def rms_apply(values, gain_vec):
    inverse = lax.rsqrt(jnp.mean(values * values, axis=-1, keepdims=True) + EPSILON)
    return values * inverse * gain_vec


def per_device(
    sizes,
    tokens,
    segments,
    routes,
    cotangent,
    gain_attn,
    w_query,
    w_key,
    w_value,
    w_output,
    rel_table,
    gain_ffn,
    w_router,
    w_inner,
    w_outer,
):
    size = sizes["dp"]
    part_index = lax.axis_index("tensor")
    rows_local, model = tokens.shape
    seq_len = segments.shape[0]
    width = w_query.shape[1]
    heads = width // HD
    all_heads = rel_table.shape[1]
    hidden = w_inner.shape[2]
    shard_rows = w_query.shape[0]

    goffs = send_offsets(shard_rows, size)
    route_row = jnp.reshape(routes, (1, seq_len))
    slot_row, slot_col, plan = make_plan(route_row)
    table = jnp.transpose(
        lax.dynamic_slice_in_dim(rel_table.astype(F32), part_index * heads, heads, 1)
    )
    if size == 8:
        attn_rows, qkv, ctx, lse, w_attn, first_key, attended, x_rows, d_rows, experts = front(
            rel_table.astype(F32), tokens, cotangent, segments[None, :], routes, gain_attn[None, :],
            gain_ffn[None, :], w_router, w_query, w_key, w_value, w_output, w_inner, w_outer,
        )
        expert_pieces = [[experts]] * E
        offsets = jnp.zeros((1,), jnp.int32)
        normed_attn, norm_one_pull = jax.vjp(rms_apply, tokens, gain_attn.astype(F32))
        xd = jnp.concatenate([x_rows, d_rows], axis=1)
    else:
        attn_shard = jnp.concatenate([w_query, w_key, w_value, jnp.transpose(w_output)], axis=1)
        attn_pieces, offsets = gather_dp(attn_shard, size)
        both_shard = jnp.concatenate([w_inner, jnp.transpose(w_outer, (0, 2, 1))], axis=2)
        expert_pieces = [gather_dp(both_shard[e], size)[0] for e in range(E)]
        counts = [jnp.sum((segments < s).astype(jnp.int32)) for s in range(1, 5)]
        first_key = jnp.zeros_like(segments)
        for s in range(1, 5):
            first_key = jnp.where(segments >= s, counts[s - 1], first_key)
        first_key = first_key[None, :]
        normed_attn, norm_one_pull = jax.vjp(rms_apply, tokens, gain_attn.astype(F32))
        attn_rows = lax.all_gather(normed_attn.astype(BF), "tensor", axis=0, tiled=True)
        qkv, ctx, lse, branch, w_attn = attend(
            attn_rows, attn_pieces, offsets, table, first_key, heads
        )
        attended = tokens + lax.psum_scatter(
            branch, "tensor", scatter_dimension=0, tiled=True
        ).astype(F32)

    normed_ffn, norm_two_pull = jax.vjp(rms_apply, attended, gain_ffn.astype(F32))
    ffn_in = normed_ffn.astype(BF)
    local_routes = lax.dynamic_slice_in_dim(routes[:, 0], part_index * rows_local, rows_local, 0)
    route_mask = (local_routes[:, None] == jnp.arange(E, dtype=jnp.int32)[None, :]).astype(F32)

    def gate_of(normed_values, router_values):
        logits = jnp.dot(normed_values, router_values, precision=lax.Precision.HIGHEST)
        return jnp.sum(jax.nn.softmax(logits, axis=-1) * route_mask, axis=-1)

    gate_weight, gate_pull = jax.vjp(gate_of, ffn_in.astype(F32), w_router.astype(F32))
    if size != 8:
        d_expert = (cotangent * gate_weight[:, None]).astype(BF)
        xd = lax.all_gather(
            jnp.concatenate([ffn_in, d_expert], axis=1), "tensor", axis=0, tiled=True
        )

    terms = None
    expert_sums = []
    for e in range(E):
        terms, parts = expert(
            e, plan, offsets, goffs, xd, slot_row, slot_col, terms, expert_pieces[e], size
        )
        expert_sums.append(reduce_dp(parts, size))
    sums = lax.psum_scatter(terms, "tensor", scatter_dimension=0, tiled=True).astype(F32)
    expert_out, d_ffn_local = sums[:, :model], sums[:, model:]
    output = attended + gate_weight[:, None] * expert_out
    d_gate = jnp.sum(cotangent * expert_out, axis=-1)

    d_ffn_router, grad_router_local = gate_pull(d_gate)
    d_attended_norm, grad_gain_two = norm_two_pull(d_ffn_local + d_ffn_router)
    d_attended = cotangent + d_attended_norm
    d_branch_rows = lax.all_gather(d_attended.astype(BF), "tensor", axis=0, tiled=True)

    total_rows, diag, attn_parts = attend_back(
        d_branch_rows, w_attn, qkv, ctx, lse, first_key, attn_rows, table, goffs, heads, size
    )
    attn_sum = reduce_dp(attn_parts, size)
    d_attn_local = lax.psum_scatter(
        total_rows, "tensor", scatter_dimension=0, tiled=True
    ).astype(F32)
    d_tokens_norm, grad_gain_one = norm_one_pull(d_attn_local)
    grad_tokens = d_attended + d_tokens_norm

    onehot = jnp.asarray((BUCKETS[:HALF, None] == np.arange(NBKT - 1)[None, :]).astype(np.float32))
    near_sums = jnp.dot(onehot.T, diag[:heads].T, precision=lax.Precision.HIGHEST)
    table_local = jnp.concatenate([near_sums, -jnp.sum(near_sums, axis=0, keepdims=True)], axis=0)
    grad_table_full = lax.dynamic_update_slice_in_dim(
        jnp.zeros((NBKT, all_heads), F32), table_local, part_index * heads, 1
    )
    small_sums = lax.psum(
        (grad_gain_one, grad_gain_two, grad_router_local, grad_table_full), ("dp", "tensor")
    )
    grad_inner = jnp.stack([s[:, :hidden] for s in expert_sums])
    grad_outer = jnp.stack([jnp.transpose(s[:, hidden:]) for s in expert_sums])
    return (
        output,
        grad_tokens,
        small_sums[0],
        attn_sum[:, :width],
        attn_sum[:, width : 2 * width],
        attn_sum[:, 2 * width : 3 * width],
        jnp.transpose(attn_sum[:, 3 * width :]),
        small_sums[3],
        small_sums[1],
        small_sums[2],
        grad_inner,
        grad_outer,
    )


def solution(mesh):
    sizes = dict(mesh.shape)
    in_specs = (
        P(("dp", "tensor"), None),
        P("dp"),
        P("dp", None),
        P(("dp", "tensor"), None),
        P(),
        P("dp", "tensor"),
        P("dp", "tensor"),
        P("dp", "tensor"),
        P("tensor", "dp"),
        P(),
        P(),
        P(),
        P(None, "dp", "tensor"),
        P(None, "tensor", "dp"),
    )
    out_specs = (
        P(("dp", "tensor"), None),
        P(("dp", "tensor"), None),
        P(),
        P("dp", "tensor"),
        P("dp", "tensor"),
        P("dp", "tensor"),
        P("tensor", "dp"),
        P(),
        P(),
        P(),
        P(None, "dp", "tensor"),
        P(None, "tensor", "dp"),
    )
    return jax.shard_map(
        functools.partial(per_device, sizes),
        mesh=mesh,
        in_specs=in_specs,
        out_specs=out_specs,
        check_vma=False,
    )
```

```python
import functools
import math

import jax
import jax.numpy as jnp
import numpy as np
from jax import lax
from jax.experimental import pallas as pl
from jax.experimental.pallas import tpu as pltpu
from jax.sharding import PartitionSpec as P

HD = 64
NBKT = 32
MAXD = 128
E = 4
WIN = 1024
QT = 256
HALF = 128
ROWS = 256

EPSILON = 1e-06
NEG_LARGE = -1e30
BF = jnp.bfloat16
F32 = jnp.float32
VMEM_MAX = 56 * 1024 * 1024


def bucket_numbers(window, buckets, far_distance):
    distance = np.arange(window)
    exact_part = buckets // 2
    safe_distance = np.maximum(distance, 1) * 1.0
    log_part = exact_part + np.floor(
        np.log(safe_distance / exact_part)
        / np.log(far_distance / exact_part)
        * (buckets - exact_part)
    ).astype(np.int32)
    log_part = np.minimum(log_part, buckets - 1)
    return np.where(distance < exact_part, distance, log_part).astype(np.int32)


BUCKETS = bucket_numbers(WIN, NBKT, MAXD)
FIRST = [int(np.argmax(BUCKETS == b)) for b in range(NBKT)]
NEAR = FIRST[NBKT - 1]


def nn(a, b):
    return lax.dot_general(a, b, (((1,), (0,)), ((), ())), preferred_element_type=F32)


def nt(a, b):
    return lax.dot_general(a, b, (((1,), (1,)), ((), ())), preferred_element_type=F32)


def tn(a, b):
    return lax.dot_general(a, b, (((0,), (0,)), ((), ())), preferred_element_type=F32)


class Names:
    pass


def iota(shape, dim):
    return lax.broadcasted_iota(jnp.int32, shape, dim)


def gather_dp(shard):
    return lax.all_gather(shard, "dp", axis=0, tiled=True)


def reduce_dp(part):
    return lax.psum_scatter(part, "dp", scatter_dimension=0, tiled=True).astype(F32)


def plan_kernel(route_ref, slot_row_ref, slot_col_ref, plan_ref):
    length = route_ref.shape[1]
    route = route_ref[...]
    chosen = jnp.where(iota((8, length), 0) == route, 1.0, 0.0).astype(F32)
    upper = jnp.where(iota((length, length), 0) < iota((length, length), 1), 1.0, 0.0)
    before = nn(chosen.astype(BF), upper.astype(BF))
    rank = jnp.sum(chosen * before, axis=0, keepdims=True)
    start = jnp.int32(0)
    base = jnp.zeros((1, length), F32)
    for e in range(E):
        here = route == e
        count = jnp.sum(jnp.where(here, 1, 0))
        tiles = (count + (ROWS - 1)) // ROWS
        plan_ref[e] = tiles
        plan_ref[E + e] = start
        base = base + jnp.where(here, start.astype(F32), 0.0)
        start = start + tiles * ROWS
    slots = jnp.broadcast_to(rank + base, (8, length))
    slot_row_ref[...] = slots.astype(jnp.int32)
    slot_col_ref[...] = jnp.transpose(slots).astype(jnp.int32)


def make_plan(route_row):
    length = route_row.shape[1]
    return pl.pallas_call(
        plan_kernel,
        out_shape=(
            jax.ShapeDtypeStruct((8, length), jnp.int32),
            jax.ShapeDtypeStruct((length, 8), jnp.int32),
            jax.ShapeDtypeStruct((2 * E,), jnp.int32),
        ),
        in_specs=[pl.BlockSpec(memory_space=pltpu.VMEM)],
        out_specs=(
            pl.BlockSpec(memory_space=pltpu.VMEM),
            pl.BlockSpec(memory_space=pltpu.VMEM),
            pl.BlockSpec(memory_space=pltpu.SMEM),
        ),
        compiler_params=pltpu.CompilerParams(vmem_limit_bytes=VMEM_MAX),
        name="route_plan",
    )(route_row)


def fill_bias(bias_ref, table_ref, heads):
    step = iota((HALF, HALF), 1) - iota((HALF, HALF), 0)
    for side in range(2):
        distance = step + side * HALF
        tiles = [jnp.full((HALF, HALF), table_ref[h, NBKT - 1], F32) for h in range(heads)]
        for b in reversed(range(NBKT - 1)):
            below = distance < FIRST[b + 1]
            tiles = [jnp.where(below, table_ref[h, b], tiles[h]) for h in range(heads)]
        for h in range(heads):
            bias_ref[h, side] = tiles[h]


def biased_scores(raw, gap, h, bias_ref, table_ref, first_key, key_start):
    far = table_ref[h, NBKT - 1]
    keys = key_start + iota((QT, QT), 0)
    if gap >= 2:
        return jnp.where(keys >= first_key, raw + far, NEG_LARGE)
    diag, near = bias_ref[h, 0], bias_ref[h, 1]
    const = jnp.full((HALF, HALF), far, F32)
    if gap == 1:
        tile = jnp.concatenate(
            [
                jnp.concatenate([const, const], axis=1),
                jnp.concatenate([near, const], axis=1),
            ],
            axis=0,
        )
        return jnp.where(keys >= first_key, raw + tile, NEG_LARGE)
    tile = jnp.concatenate(
        [jnp.concatenate([diag, near], axis=1), jnp.concatenate([const, diag], axis=1)], axis=0
    )
    causal = iota((QT, QT), 0) <= iota((QT, QT), 1)
    return jnp.where((keys >= first_key) & causal, raw + tile, NEG_LARGE)


def attend_blocks(heads, seq, first_ref, table_ref, q_t, v_t, kn, bias_ref, s_ref, ctx_t, lse_ref, blocks):
    for i in blocks:
        cols = slice(i * QT, (i + 1) * QT)
        first_key = first_ref[0:1, cols]
        for h in range(heads):
            band = slice(h * HD, (h + 1) * HD)
            q_blk = q_t[band, cols]
            peak = None
            for j in range(i + 1):
                raw = nn(kn[h, j * QT : (j + 1) * QT], q_blk)
                s = biased_scores(raw, i - j, h, bias_ref, table_ref, first_key, j * QT)
                s_ref[h * QT : (h + 1) * QT, j * QT : (j + 1) * QT] = s
                top = jnp.max(s, axis=0, keepdims=True)
                peak = top if peak is None else jnp.maximum(peak, top)
            total = jnp.zeros((1, QT), F32)
            acc = jnp.zeros((HD, QT), F32)
            for j in range(i + 1):
                p = jnp.exp(s_ref[h * QT : (h + 1) * QT, j * QT : (j + 1) * QT] - peak)
                total = total + jnp.sum(p, axis=0, keepdims=True)
                acc = acc + nn(v_t[band, j * QT : (j + 1) * QT], p.astype(BF))
            ctx_t[band, cols] = (acc / total).astype(BF)
            lse_ref[h : h + 1, cols] = peak + jnp.log(total)


def project(heads, x, w_ref, qkv_ref, q_t, v_t, kn):
    width = heads * HD
    qkv = nn(x, w_ref[:, : 3 * width]).astype(BF)
    qkv_ref[...] = qkv
    q_t[...] = jnp.transpose(qkv[:, :width]) * jnp.asarray(1.0 / math.sqrt(HD), BF)
    v_t[...] = jnp.transpose(qkv[:, 2 * width :])
    for h in range(heads):
        kn[h] = qkv[:, width + h * HD : width + (h + 1) * HD]


def attend_kernel(heads, table_ref, x_ref, first_ref, w_ref, *refs):
    qkv_ref, ctx_ref, lse_ref, branch_ref, q_t, v_t, kn, bias_ref, s_ref, ctx_t = refs
    width = heads * HD
    seq = x_ref.shape[0]
    fill_bias(bias_ref, table_ref, heads)
    project(heads, x_ref[...], w_ref, qkv_ref, q_t, v_t, kn)
    blocks = range(seq // QT)
    attend_blocks(
        heads, seq, first_ref, table_ref, q_t, v_t, kn, bias_ref, s_ref, ctx_t, lse_ref, blocks
    )
    ctx = jnp.transpose(ctx_t[...])
    ctx_ref[...] = ctx
    branch_ref[...] = nt(ctx, w_ref[:, 3 * width :]).astype(BF)


def attend(x, w, table, first_key, heads):
    seq, model = x.shape
    width = heads * HD
    vmem = pl.BlockSpec(memory_space=pltpu.VMEM)
    return pl.pallas_call(
        functools.partial(attend_kernel, heads),
        out_shape=(
            jax.ShapeDtypeStruct((seq, 3 * width), BF),
            jax.ShapeDtypeStruct((seq, width), BF),
            jax.ShapeDtypeStruct((8, seq), F32),
            jax.ShapeDtypeStruct((seq, model), BF),
        ),
        in_specs=[pl.BlockSpec(memory_space=pltpu.SMEM)] + [vmem] * 3,
        out_specs=(vmem,) * 4,
        scratch_shapes=[
            pltpu.VMEM((width, seq), BF),
            pltpu.VMEM((width, seq), BF),
            pltpu.VMEM((heads, seq, HD), BF),
            pltpu.VMEM((heads, 2, HALF, HALF), F32),
            pltpu.VMEM((heads * QT, seq), F32),
            pltpu.VMEM((width, seq), BF),
        ],
        compiler_params=pltpu.CompilerParams(vmem_limit_bytes=VMEM_MAX),
        cost_estimate=pl.CostEstimate(flops=4 * 10**9, bytes_accessed=10**7, transcendentals=2 * 10**6),
        name="attend",
    )(table, x, first_key, w)


def attend_back_block(heads, s, j, seq):
    width = heads * HD
    keys = slice(j * QT, (j + 1) * QT)
    for h in range(heads):
        band = slice(h * HD, (h + 1) * HD)
        dk = jnp.zeros((QT, HD), F32)
        dv = jnp.zeros((QT, HD), F32)
        for i in range(j, seq // QT):
            cols = slice(i * QT, (i + 1) * QT)
            raw = nn(s.kn[h, keys], s.q_t[band, cols])
            scores = biased_scores(raw, i - j, h, s.bias, s.tab, s.first[0:1, cols], j * QT)
            p = jnp.exp(scores - s.lse[h : h + 1, cols])
            dp = nn(s.vn[h, keys], s.dc_t[band, cols])
            ds = p * (dp - s.delta[h : h + 1, cols])
            if i == j:
                s.near[h, 0] += ds[:HALF, :HALF] + ds[HALF:, HALF:]
                s.near[h, 1] += ds[:HALF, HALF:]
            elif i == j + 1:
                s.near[h, 1] += ds[HALF:, :HALF]
            ds = ds.astype(BF)
            dv = dv + nn(p.astype(BF), s.dcn[h, cols])
            dk = dk + nn(ds, s.qn[h, cols])
            s.dq_t[band, cols] += nn(s.k_t[band, keys], ds)
        s.dqkv[keys, width + h * HD : width + (h + 1) * HD] = dk.astype(BF)
        s.dqkv[keys, 2 * width + h * HD : 2 * width + (h + 1) * HD] = dv.astype(BF)


def diagonal_lines(heads, near):
    key, query = iota((HALF, HALF), 0), iota((HALF, HALF), 1)
    lines = []
    for h in range(heads):
        both = near[h, 0] + jnp.where(query < key, near[h, 1], 0.0)
        for bit in range(7):
            turned = pltpu.roll(both, HALF - (1 << bit), 1)
            both = jnp.where((key >> bit) & 1 == 1, turned, both)
        lines.append(jnp.sum(both, axis=0, keepdims=True))
    return lines


def attend_back_kernel(heads, blocks, names, *refs):
    s = Names()
    for name, ref in zip(names, refs):
        setattr(s, name, ref)
    grads = refs[len(names) :]
    width = heads * HD
    seq = s.d.shape[0]
    scale = jnp.asarray(1.0 / math.sqrt(HD), BF)
    fill_bias(s.bias, s.tab, heads)
    d_rows = s.d[...]
    ctx = s.ctx[...]
    dc = nn(d_rows, s.w[:, 3 * width :]).astype(BF)
    s.acc[:, 3 * width :] = tn(d_rows, ctx)
    dct = jnp.transpose(dc)
    s.dc_t[...] = dct
    qkv = s.qkv[...]
    s.q_t[...] = jnp.transpose(qkv[:, :width]) * scale
    s.k_t[...] = jnp.transpose(qkv[:, width : 2 * width])
    product = dct.astype(F32) * jnp.transpose(ctx).astype(F32)
    for h in range(heads):
        band = slice(h * HD, (h + 1) * HD)
        s.qn[h] = qkv[:, band] * scale
        s.kn[h] = qkv[:, width + h * HD : width + (h + 1) * HD]
        s.vn[h] = qkv[:, 2 * width + h * HD : 2 * width + (h + 1) * HD]
        s.dcn[h] = dc[:, band]
        s.delta[h : h + 1] = jnp.sum(product[band], axis=0, keepdims=True)
    s.dq_t[...] = jnp.zeros_like(s.dq_t)
    s.near[...] = jnp.zeros_like(s.near)
    for j in range(seq // QT):
        attend_back_block(heads, s, j, seq)
    s.dqkv[:, :width] = jnp.transpose((s.dq_t[...] * (1.0 / math.sqrt(HD))).astype(BF))
    d_qkv = s.dqkv[...]
    s.rows[...] = nt(d_qkv, s.w[:, : 3 * width]).astype(BF)
    s.acc[:, : 3 * width] = tn(s.x[...], d_qkv)
    scatter_rows(s.acc, s.offs, grads, blocks)
    lines = diagonal_lines(heads, s.near) + [jnp.zeros((8 - heads, HALF), F32)]
    s.diag[...] = jnp.concatenate(lines, axis=0)


def scatter_rows(acc_ref, offs_ref, outs, blocks):
    k = 0
    for out, count in zip(outs, blocks):
        rows = out.shape[1]
        for b in range(count):
            at = pl.ds(pl.multiple_of(offs_ref[k], rows), rows)
            out[b] = acc_ref[at, :].astype(BF)
            k += 1


def attend_back(d_rows, w, qkv, ctx, lse, first_key, x, table, offs, heads):
    seq, model = x.shape
    width = heads * HD
    vmem = pl.BlockSpec(memory_space=pltpu.VMEM)
    smem = pl.BlockSpec(memory_space=pltpu.SMEM)
    scratch = [
        ("q_t", (width, seq), BF),
        ("k_t", (width, seq), BF),
        ("dc_t", (width, seq), BF),
        ("kn", (heads, seq, HD), BF),
        ("vn", (heads, seq, HD), BF),
        ("qn", (heads, seq, HD), BF),
        ("dcn", (heads, seq, HD), BF),
        ("bias", (heads, 2, HALF, HALF), F32),
        ("dq_t", (width, seq), F32),
        ("dqkv", (seq, 3 * width), BF),
        ("near", (heads, 2, HALF, HALF), F32),
        ("delta", (8, seq), F32),
        ("acc", (model, 4 * width), F32),
    ]
    ins = ["offs", "tab", "d", "w", "qkv", "ctx", "lse", "first", "x"]
    names = ins + ["rows", "diag", "grads"] + [c[0] for c in scratch]

    def kernel(*refs):
        at = len(ins) + 2
        plain = refs[:at] + refs[at + 1 :]
        attend_back_kernel(
            heads, (1,), names[:at] + names[at + 1 :], *plain, refs[at]
        )

    out = pl.pallas_call(
        kernel,
        out_shape=(
            jax.ShapeDtypeStruct((seq, model), BF),
            jax.ShapeDtypeStruct((8, HALF), F32),
            jax.ShapeDtypeStruct((1, model, 4 * width), BF),
        ),
        in_specs=[smem, smem] + [vmem] * 7,
        out_specs=(vmem,) * 3,
        scratch_shapes=[pltpu.VMEM(c[1], c[2]) for c in scratch],
        compiler_params=pltpu.CompilerParams(vmem_limit_bytes=VMEM_MAX),
        cost_estimate=pl.CostEstimate(flops=10**10, bytes_accessed=10**7, transcendentals=2 * 10**6),
        name="attend_back",
    )(offs, table, d_rows, w, qkv, ctx, lse, first_key, x)
    return out[0], out[1], out[2]


def expert_kernel(e, plan_ref, offs_ref, xd_ref, row_ref, col_ref, w_ref, *refs):
    terms_in = refs[0] if e > 0 else None
    terms_ref, grad, acc_ref = refs[-3:]
    model = xd_ref.shape[1] // 2
    hidden = w_ref.shape[1] // 2
    length = xd_ref.shape[0]
    terms_ref[...] = jnp.zeros_like(terms_ref) if terms_in is None else terms_in[...]
    acc_ref[...] = jnp.zeros_like(acc_ref)
    base = plan_ref[E + e]

    @pl.loop(0, plan_ref[e])
    def _(t):
        start = base + t * ROWS
        pick = jnp.where(row_ref[0:1, :] == start + iota((ROWS, length), 0), 1.0, 0.0).astype(BF)
        xd = nn(pick, xd_ref[...]).astype(BF)
        x, d = xd[:, :model], xd[:, model:]
        inner = nn(x, w_ref[:, :hidden])
        cubic = 0.044715 * inner * inner
        tanh = jnp.tanh(math.sqrt(2.0 / math.pi) * inner * (1.0 + cubic))
        half = 0.5 * (1.0 + tanh)
        active = (inner * half).astype(BF)
        slope = half + (0.5 * math.sqrt(2.0 / math.pi)) * inner * (1.0 - tanh * tanh) * (1.0 + 3.0 * cubic)
        out = nt(active, w_ref[:, hidden:]).astype(BF)
        d_inner = (nn(d, w_ref[:, hidden:]) * slope).astype(BF)
        acc_ref[:, :hidden] += tn(x, d_inner)
        acc_ref[:, hidden:] += tn(d, active)
        d_x = nt(d_inner, w_ref[:, :hidden]).astype(BF)
        place = jnp.where(col_ref[:, 0:1] == start + iota((length, ROWS), 1), 1.0, 0.0).astype(BF)
        terms_ref[:, :model] = (terms_ref[:, :model].astype(F32) + nn(place, out)).astype(BF)
        terms_ref[:, model:] = (terms_ref[:, model:].astype(F32) + nn(place, d_x)).astype(BF)

    scatter_rows(acc_ref, offs_ref, [grad], (1,))


def expert(e, plan, offs, xd, slot_row, slot_col, terms, w):
    length, both = xd.shape
    model, hidden2 = w.shape
    vmem = pl.BlockSpec(memory_space=pltpu.VMEM)
    smem = pl.BlockSpec(memory_space=pltpu.SMEM)
    extra = [] if terms is None else [terms]
    return pl.pallas_call(
        functools.partial(expert_kernel, e),
        out_shape=(
            jax.ShapeDtypeStruct((length, both), BF),
            jax.ShapeDtypeStruct((1, model, hidden2), BF),
        ),
        in_specs=[smem] * 2 + [vmem] * (4 + len(extra)),
        out_specs=(vmem,) * 2,
        scratch_shapes=[pltpu.VMEM((model, hidden2), F32)],
        compiler_params=pltpu.CompilerParams(vmem_limit_bytes=VMEM_MAX),
        cost_estimate=pl.CostEstimate(flops=3 * 10**9, bytes_accessed=10**7, transcendentals=10**6),
        name=f"expert_{e}",
    )(plan, offs, xd, slot_row, slot_col, w, *extra)


MESH = pl.DeviceIdType.MESH
PIECES = 1 + 2 * E
T_SEMS = 48
W_SEMS = 7 * PIECES
G_SEMS = 4 * (2 * E + 1)
OTHERS = 4


class Here:
    def __init__(self):
        self.d = lax.axis_index("dp")
        self.t = lax.axis_index("tensor")
        self.z, self.y = self.d // 2, self.d % 2
        self.x, self.c = self.t // 2, self.t % 2
        self.core = {"dp": self.d, "tensor": 2 * self.x + 1 - self.c}
        self.side = {"dp": self.d, "tensor": 2 * (1 - self.x) + self.c}
        self.over = {"dp": 2 * self.z + 1 - self.y, "tensor": self.t}

    def z_dp(self, k):
        return 2 * ((self.z + 4 + k) % 4) + self.y

    def z_peer(self, k):
        return {"dp": self.z_dp(k), "tensor": self.t}

    def greet(self):
        barrier = pltpu.get_barrier_semaphore()
        peers = [self.core, self.side, self.over] + [self.z_peer(k) for k in (1, 2, 3)]
        for peer in peers:
            pl.semaphore_signal(barrier, inc=1, device_id=peer, device_id_type=MESH)
        pl.semaphore_wait(barrier, len(peers))


class Wire:
    def __init__(self, send, recv):
        self.send, self.recv, self.sent, self.count = send, recv, [], 0

    def __call__(self, src, dst, peer):
        k = self.count
        self.count += 1
        copy = pltpu.make_async_remote_copy(
            src_ref=src, dst_ref=dst, send_sem=self.send.at[k], recv_sem=self.recv.at[k],
            device_id=peer, device_id_type=MESH,
        )
        copy.start()
        self.sent.append(copy)
        return copy

    def settle(self):
        for copy in self.sent:
            copy.wait_send()
        self.sent = []


class Rows:
    def __init__(self, here, wire, buf, rows, part, parts):
        self.here, self.wire, self.buf = here, wire, buf
        self.rows, self.size = rows, rows // parts
        self.shift = part * self.size

    def at(self, t):
        return self.buf.at[pl.ds(pl.multiple_of(t * self.rows + self.shift, 16), self.size)]

    def start(self):
        mine = self.at(self.here.t)
        self.far = self.wire(mine, mine, self.here.side)
        self.near = self.wire(mine, mine, self.here.core)

    def forward(self):
        self.far.wait_recv()
        theirs = self.at(2 * (1 - self.here.x) + self.here.c)
        self.last = self.wire(theirs, theirs, self.here.core)

    def finish(self):
        self.near.wait_recv()
        self.last.wait_recv()


class Sums:
    def __init__(self, here, wire, src, landed, out, back, rows, part, parts):
        self.here, self.wire, self.src = here, wire, src
        self.landed, self.out, self.back = landed, out, back
        self.rows, self.size = rows, rows // parts
        self.shift = part * self.size
        self.part = part

    def at(self, t):
        return pl.ds(pl.multiple_of(t * self.rows + self.shift, 16), self.size)

    def start(self):
        h = self.here
        self.copies = []
        for slot, x in ((0, 1 - h.x), (1, h.x)):
            src = self.src.at[self.at(2 * x + 1 - h.c)]
            self.copies.append(self.wire(src, self.landed.at[slot, self.part], h.core))

    def cross(self):
        h = self.here
        self.copies[0].wait_recv()
        mine = self.src[self.at(2 * (1 - h.x) + h.c)].astype(F32)
        self.out[self.part] = (mine + self.landed[0, self.part].astype(F32)).astype(BF)
        self.last = self.wire(self.out.at[self.part], self.back.at[self.part], h.side)

    def total(self):
        h = self.here
        self.copies[1].wait_recv()
        near = self.src[self.at(2 * h.x + h.c)].astype(F32) + self.landed[1, self.part].astype(F32)
        self.last.wait_recv()
        return near + self.back[self.part].astype(F32)


class Weights:
    def __init__(self, here, wire, own_sem, sources, target):
        self.here, self.wire, self.own_sem = here, wire, own_sem
        self.sources, self.target = sources, target
        self.z, self.over, self.own = {}, {}, {}

    def at(self, p, dp):
        rows = self.sources[p].shape[0]
        return self.target(p, pl.ds(pl.multiple_of(dp * rows, 16), rows))

    def start(self, p):
        if p >= PIECES:
            return
        h, src = self.here, self.sources[p]
        dst = self.at(p, h.d)
        self.z[p] = [self.wire(src, dst, h.z_peer(k)) for k in (1, 2, 3)]
        self.over[p] = [self.wire(src, dst, h.over)]
        self.own[p] = pltpu.make_async_copy(src, dst, self.own_sem.at[p])
        self.own[p].start()

    def forward(self, p):
        if p >= PIECES:
            return
        h = self.here
        for k, copy in zip((1, 2, 3), self.z[p]):
            copy.wait_recv()
            part = self.at(p, h.z_dp(-k))
            self.over[p].append(self.wire(part, part, h.over))

    def finish(self, p):
        for copy in self.over[p]:
            copy.wait_recv()
        self.own[p].wait()


def normed(values, gain):
    inverse = lax.rsqrt(jnp.mean(values * values, axis=-1, keepdims=True) + EPSILON)
    return values * inverse * gain


class Reduce:
    def __init__(self, here, wire, local, mine, other, y_land, z_land, y_stage, z_stage):
        self.here, self.wire, self.local = here, wire, local
        self.mine, self.other, self.y_land, self.z_land = mine, other, y_land, z_land
        self.y_stage, self.z_stage = y_stage, z_stage
        self.y, self.z = {}, {}

    def start(self, q, acc, shard):
        h = self.here
        slot = q % OTHERS
        if q >= OTHERS:
            self.y[q - OTHERS].wait_send()
        for k in range(4):
            for side, target in ((h.y, self.mine.at[q]), (1 - h.y, self.other.at[slot])):
                at = pl.ds(pl.multiple_of((2 * ((h.z + k) % 4) + side) * shard, 16), shard)
                target[k] = acc[at, : target.shape[2]].astype(BF)
        self.y[q] = self.wire(self.other.at[slot], self.y_land.at[q], h.over)

    def arrive(self, q):
        h = self.here
        self.y[q].wait_recv()
        copy = pltpu.make_async_copy(self.y_land.at[q], self.y_stage, self.local.at[0])
        copy.start()
        copy.wait()
        self.z[q] = []
        for k in (1, 2, 3, 0):
            pair = self.mine[q, k].astype(F32) + self.y_stage[k].astype(F32)
            self.mine[q, k] = pair.astype(BF)
            if k:
                self.z[q].append(
                    self.wire(self.mine.at[q, k], self.z_land.at[q, k - 1], h.z_peer(k))
                )

    def total(self, q):
        for copy in self.z[q]:
            copy.wait_recv()
        copy = pltpu.make_async_copy(self.z_land.at[q], self.z_stage, self.local.at[1])
        copy.start()
        copy.wait()
        result = self.mine[q, 0].astype(F32)
        for k in range(3):
            result = result + self.z_stage[k].astype(F32)
        return result

    def close(self):
        for q in self.y:
            if q + OTHERS not in self.y:
                self.y[q].wait_send()
        for copies in self.z.values():
            for copy in copies:
                copy.wait_send()


def add_everywhere(here, wire, value, land):
    for k, peer in enumerate((here.core, here.side, here.over)):
        land[2 * k] = value
        copy = wire(land.at[2 * k], land.at[2 * k + 1], peer)
        copy.wait_recv()
        value = value + land[2 * k + 1]
    own = 6 + here.z
    land[own] = value
    copies = [wire(land.at[own], land.at[own], here.z_peer(k)) for k in (1, 2, 3)]
    for copy in copies:
        copy.wait_recv()
    return (land[6] + land[7]) + (land[8] + land[9])


def norm_back(values, gain, d_normed):
    inverse = lax.rsqrt(jnp.mean(values * values, axis=-1, keepdims=True) + EPSILON)
    scaled = d_normed * gain
    inner = jnp.mean(scaled * values, axis=-1, keepdims=True)
    grad = inverse * scaled - values * (inverse * inverse * inverse * inner)
    return grad, jnp.sum(d_normed * values * inverse, axis=0, keepdims=True)


def gate_parts(normed_rows, router, route):
    logits = nn(normed_rows, router)
    raised = jnp.exp(logits - jnp.max(logits, axis=1, keepdims=True))
    probs = raised / jnp.sum(raised, axis=1, keepdims=True)
    chosen = jnp.where(route == iota(logits.shape, 1), 1.0, 0.0)
    return probs, chosen, jnp.sum(probs * chosen, axis=1, keepdims=True)


def expert_dense(e, w, s, route_ref):
    model = s.x_rows.shape[1]

    @pl.loop(0, s.x_rows.shape[0] // ROWS)
    def _(t):
        at = pl.ds(pl.multiple_of(t * ROWS, ROWS), ROWS)
        here = route_ref[at, :] == e
        inner = nn(s.x_rows[at], w[0])
        cubic = 0.044715 * inner * inner
        tanh = jnp.tanh(math.sqrt(2.0 / math.pi) * inner * (1.0 + cubic))
        half = 0.5 * (1.0 + tanh)
        active = jnp.where(here, inner * half, 0.0).astype(BF)
        slope = half + (0.5 * math.sqrt(2.0 / math.pi)) * inner * (1.0 - tanh * tanh) * (
            1.0 + 3.0 * cubic
        )
        d_inner = jnp.where(here, nn(s.d_rows[at], w[1]) * slope, 0.0).astype(BF)
        s.active[at] = active
        s.d_inner[at] = d_inner
        out = nt(active, w[1]).astype(BF)
        d_x = nt(d_inner, w[0]).astype(BF)
        if e == 0:
            s.terms[at, :model] = out
            s.terms[at, model:] = d_x
        else:
            s.terms[at, :model] = jnp.where(here, out, s.terms[at, :model])
            s.terms[at, model:] = jnp.where(here, d_x, s.terms[at, model:])


def layer_kernel(heads, names, *refs):
    s = Names()
    for name, ref in zip(names, refs):
        setattr(s, name, ref)
    h = Here()
    width = heads * HD
    seq, model = s.attn_rows.shape
    rows = s.tokens.shape[0]
    half = rows // 2
    shard = s.wq.shape[0]
    wire = Wire(s.t_send, s.t_recv)
    sources = [s.attn_shard]
    for e in range(E):
        sources += [s.w_in.at[e], s.outer_shard.at[e]]

    def target(p, at):
        return s.w_attn.at[at] if p == 0 else s.experts.at[p - 1, at]

    weights = Weights(h, Wire(s.w_send, s.w_recv), s.own_sem, sources, target)
    reduce = Reduce(
        h, Wire(s.g_send, s.g_recv), s.local_sem, s.mine, s.other, s.y_land, s.z_land,
        s.y_stage, s.z_stage,
    )
    s.attn_shard[:, :width] = s.wq[...]
    s.attn_shard[:, width : 2 * width] = s.wk[...]
    s.attn_shard[:, 2 * width : 3 * width] = s.wv[...]
    s.attn_shard[:, 3 * width :] = jnp.transpose(s.wo[...])
    h.greet()
    weights.start(0)

    def block(part):
        return pl.ds(pl.multiple_of(h.t * rows + part * half, 16), half)

    gathers = [Rows(h, wire, s.attn_rows, rows, part, 2) for part in range(2)]
    gain_a = s.gain_a[...].astype(F32)
    for part in range(2):
        s.attn_rows[block(part)] = normed(
            s.tokens[part * half : (part + 1) * half], gain_a
        ).astype(BF)
        gathers[part].start()
    s.d_rows[pl.ds(pl.multiple_of(h.t * rows, 16), rows)] = s.cot[...].astype(BF)
    for hd in range(heads):
        for b in range(NBKT):
            s.tab[hd, b] = s.table[b, h.t * heads + hd]
    fill_bias(s.bias, s.tab, heads)
    segments = s.segments[...]
    first = jnp.zeros(segments.shape, jnp.int32)
    for seg in range(1, 5):
        first = jnp.where(segments >= seg, jnp.sum(jnp.where(segments < seg, 1, 0)), first)
    s.first[...] = jnp.broadcast_to(first, s.first.shape)
    for e in range(E):
        s.outer_shard[e] = jnp.transpose(s.w_out[e])
    gathers[0].forward()
    gathers[1].forward()
    weights.forward(0)
    weights.start(1)
    weights.start(2)
    weights.start(3)
    gathers[0].finish()
    gathers[1].finish()
    cots = Rows(h, wire, s.d_rows, rows, 0, 1)
    cots.start()
    weights.finish(0)

    project(heads, s.attn_rows[...], s.w_attn, s.qkv, s.q_t, s.v_t, s.kn)
    state = (s.first, s.tab, s.q_t, s.v_t, s.kn, s.bias, s.acc, s.ctx_t, s.lse)
    attend_blocks(heads, seq, *state, range(0, 3))
    cots.forward()
    weights.forward(1)
    weights.start(4)
    attend_blocks(heads, seq, *state, range(3, seq // QT))
    s.ctx[...] = jnp.transpose(s.ctx_t[...])
    s.branch[...] = nt(s.ctx[...], s.w_attn[:, 3 * width :]).astype(BF)
    narrow = [ref.at[:, :, :, :model] for ref in (s.landed,)] + [
        ref.at[:, :, :model] for ref in (s.out, s.back)
    ]
    sums = [Sums(h, wire, s.branch, *narrow, rows, part, 2) for part in range(2)]
    for part in range(2):
        sums[part].start()
    for part in range(2):
        sums[part].cross()
    weights.forward(2)
    weights.start(5)

    gathers = [Rows(h, wire, s.x_rows, rows, part, 2) for part in range(2)]
    gain_f = s.gain_f[...].astype(F32)
    for part in range(2):
        at = slice(part * half, (part + 1) * half)
        attended = s.tokens[at] + sums[part].total()
        s.attended[at] = attended
        s.x_rows[block(part)] = normed(attended, gain_f).astype(BF)
        gathers[part].start()
    weights.forward(3)
    weights.start(6)
    for part in range(2):
        gathers[part].forward()
    cots.finish()
    for part in range(2):
        gathers[part].finish()
    wire.settle()
    gate = gate_parts(s.x_rows[...], s.router[...], s.routes[...])[2]
    s.d_rows[...] = (s.d_rows[...].astype(F32) * gate).astype(BF)
    s.x_t[...] = jnp.transpose(s.x_rows[...])
    s.d_t[...] = jnp.transpose(s.d_rows[...])

    def load_weights(e):
        copies = []
        for side in range(2):
            weights.finish(2 * e + 1 + side)
            copies.append(
                pltpu.make_async_copy(
                    s.experts.at[2 * e + side], s.w_buf.at[side], s.local_sem.at[2 + side]
                )
            )
            copies[-1].start()
        for copy in copies:
            copy.wait()

    for e in range(E):
        weights.forward(2 * e + 4)
        weights.start(2 * e + 7)
        load_weights(e)
        expert_dense(e, s.w_buf, s, s.routes)
        weights.forward(2 * e + 5)
        weights.start(2 * e + 8)
        s.acc[:, :model] = nn(s.x_t[...], s.d_inner[...])
        reduce.start(2 * e, s.acc, shard)
        s.acc[:, :model] = nn(s.d_t[...], s.active[...])
        reduce.start(2 * e + 1, s.acc, shard)
        if e >= 1:
            reduce.arrive(2 * e - 2)
            reduce.arrive(2 * e - 1)

    sums = [
        Sums(h, wire, s.terms, s.landed, s.out, s.back, rows, part, 2) for part in range(2)
    ]
    for part in range(2):
        sums[part].start()
    for part in range(2):
        sums[part].cross()
    reduce.arrive(2 * E - 2)
    gathers = [Rows(h, wire, s.x_rows, rows, part, 2) for part in range(2)]
    router_rows = jnp.transpose(s.router[...].astype(F32))
    small = jnp.zeros((8, model), F32)
    row_id = iota((8, model), 0)
    for part in range(2):
        at = slice(part * half, (part + 1) * half)
        attended, cot = s.attended[at], s.cot[at]
        total = sums[part].total()
        expert_out, d_normed = total[:, :model], total[:, model:]
        ffn = normed(attended, gain_f).astype(BF)
        route = s.routes[block(part), :]
        probs, chosen, gate = gate_parts(ffn, s.router[...], route)
        s.output[at] = attended + gate * expert_out
        d_gate = jnp.sum(cot * expert_out, axis=1, keepdims=True)
        d_logits = d_gate * gate * (chosen - probs)
        for e in range(E):
            d_normed = d_normed + d_logits[:, e : e + 1] * router_rows[e : e + 1]
            grad = jnp.sum(d_logits[:, e : e + 1] * ffn.astype(F32), axis=0, keepdims=True)
            small = small + jnp.where(row_id == 2 + e, grad, 0.0)
        back, gain_grad = norm_back(attended, gain_f, d_normed)
        small = small + jnp.where(row_id == 1, gain_grad, 0.0)
        d_attended = cot + back
        s.attended[at] = d_attended
        s.x_rows[block(part)] = d_attended.astype(BF)
        gathers[part].start()
    s.small[...] = small
    for part in range(2):
        gathers[part].forward()
    reduce.arrive(2 * E - 1)
    for part in range(2):
        gathers[part].finish()

    scale = jnp.asarray(1.0 / math.sqrt(HD), BF)
    d_ctx = nn(s.x_rows[...], s.w_attn[:, 3 * width :]).astype(BF)
    d_ctx_t = jnp.transpose(d_ctx)
    s.dc_t[...] = d_ctx_t
    s.k_t[...] = jnp.transpose(s.qkv[:, width : 2 * width])
    product = d_ctx_t.astype(F32) * s.ctx_t[...].astype(F32)
    for hd in range(heads):
        band = slice(hd * HD, (hd + 1) * HD)
        s.qn[hd] = s.qkv[:, band] * scale
        s.vn[hd] = s.qkv[:, 2 * width + hd * HD : 2 * width + (hd + 1) * HD]
        s.dcn[hd] = d_ctx[:, band]
        s.delta[hd : hd + 1] = jnp.sum(product[band], axis=0, keepdims=True)
    s.dq_t[...] = jnp.zeros_like(s.dq_t)
    s.near[...] = jnp.zeros_like(s.near)
    for j in range(seq // QT):
        attend_back_block(heads, s, j, seq)
    wire.settle()
    s.dqkv[:, :width] = jnp.transpose((s.dq_t[...] * (1.0 / math.sqrt(HD))).astype(BF))
    s.branch[...] = nt(s.dqkv[...], s.w_attn[:, : 3 * width]).astype(BF)
    sums = [Sums(h, wire, s.branch, *narrow, rows, part, 2) for part in range(2)]
    for part in range(2):
        sums[part].start()
    s.acc[:, : 3 * width] = tn(s.attn_rows[...], s.dqkv[...])
    s.acc[:, 3 * width : model] = tn(s.x_rows[...], s.ctx[...])
    reduce.start(2 * E, s.acc, shard)
    for part in range(2):
        sums[part].cross()
    lines = diagonal_lines(heads, s.near)
    flat = jnp.concatenate(lines, axis=1)
    small = s.small[...]
    places = jnp.concatenate([flat, flat], axis=1)
    lane = iota((8, model), 1) // flat.shape[1]
    mine = (row_id == 6 + h.t // 2) & (lane == h.t % 2)
    small = small + jnp.where(mine, places, 0.0)

    for part in range(2):
        at = slice(part * half, (part + 1) * half)
        back, gain_grad = norm_back(s.tokens[at], gain_a, sums[part].total())
        s.grad_tokens[at] = s.attended[at] + back
        small = small + jnp.where(row_id == 0, gain_grad, 0.0)
    reduce.arrive(2 * E)
    s.small[...] = add_everywhere(h, wire, small, s.small_land)
    for e in range(E):
        s.grad_inner[e] = reduce.total(2 * e)
        s.grad_outer[e] = jnp.transpose(reduce.total(2 * e + 1))
    attn = reduce.total(2 * E)
    s.grad_q[...] = attn[:, :width]
    s.grad_k[...] = attn[:, width : 2 * width]
    s.grad_v[...] = attn[:, 2 * width : 3 * width]
    s.grad_o[...] = jnp.transpose(attn[:, 3 * width :])
    wire.settle()
    weights.wire.settle()
    reduce.close()


def layer(table, tokens, cot, segments, routes, gain_a, gain_f, router, wq, wk, wv, wo, w_in, w_out):
    rows, model = tokens.shape
    seq = segments.shape[1]
    shard, width = wq.shape
    heads = width // HD
    hidden = w_in.shape[2]
    vmem = pl.BlockSpec(memory_space=pltpu.VMEM)
    smem = pl.BlockSpec(memory_space=pltpu.SMEM)
    hbm = pl.BlockSpec(memory_space=pl.ANY)
    ins = [
        ("table", table, smem), ("tokens", tokens, vmem), ("cot", cot, vmem),
        ("segments", segments, vmem), ("routes", routes, vmem), ("gain_a", gain_a, vmem),
        ("gain_f", gain_f, vmem), ("router", router, vmem), ("wq", wq, vmem), ("wk", wk, vmem),
        ("wv", wv, vmem), ("wo", wo, vmem), ("w_in", w_in, hbm), ("w_out", w_out, vmem),
    ]
    outs = [
        ("output", (rows, model), F32, vmem),
        ("grad_tokens", (rows, model), F32, vmem),
        ("grad_q", (shard, width), F32, vmem),
        ("grad_k", (shard, width), F32, vmem),
        ("grad_v", (shard, width), F32, vmem),
        ("grad_o", (width, shard), F32, vmem),
        ("small", (8, model), F32, vmem),
        ("grad_inner", (E, shard, hidden), F32, vmem),
        ("grad_outer", (E, hidden, shard), F32, vmem),
        ("experts", (2 * E, model, hidden), BF, hbm),
        ("y_land", (2 * E + 1, 4, shard, model), BF, hbm),
        ("z_land", (2 * E + 1, 3, shard, model), BF, hbm),
    ]
    scratch = [
        ("attn_shard", (shard, model), BF),
        ("outer_shard", (E, shard, hidden), BF),
        ("attn_rows", (seq, model), BF),
        ("qkv", (seq, 3 * width), BF),
        ("ctx", (seq, width), BF),
        ("lse", (8, seq), F32),
        ("delta", (8, seq), F32),
        ("w_attn", (model, 4 * width), BF),
        ("first", (8, seq), jnp.int32),
        ("attended", (rows, model), F32),
        ("x_rows", (seq, model), BF),
        ("d_rows", (seq, model), BF),
        ("x_t", (model, seq), BF),
        ("d_t", (model, seq), BF),
        ("active", (seq, hidden), BF),
        ("d_inner", (seq, hidden), BF),
        ("terms", (seq, 2 * model), BF),
        ("w_buf", (2, model, hidden), BF),
        ("acc", (heads * QT, seq), F32),
        ("q_t", (width, seq), BF),
        ("k_t", (width, seq), BF),
        ("v_t", (width, seq), BF),
        ("dc_t", (width, seq), BF),
        ("ctx_t", (width, seq), BF),
        ("kn", (heads, seq, HD), BF),
        ("vn", (heads, seq, HD), BF),
        ("qn", (heads, seq, HD), BF),
        ("dcn", (heads, seq, HD), BF),
        ("bias", (heads, 2, HALF, HALF), F32),
        ("near", (heads, 2, HALF, HALF), F32),
        ("dq_t", (width, seq), F32),
        ("dqkv", (seq, 3 * width), BF),
        ("branch", (seq, model), BF),
        ("landed", (2, 2, rows // 2, 2 * model), BF),
        ("out", (2, rows // 2, 2 * model), BF),
        ("back", (2, rows // 2, 2 * model), BF),
        ("mine", (2 * E + 1, 4, shard, model), BF),
        ("other", (OTHERS, 4, shard, model), BF),
        ("y_stage", (4, shard, model), BF),
        ("z_stage", (3, shard, model), BF),
        ("small_land", (10, 8, model), F32),
    ]
    sems = [
        ("t_send", T_SEMS), ("t_recv", T_SEMS), ("w_send", W_SEMS), ("w_recv", W_SEMS),
        ("g_send", G_SEMS), ("g_recv", G_SEMS), ("own_sem", PIECES), ("local_sem", 4),
    ]
    names = [i[0] for i in ins] + [o[0] for o in outs] + [c[0] for c in scratch]
    names += ["tab"] + [c[0] for c in sems]
    return pl.pallas_call(
        functools.partial(layer_kernel, heads, names),
        out_shape=tuple(jax.ShapeDtypeStruct(o[1], o[2]) for o in outs),
        in_specs=[i[2] for i in ins],
        out_specs=tuple(o[3] for o in outs),
        scratch_shapes=[pltpu.VMEM(c[1], c[2]) for c in scratch]
        + [pltpu.SMEM((heads, NBKT), F32)]
        + [pltpu.SemaphoreType.DMA((c[1],)) for c in sems],
        compiler_params=pltpu.CompilerParams(
            vmem_limit_bytes=VMEM_MAX, collective_id=1, has_side_effects=True
        ),
        cost_estimate=pl.CostEstimate(flops=4 * 10**10, bytes_accessed=10**8, transcendentals=10**7),
        name="layer",
    )(*[i[1] for i in ins])


def rms_apply(values, gain_vec):
    inverse = lax.rsqrt(jnp.mean(values * values, axis=-1, keepdims=True) + EPSILON)
    return values * inverse * gain_vec


def table_grad(diag):
    onehot = jnp.asarray((BUCKETS[:HALF, None] == np.arange(NBKT - 1)[None, :]).astype(np.float32))
    near_sums = jnp.dot(onehot.T, diag.T, precision=lax.Precision.HIGHEST)
    return jnp.concatenate([near_sums, -jnp.sum(near_sums, axis=0, keepdims=True)], axis=0)


def per_device_grid(
    tokens, segments, routes, cotangent, gain_attn, w_query, w_key, w_value, w_output, rel_table,
    gain_ffn, w_router, w_inner, w_outer,
):
    out = layer(
        rel_table.astype(F32), tokens, cotangent, segments[None, :], routes, gain_attn[None, :],
        gain_ffn[None, :], w_router, w_query, w_key, w_value, w_output, w_inner, w_outer,
    )
    output, grad_tokens, grad_q, grad_k, grad_v, grad_o, small, grad_inner, grad_outer = out[:9]
    diag = small[6:8].reshape(rel_table.shape[1], HALF)
    return (
        output, grad_tokens, small[0], grad_q, grad_k, grad_v, grad_o, table_grad(diag), small[1],
        jnp.transpose(small[2 : 2 + E]), grad_inner, grad_outer,
    )


def per_device(
    tokens, segments, routes, cotangent, gain_attn, w_query, w_key, w_value, w_output, rel_table,
    gain_ffn, w_router, w_inner, w_outer,
):
    part_index = lax.axis_index("tensor")
    rows_local, model = tokens.shape
    seq_len = segments.shape[0]
    width = w_query.shape[1]
    heads = width // HD
    all_heads = rel_table.shape[1]
    hidden = w_inner.shape[2]

    attn_shard = jnp.concatenate([w_query, w_key, w_value, jnp.transpose(w_output)], axis=1)
    w_attn = gather_dp(attn_shard)
    both_shard = jnp.concatenate([w_inner, jnp.transpose(w_outer, (0, 2, 1))], axis=2)
    w_experts = [gather_dp(both_shard[e]) for e in range(E)]
    offs = jnp.zeros((1,), jnp.int32)
    slot_row, slot_col, plan = make_plan(jnp.reshape(routes, (1, seq_len)))
    counts = [jnp.sum((segments < s).astype(jnp.int32)) for s in range(1, 5)]
    first_key = jnp.zeros_like(segments)
    for s in range(1, 5):
        first_key = jnp.where(segments >= s, counts[s - 1], first_key)
    first_key = first_key[None, :]
    table = jnp.transpose(
        lax.dynamic_slice_in_dim(rel_table.astype(F32), part_index * heads, heads, 1)
    )

    normed_attn, norm_one_pull = jax.vjp(rms_apply, tokens, gain_attn.astype(F32))
    attn_rows = lax.all_gather(normed_attn.astype(BF), "tensor", axis=0, tiled=True)
    qkv, ctx, lse, branch = attend(attn_rows, w_attn, table, first_key, heads)
    attended = tokens + lax.psum_scatter(
        branch, "tensor", scatter_dimension=0, tiled=True
    ).astype(F32)

    normed_ffn, norm_two_pull = jax.vjp(rms_apply, attended, gain_ffn.astype(F32))
    ffn_in = normed_ffn.astype(BF)
    local_routes = lax.dynamic_slice_in_dim(routes[:, 0], part_index * rows_local, rows_local, 0)
    route_mask = (local_routes[:, None] == jnp.arange(E, dtype=jnp.int32)[None, :]).astype(F32)

    def gate_of(normed_values, router_values):
        logits = jnp.dot(normed_values, router_values, precision=lax.Precision.HIGHEST)
        return jnp.sum(jax.nn.softmax(logits, axis=-1) * route_mask, axis=-1)

    gate_weight, gate_pull = jax.vjp(gate_of, ffn_in.astype(F32), w_router.astype(F32))
    d_expert = (cotangent * gate_weight[:, None]).astype(BF)
    xd = lax.all_gather(jnp.concatenate([ffn_in, d_expert], axis=1), "tensor", axis=0, tiled=True)

    terms = None
    expert_sums = []
    for e in range(E):
        terms, part = expert(e, plan, offs, xd, slot_row, slot_col, terms, w_experts[e])
        expert_sums.append(reduce_dp(part[0]))
    sums = lax.psum_scatter(terms, "tensor", scatter_dimension=0, tiled=True).astype(F32)
    expert_out, d_ffn_local = sums[:, :model], sums[:, model:]
    output = attended + gate_weight[:, None] * expert_out
    d_gate = jnp.sum(cotangent * expert_out, axis=-1)

    d_ffn_router, grad_router_local = gate_pull(d_gate)
    d_attended_norm, grad_gain_two = norm_two_pull(d_ffn_local + d_ffn_router)
    d_attended = cotangent + d_attended_norm
    d_branch_rows = lax.all_gather(d_attended.astype(BF), "tensor", axis=0, tiled=True)

    total_rows, diag, attn_part = attend_back(
        d_branch_rows, w_attn, qkv, ctx, lse, first_key, attn_rows, table, offs, heads
    )
    attn_sum = reduce_dp(attn_part[0])
    d_attn_local = lax.psum_scatter(
        total_rows, "tensor", scatter_dimension=0, tiled=True
    ).astype(F32)
    d_tokens_norm, grad_gain_one = norm_one_pull(d_attn_local)
    grad_tokens = d_attended + d_tokens_norm
    grad_table_full = lax.dynamic_update_slice_in_dim(
        jnp.zeros((NBKT, all_heads), F32), table_grad(diag[:heads]), part_index * heads, 1
    )
    small_sums = lax.psum(
        (grad_gain_one, grad_gain_two, grad_router_local, grad_table_full), ("dp", "tensor")
    )
    return (
        output,
        grad_tokens,
        small_sums[0],
        attn_sum[:, :width],
        attn_sum[:, width : 2 * width],
        attn_sum[:, 2 * width : 3 * width],
        jnp.transpose(attn_sum[:, 3 * width :]),
        small_sums[3],
        small_sums[1],
        small_sums[2],
        jnp.stack([part[:, :hidden] for part in expert_sums]),
        jnp.stack([jnp.transpose(part[:, hidden:]) for part in expert_sums]),
    )


def solution(mesh):
    sizes = dict(mesh.shape)
    in_specs = (
        P(("dp", "tensor"), None),
        P("dp"),
        P("dp", None),
        P(("dp", "tensor"), None),
        P(),
        P("dp", "tensor"),
        P("dp", "tensor"),
        P("dp", "tensor"),
        P("tensor", "dp"),
        P(),
        P(),
        P(),
        P(None, "dp", "tensor"),
        P(None, "tensor", "dp"),
    )
    out_specs = (
        P(("dp", "tensor"), None),
        P(("dp", "tensor"), None),
        P(),
        P("dp", "tensor"),
        P("dp", "tensor"),
        P("dp", "tensor"),
        P("tensor", "dp"),
        P(),
        P(),
        P(),
        P(None, "dp", "tensor"),
        P(None, "tensor", "dp"),
    )
    return jax.shard_map(
        per_device_grid if sizes["dp"] == 8 and sizes["tensor"] == 4 else per_device,
        mesh=mesh,
        in_specs=in_specs,
        out_specs=out_specs,
        check_vma=False,
    )
```

```python
import functools
import math

import jax
import jax.numpy as jnp
import numpy as np
from jax import lax
from jax.experimental import pallas as pl
from jax.experimental.pallas import tpu as pltpu
from jax.sharding import PartitionSpec as P

HD = 64
NBKT = 32
MAXD = 128
E = 4
WIN = 1024
QT = 256
HALF = 128
ROWS = 256

EPSILON = 1e-06
NEG_LARGE = -1e30
BF = jnp.bfloat16
F32 = jnp.float32
VMEM_MAX = 60 * 1024 * 1024


def bucket_numbers(window, buckets, far_distance):
    distance = np.arange(window)
    exact_part = buckets // 2
    safe_distance = np.maximum(distance, 1) * 1.0
    log_part = exact_part + np.floor(
        np.log(safe_distance / exact_part)
        / np.log(far_distance / exact_part)
        * (buckets - exact_part)
    ).astype(np.int32)
    log_part = np.minimum(log_part, buckets - 1)
    return np.where(distance < exact_part, distance, log_part).astype(np.int32)


BUCKETS = bucket_numbers(WIN, NBKT, MAXD)
FIRST = [int(np.argmax(BUCKETS == b)) for b in range(NBKT)]
NEAR = FIRST[NBKT - 1]


def nn(a, b):
    return lax.dot_general(a, b, (((1,), (0,)), ((), ())), preferred_element_type=F32)


def nt(a, b):
    return lax.dot_general(a, b, (((1,), (1,)), ((), ())), preferred_element_type=F32)


def tn(a, b):
    return lax.dot_general(a, b, (((0,), (0,)), ((), ())), preferred_element_type=F32)


class Names:
    pass


def iota(shape, dim):
    return lax.broadcasted_iota(jnp.int32, shape, dim)


def gather_dp(shard):
    return lax.all_gather(shard, "dp", axis=0, tiled=True)


def reduce_dp(part):
    return lax.psum_scatter(part, "dp", scatter_dimension=0, tiled=True).astype(F32)


def plan_kernel(route_ref, slot_row_ref, slot_col_ref, plan_ref):
    length = route_ref.shape[1]
    route = route_ref[...]
    chosen = jnp.where(iota((8, length), 0) == route, 1.0, 0.0).astype(F32)
    upper = jnp.where(iota((length, length), 0) < iota((length, length), 1), 1.0, 0.0)
    before = nn(chosen.astype(BF), upper.astype(BF))
    rank = jnp.sum(chosen * before, axis=0, keepdims=True)
    start = jnp.int32(0)
    base = jnp.zeros((1, length), F32)
    for e in range(E):
        here = route == e
        count = jnp.sum(jnp.where(here, 1, 0))
        tiles = (count + (ROWS - 1)) // ROWS
        plan_ref[e] = tiles
        plan_ref[E + e] = start
        base = base + jnp.where(here, start.astype(F32), 0.0)
        start = start + tiles * ROWS
    slots = jnp.broadcast_to(rank + base, (8, length))
    slot_row_ref[...] = slots.astype(jnp.int32)
    slot_col_ref[...] = jnp.transpose(slots).astype(jnp.int32)


def make_plan(route_row):
    length = route_row.shape[1]
    return pl.pallas_call(
        plan_kernel,
        out_shape=(
            jax.ShapeDtypeStruct((8, length), jnp.int32),
            jax.ShapeDtypeStruct((length, 8), jnp.int32),
            jax.ShapeDtypeStruct((2 * E,), jnp.int32),
        ),
        in_specs=[pl.BlockSpec(memory_space=pltpu.VMEM)],
        out_specs=(
            pl.BlockSpec(memory_space=pltpu.VMEM),
            pl.BlockSpec(memory_space=pltpu.VMEM),
            pl.BlockSpec(memory_space=pltpu.SMEM),
        ),
        compiler_params=pltpu.CompilerParams(vmem_limit_bytes=VMEM_MAX),
        name="route_plan",
    )(route_row)


def fill_bias(bias_ref, far_ref, table_rows):
    step = iota((HALF, HALF), 1) - iota((HALF, HALF), 0)
    for h, row in enumerate(table_rows):
        far_ref[h : h + 1] = jnp.broadcast_to(row[:, NBKT - 1 :], (1, far_ref.shape[1]))
    for side in range(2):
        distance = step + side * HALF
        tiles = [jnp.broadcast_to(row[:, NBKT - 1 :], (HALF, HALF)) for row in table_rows]
        for b in reversed(range(NBKT - 1)):
            below = distance < FIRST[b + 1]
            for h, row in enumerate(table_rows):
                tiles[h] = jnp.where(below, row[:, b : b + 1], tiles[h])
        for h, tile in enumerate(tiles):
            bias_ref[h, side] = tile


def biased_scores(raw, gap, h, bias_ref, far_ref, first_key, key_start):
    far = far_ref[h : h + 1]
    keys = key_start + iota((QT, QT), 0)
    if gap >= 2:
        return jnp.where(keys >= first_key, raw + far, NEG_LARGE)
    diag, near = bias_ref[h, 0], bias_ref[h, 1]
    const = jnp.broadcast_to(far[:, :HALF], (HALF, HALF))
    if gap == 1:
        tile = jnp.concatenate(
            [
                jnp.concatenate([const, const], axis=1),
                jnp.concatenate([near, const], axis=1),
            ],
            axis=0,
        )
        return jnp.where(keys >= first_key, raw + tile, NEG_LARGE)
    tile = jnp.concatenate(
        [jnp.concatenate([diag, near], axis=1), jnp.concatenate([const, diag], axis=1)], axis=0
    )
    causal = iota((QT, QT), 0) <= iota((QT, QT), 1)
    return jnp.where((keys >= first_key) & causal, raw + tile, NEG_LARGE)


def attend_blocks(heads, first_ref, q_t, v_t, kn, bias_ref, far_ref, s_ref, ctx_t, lse_ref, blocks):
    for i in blocks:
        cols = slice(i * QT, (i + 1) * QT)
        first_key = first_ref[0:1, cols]
        for h in range(heads):
            band = slice(h * HD, (h + 1) * HD)
            q_blk = q_t[band, cols]
            peak = None
            for j in range(i + 1):
                raw = nn(kn[h, j * QT : (j + 1) * QT], q_blk)
                s = biased_scores(raw, i - j, h, bias_ref, far_ref, first_key, j * QT)
                s_ref[h * QT : (h + 1) * QT, j * QT : (j + 1) * QT] = s
                top = jnp.max(s, axis=0, keepdims=True)
                peak = top if peak is None else jnp.maximum(peak, top)
            total = jnp.zeros((1, QT), F32)
            acc = jnp.zeros((HD, QT), F32)
            for j in range(i + 1):
                p = jnp.exp(s_ref[h * QT : (h + 1) * QT, j * QT : (j + 1) * QT] - peak)
                total = total + jnp.sum(p, axis=0, keepdims=True)
                acc = acc + nn(v_t[band, j * QT : (j + 1) * QT], p.astype(BF))
            ctx_t[band, cols] = (acc / total).astype(BF)
            lse_ref[h : h + 1, cols] = peak + jnp.log(total)


def project(heads, x, w_ref, qkv_ref, q_t, v_t, kn):
    width = heads * HD
    qkv = nn(x, w_ref[:, : 3 * width]).astype(BF)
    qkv_ref[...] = qkv
    q_t[...] = jnp.transpose(qkv[:, :width]) * jnp.asarray(1.0 / math.sqrt(HD), BF)
    v_t[...] = jnp.transpose(qkv[:, 2 * width :])
    for h in range(heads):
        kn[h] = qkv[:, width + h * HD : width + (h + 1) * HD]


def attend_kernel(heads, table_ref, x_ref, first_ref, w_ref, *refs):
    qkv_ref, ctx_ref, lse_ref, branch_ref, q_t, v_t, kn, bias_ref, far_ref, s_ref, ctx_t = refs
    width = heads * HD
    seq = x_ref.shape[0]
    fill_bias(bias_ref, far_ref, [table_ref[hd : hd + 1, :] for hd in range(heads)])
    project(heads, x_ref[...], w_ref, qkv_ref, q_t, v_t, kn)
    blocks = range(seq // QT)
    attend_blocks(
        heads, first_ref, q_t, v_t, kn, bias_ref, far_ref, s_ref, ctx_t, lse_ref, blocks
    )
    ctx = jnp.transpose(ctx_t[...])
    ctx_ref[...] = ctx
    branch_ref[...] = nt(ctx, w_ref[:, 3 * width :]).astype(BF)


def attend(x, w, table, first_key, heads):
    seq, model = x.shape
    width = heads * HD
    vmem = pl.BlockSpec(memory_space=pltpu.VMEM)
    return pl.pallas_call(
        functools.partial(attend_kernel, heads),
        out_shape=(
            jax.ShapeDtypeStruct((seq, 3 * width), BF),
            jax.ShapeDtypeStruct((seq, width), BF),
            jax.ShapeDtypeStruct((8, seq), F32),
            jax.ShapeDtypeStruct((seq, model), BF),
        ),
        in_specs=[vmem] * 4,
        out_specs=(vmem,) * 4,
        scratch_shapes=[
            pltpu.VMEM((width, seq), BF),
            pltpu.VMEM((width, seq), BF),
            pltpu.VMEM((heads, seq, HD), BF),
            pltpu.VMEM((heads, 2, HALF, HALF), F32),
            pltpu.VMEM((8, QT), F32),
            pltpu.VMEM((heads * QT, seq), F32),
            pltpu.VMEM((width, seq), BF),
        ],
        compiler_params=pltpu.CompilerParams(vmem_limit_bytes=VMEM_MAX),
        cost_estimate=pl.CostEstimate(flops=4 * 10**9, bytes_accessed=10**7, transcendentals=2 * 10**6),
        name="attend",
    )(table, x, first_key, w)


def attend_back_block(heads, s, j, seq):
    width = heads * HD
    keys = slice(j * QT, (j + 1) * QT)
    for h in range(heads):
        band = slice(h * HD, (h + 1) * HD)
        dk = jnp.zeros((QT, HD), F32)
        dv = jnp.zeros((QT, HD), F32)
        for i in range(j, seq // QT):
            cols = slice(i * QT, (i + 1) * QT)
            raw = nn(s.kn[h, keys], s.q_t[band, cols])
            scores = biased_scores(raw, i - j, h, s.bias, s.far, s.first[0:1, cols], j * QT)
            p = jnp.exp(scores - s.lse[h : h + 1, cols])
            dp = nn(s.vn[h, keys], s.dc_t[band, cols])
            ds = p * (dp - s.delta[h : h + 1, cols])
            if i == j:
                s.near[h, 0] += ds[:HALF, :HALF] + ds[HALF:, HALF:]
                s.near[h, 1] += ds[:HALF, HALF:]
            elif i == j + 1:
                s.near[h, 1] += ds[HALF:, :HALF]
            ds = ds.astype(BF)
            dv = dv + nn(p.astype(BF), s.dcn[h, cols])
            dk = dk + nn(ds, s.qn[h, cols])
            s.dq_t[band, cols] += nn(s.k_t[band, keys], ds)
        s.dqkv[keys, width + h * HD : width + (h + 1) * HD] = dk.astype(BF)
        s.dqkv[keys, 2 * width + h * HD : 2 * width + (h + 1) * HD] = dv.astype(BF)


def diagonal_lines(heads, near):
    key, query = iota((HALF, HALF), 0), iota((HALF, HALF), 1)
    lines = []
    for h in range(heads):
        both = near[h, 0] + jnp.where(query < key, near[h, 1], 0.0)
        for bit in range(7):
            turned = pltpu.roll(both, HALF - (1 << bit), 1)
            both = jnp.where((key >> bit) & 1 == 1, turned, both)
        lines.append(jnp.sum(both, axis=0, keepdims=True))
    return lines


def attend_back_kernel(heads, blocks, names, *refs):
    s = Names()
    for name, ref in zip(names, refs):
        setattr(s, name, ref)
    grads = refs[len(names) :]
    width = heads * HD
    seq = s.d.shape[0]
    scale = jnp.asarray(1.0 / math.sqrt(HD), BF)
    fill_bias(s.bias, s.far, [s.tab[hd : hd + 1, :] for hd in range(heads)])
    d_rows = s.d[...]
    ctx = s.ctx[...]
    dc = nn(d_rows, s.w[:, 3 * width :]).astype(BF)
    s.acc[:, 3 * width :] = tn(d_rows, ctx)
    dct = jnp.transpose(dc)
    s.dc_t[...] = dct
    qkv = s.qkv[...]
    s.q_t[...] = jnp.transpose(qkv[:, :width]) * scale
    s.k_t[...] = jnp.transpose(qkv[:, width : 2 * width])
    product = dct.astype(F32) * jnp.transpose(ctx).astype(F32)
    for h in range(heads):
        band = slice(h * HD, (h + 1) * HD)
        s.qn[h] = qkv[:, band] * scale
        s.kn[h] = qkv[:, width + h * HD : width + (h + 1) * HD]
        s.vn[h] = qkv[:, 2 * width + h * HD : 2 * width + (h + 1) * HD]
        s.dcn[h] = dc[:, band]
        s.delta[h : h + 1] = jnp.sum(product[band], axis=0, keepdims=True)
    s.dq_t[...] = jnp.zeros_like(s.dq_t)
    s.near[...] = jnp.zeros_like(s.near)
    for j in range(seq // QT):
        attend_back_block(heads, s, j, seq)
    s.dqkv[:, :width] = jnp.transpose((s.dq_t[...] * (1.0 / math.sqrt(HD))).astype(BF))
    d_qkv = s.dqkv[...]
    s.rows[...] = nt(d_qkv, s.w[:, : 3 * width]).astype(BF)
    s.acc[:, : 3 * width] = tn(s.x[...], d_qkv)
    scatter_rows(s.acc, s.offs, grads, blocks)
    lines = diagonal_lines(heads, s.near) + [jnp.zeros((8 - heads, HALF), F32)]
    s.diag[...] = jnp.concatenate(lines, axis=0)


def scatter_rows(acc_ref, offs_ref, outs, blocks):
    k = 0
    for out, count in zip(outs, blocks):
        rows = out.shape[1]
        for b in range(count):
            at = pl.ds(pl.multiple_of(offs_ref[k], rows), rows)
            out[b] = acc_ref[at, :].astype(BF)
            k += 1


def attend_back(d_rows, w, qkv, ctx, lse, first_key, x, table, offs, heads):
    seq, model = x.shape
    width = heads * HD
    vmem = pl.BlockSpec(memory_space=pltpu.VMEM)
    smem = pl.BlockSpec(memory_space=pltpu.SMEM)
    scratch = [
        ("q_t", (width, seq), BF),
        ("k_t", (width, seq), BF),
        ("dc_t", (width, seq), BF),
        ("kn", (heads, seq, HD), BF),
        ("vn", (heads, seq, HD), BF),
        ("qn", (heads, seq, HD), BF),
        ("dcn", (heads, seq, HD), BF),
        ("bias", (heads, 2, HALF, HALF), F32),
        ("far", (8, QT), F32),
        ("dq_t", (width, seq), F32),
        ("dqkv", (seq, 3 * width), BF),
        ("near", (heads, 2, HALF, HALF), F32),
        ("delta", (8, seq), F32),
        ("acc", (model, 4 * width), F32),
    ]
    ins = ["offs", "tab", "d", "w", "qkv", "ctx", "lse", "first", "x"]
    names = ins + ["rows", "diag", "grads"] + [c[0] for c in scratch]

    def kernel(*refs):
        at = len(ins) + 2
        plain = refs[:at] + refs[at + 1 :]
        attend_back_kernel(
            heads, (1,), names[:at] + names[at + 1 :], *plain, refs[at]
        )

    out = pl.pallas_call(
        kernel,
        out_shape=(
            jax.ShapeDtypeStruct((seq, model), BF),
            jax.ShapeDtypeStruct((8, HALF), F32),
            jax.ShapeDtypeStruct((1, model, 4 * width), BF),
        ),
        in_specs=[smem] + [vmem] * 8,
        out_specs=(vmem,) * 3,
        scratch_shapes=[pltpu.VMEM(c[1], c[2]) for c in scratch],
        compiler_params=pltpu.CompilerParams(vmem_limit_bytes=VMEM_MAX),
        cost_estimate=pl.CostEstimate(flops=10**10, bytes_accessed=10**7, transcendentals=2 * 10**6),
        name="attend_back",
    )(offs, table, d_rows, w, qkv, ctx, lse, first_key, x)
    return out[0], out[1], out[2]


def expert_kernel(e, plan_ref, offs_ref, xd_ref, row_ref, col_ref, w_ref, *refs):
    terms_in = refs[0] if e > 0 else None
    terms_ref, grad, acc_ref = refs[-3:]
    model = xd_ref.shape[1] // 2
    hidden = w_ref.shape[1] // 2
    length = xd_ref.shape[0]
    terms_ref[...] = jnp.zeros_like(terms_ref) if terms_in is None else terms_in[...]
    acc_ref[...] = jnp.zeros_like(acc_ref)
    base = plan_ref[E + e]

    @pl.loop(0, plan_ref[e])
    def _(t):
        start = base + t * ROWS
        pick = jnp.where(row_ref[0:1, :] == start + iota((ROWS, length), 0), 1.0, 0.0).astype(BF)
        xd = nn(pick, xd_ref[...]).astype(BF)
        x, d = xd[:, :model], xd[:, model:]
        inner = nn(x, w_ref[:, :hidden])
        cubic = 0.044715 * inner * inner
        tanh = jnp.tanh(math.sqrt(2.0 / math.pi) * inner * (1.0 + cubic))
        half = 0.5 * (1.0 + tanh)
        active = (inner * half).astype(BF)
        slope = half + (0.5 * math.sqrt(2.0 / math.pi)) * inner * (1.0 - tanh * tanh) * (1.0 + 3.0 * cubic)
        out = nt(active, w_ref[:, hidden:]).astype(BF)
        d_inner = (nn(d, w_ref[:, hidden:]) * slope).astype(BF)
        acc_ref[:, :hidden] += tn(x, d_inner)
        acc_ref[:, hidden:] += tn(d, active)
        d_x = nt(d_inner, w_ref[:, :hidden]).astype(BF)
        place = jnp.where(col_ref[:, 0:1] == start + iota((length, ROWS), 1), 1.0, 0.0).astype(BF)
        terms_ref[:, :model] = (terms_ref[:, :model].astype(F32) + nn(place, out)).astype(BF)
        terms_ref[:, model:] = (terms_ref[:, model:].astype(F32) + nn(place, d_x)).astype(BF)

    scatter_rows(acc_ref, offs_ref, [grad], (1,))


def expert(e, plan, offs, xd, slot_row, slot_col, terms, w):
    length, both = xd.shape
    model, hidden2 = w.shape
    vmem = pl.BlockSpec(memory_space=pltpu.VMEM)
    smem = pl.BlockSpec(memory_space=pltpu.SMEM)
    extra = [] if terms is None else [terms]
    return pl.pallas_call(
        functools.partial(expert_kernel, e),
        out_shape=(
            jax.ShapeDtypeStruct((length, both), BF),
            jax.ShapeDtypeStruct((1, model, hidden2), BF),
        ),
        in_specs=[smem] * 2 + [vmem] * (4 + len(extra)),
        out_specs=(vmem,) * 2,
        scratch_shapes=[pltpu.VMEM((model, hidden2), F32)],
        compiler_params=pltpu.CompilerParams(vmem_limit_bytes=VMEM_MAX),
        cost_estimate=pl.CostEstimate(flops=3 * 10**9, bytes_accessed=10**7, transcendentals=10**6),
        name=f"expert_{e}",
    )(plan, offs, xd, slot_row, slot_col, w, *extra)


MESH = pl.DeviceIdType.MESH
PIECES = 1 + 2 * E
T_SEMS = 48
W_SEMS = 9 * PIECES
Y_FIRST = (PIECES - 2, PIECES - 1)
Z_FIRST = {0: 2 * E + 1, 1: 2 * E + 2}
LEGS = 2 * E + 1 + len(Z_FIRST)
G_SEMS = 6 * LEGS


class Here:
    def __init__(self):
        self.d = lax.axis_index("dp")
        self.t = lax.axis_index("tensor")
        self.z, self.y = self.d // 2, self.d % 2
        self.x, self.c = self.t // 2, self.t % 2
        self.core = {"dp": self.d, "tensor": 2 * self.x + 1 - self.c}
        self.side = {"dp": self.d, "tensor": 2 * (1 - self.x) + self.c}
        self.over = {"dp": 2 * self.z + 1 - self.y, "tensor": self.t}

        self.low = self.z // 2
        self.middle = (self.z == 1) | (self.z == 2)
        self.pair_z = self.z + 1 - 2 * (self.z % 2)
        self.mid_z = 2 - self.low
        self.end_z = 3 - 3 * self.low
        self.order = [self.z, self.pair_z, self.mid_z, self.end_z]
        self.pair, self.far_mid, self.far_end = (self.at_z(z) for z in self.order[1:])

    def at_z(self, z):
        return {"dp": 2 * z + self.y, "tensor": self.t}

    def greet(self):
        barrier = pltpu.get_barrier_semaphore()
        peers = [self.core, self.side, self.over, self.pair, self.far_mid, self.far_end]
        for peer in peers:
            pl.semaphore_signal(barrier, inc=1, device_id=peer, device_id_type=MESH)
        pl.semaphore_wait(barrier, len(peers))


class Wire:
    def __init__(self, send, recv):
        self.send, self.recv, self.sent, self.count = send, recv, [], 0

    def take(self, number):
        self.count += number
        return self.count - number

    def plan(self, src, dst, peer, send, recv):
        return pltpu.make_async_remote_copy(
            src_ref=src, dst_ref=dst, send_sem=self.send.at[send], recv_sem=self.recv.at[recv],
            device_id=peer, device_id_type=MESH,
        )

    def __call__(self, src, dst, peer):
        k = self.take(1)
        copy = self.plan(src, dst, peer, k, k)
        copy.start()
        self.sent.append(copy)
        return copy

    def settle(self):
        for copy in self.sent:
            copy.wait_send()
        self.sent = []


class Rows:
    def __init__(self, here, wire, buf, rows, part, parts):
        self.here, self.wire, self.buf = here, wire, buf
        self.rows, self.size = rows, rows // parts
        self.shift = part * self.size

    def at(self, t):
        return self.buf.at[pl.ds(pl.multiple_of(t * self.rows + self.shift, 16), self.size)]

    def start(self):
        mine = self.at(self.here.t)
        self.far = self.wire(mine, mine, self.here.side)
        self.near = self.wire(mine, mine, self.here.core)

    def forward(self):
        self.far.wait_recv()
        theirs = self.at(2 * (1 - self.here.x) + self.here.c)
        self.last = self.wire(theirs, theirs, self.here.core)

    def finish(self):
        self.near.wait_recv()
        self.last.wait_recv()


class Sums:
    def __init__(self, here, wire, src, landed, out, back, rows, part, parts):
        self.here, self.wire, self.src = here, wire, src
        self.landed, self.out, self.back = landed, out, back
        self.rows, self.size = rows, rows // parts
        self.shift = part * self.size
        self.part = part

    def at(self, t):
        return pl.ds(pl.multiple_of(t * self.rows + self.shift, 16), self.size)

    def start(self):
        h = self.here
        self.copies = []
        for slot, x in ((0, 1 - h.x), (1, h.x)):
            src = self.src.at[self.at(2 * x + 1 - h.c)]
            self.copies.append(self.wire(src, self.landed.at[slot, self.part], h.core))

    def cross(self):
        h = self.here
        self.copies[0].wait_recv()
        mine = self.src[self.at(2 * (1 - h.x) + h.c)].astype(F32)
        self.out[self.part] = (mine + self.landed[0, self.part].astype(F32)).astype(BF)
        self.last = self.wire(self.out.at[self.part], self.back.at[self.part], h.side)

    def total(self):
        h = self.here
        self.copies[1].wait_recv()
        near = self.src[self.at(2 * h.x + h.c)].astype(F32) + self.landed[1, self.part].astype(F32)
        self.last.wait_recv()
        return near + self.back[self.part].astype(F32)


class Weights:
    def __init__(self, here, wire, own_sem, sources, target):
        self.here, self.wire, self.own_sem = here, wire, own_sem
        self.sources, self.target = sources, target
        self.over, self.own, self.z, self.relays = {}, {}, {}, []

    def at(self, p, z):
        rows = self.sources[p].shape[0]
        if p in Y_FIRST:
            return self.target(p, pl.ds(pl.multiple_of(2 * z * rows, 16), 2 * rows))
        return self.target(p, pl.ds(pl.multiple_of((2 * z + self.here.y) * rows, 16), rows))

    def start(self, p):
        h, src = self.here, self.sources[p]
        rows = src.shape[0]
        dst = self.target(p, pl.ds(pl.multiple_of(h.d * rows, 16), rows))
        self.own[p] = pltpu.make_async_copy(src, dst, self.own_sem.at[p])
        self.own[p].start()
        if p not in Y_FIRST:
            self.spread(p, src)
        self.over[p] = [self.wire(src, dst, h.over)]

    def pairs(self, p):
        self.over[p][0].wait_recv()
        self.own[p].wait()
        self.spread(p, self.at(p, self.here.z))

    def spread(self, p, src):
        h, wire = self.here, self.wire
        dst = self.at(p, h.z)
        k = wire.take(5)
        end = jnp.where(h.middle, 0, 1)
        near = wire.plan(src, dst, h.pair, k, k)
        far = wire.plan(src, dst, h.far_mid, k + 1, k + 1 + end)
        near.start()
        far.start()
        wire.sent += [near, far]
        relays = []
        for j, z in ((1, h.mid_z), (2, h.end_z)):
            block = self.at(p, z)
            relays.append(wire.plan(block, block, h.pair, k + 2 + j, k + j))
        self.z[p] = [near] + relays
        self.relays += relays

    def forward(self, p):
        h = self.here
        near, *relays = self.z[p]
        for copy, z in zip(self.z[p], h.order[1:]):
            copy.wait_recv()
            if copy is not near:
                pl.when(h.middle)(copy.start)
            if p not in Y_FIRST:
                block = self.at(p, z)
                self.over[p].append(self.wire(block, block, h.over))

    def finish(self, p):
        if p in Y_FIRST:
            return
        for copy in self.over[p]:
            copy.wait_recv()
        self.own[p].wait()

    def close(self):
        self.wire.settle()
        for copy in self.relays:
            pl.when(self.here.middle)(copy.wait_send)


def normed(values, gain):
    inverse = lax.rsqrt(jnp.mean(values * values, axis=-1, keepdims=True) + EPSILON)
    return values * inverse * gain


class Reduce:
    def __init__(self, here, wire, local, mine, other, y_land, e_land, z_land, y_stage, e_stage, z_stage):
        self.here, self.wire, self.local = here, wire, local
        self.mine, self.other = mine, other
        self.y_land, self.e_land, self.z_land = y_land, e_land, z_land
        self.y_stage, self.e_stage, self.z_stage = y_stage, e_stage, z_stage
        self.y, self.legs = {}, {}

    def fetch(self, src, dst, sem):
        copy = pltpu.make_async_copy(src, dst, self.local.at[sem])
        copy.start()
        copy.wait()

    def store(self, q, acc, shard):
        h = self.here
        for k, z in enumerate(h.order):
            for side, target in ((h.y, self.mine.at[q]), (1 - h.y, self.other.at[q])):
                at = pl.ds(pl.multiple_of((2 * z + side) * shard, 16), shard)
                target[k] = acc[at, : target.shape[2]].astype(BF)

    def start(self, q):
        if q in Z_FIRST:
            self.leg(q, self.mine.at[q])
            self.leg(Z_FIRST[q], self.other.at[q])
        else:
            self.y[q] = self.wire(self.other.at[q], self.y_land.at[q], self.here.over)

    def arrive(self, q):
        self.y[q].wait_recv()
        self.fetch(self.y_land.at[q], self.y_stage, 0)
        for k in range(4):
            pair = self.mine[q, k].astype(F32) + self.y_stage[k].astype(F32)
            self.mine[q, k] = pair.astype(BF)
        self.leg(q, self.mine.at[q])

    def leg(self, j, blocks):
        h, wire = self.here, self.wire
        k = wire.take(5)
        near = wire.plan(blocks.at[1], self.z_land.at[j, 0], h.pair, k, k)
        hand = [
            wire.plan(blocks.at[2 + i], self.e_land.at[j, i], h.pair, k + 1 + i, k + 2 + i)
            for i in range(2)
        ]
        on = [
            wire.plan(blocks.at[2 + i], self.z_land.at[j, 1], peer, k + 3 + i, k + 1)
            for i, peer in enumerate((h.far_mid, h.far_end))
        ]

        @pl.when(jnp.logical_not(h.middle))
        def _():
            for copy in hand:
                copy.start()

        near.start()
        self.legs[j] = (blocks, near, hand, on)

    def relay(self, j):
        blocks, _, hand, on = self.legs[j]

        @pl.when(self.here.middle)
        def _():
            for copy in hand:
                copy.wait_recv()
            self.fetch(self.e_land.at[j], self.e_stage, 1)
            for i in range(2):
                both = blocks[2 + i].astype(F32) + self.e_stage[i].astype(F32)
                blocks[2 + i] = both.astype(BF)
                on[i].start()

    def along_z(self, j):
        blocks, near, _, on = self.legs[j]
        near.wait_recv()
        on[0].wait_recv()
        self.fetch(self.z_land.at[j], self.z_stage, 2)
        return (
            blocks[0].astype(F32) + self.z_stage[0].astype(F32) + self.z_stage[1].astype(F32)
        )

    def cross(self, q):
        self.other[q, 0] = self.along_z(Z_FIRST[q]).astype(BF)
        self.y[q] = self.wire(self.other.at[q, 0], self.y_land.at[q, 0], self.here.over)

    def total(self, q):
        result = self.along_z(q)
        if q in Z_FIRST:
            self.y[q].wait_recv()
            self.fetch(self.y_land.at[q, 0], self.y_stage.at[0], 0)
            result = result + self.y_stage[0].astype(F32)
        return result

    def close(self):
        self.wire.settle()
        for _, near, hand, on in self.legs.values():
            near.wait_send()
            for copy in on:
                pl.when(self.here.middle)(copy.wait_send)
            for copy in hand:
                pl.when(jnp.logical_not(self.here.middle))(copy.wait_send)


def add_everywhere(here, wire, value, land):
    for k, peer in enumerate((here.core, here.side, here.over)):
        land[2 * k] = value
        copy = wire(land.at[2 * k], land.at[2 * k + 1], peer)
        copy.wait_recv()
        value = value + land[2 * k + 1]
    land[6 + here.z] = value
    k = wire.take(3)
    own = land.at[6 + here.z]
    copies = []
    for i, (peer, z) in enumerate(zip((here.pair, here.far_mid, here.far_end), here.order[1:])):
        back = k if i == 0 else k + 1 + jnp.where(here.middle, 0, 1)
        copies.append(wire.plan(own, own, peer, k + i, back))
        copies[-1].start()
    wire.sent += copies
    for i, z in enumerate(here.order[1:]):
        wire.plan(own, land.at[6 + z], here.pair, k + i, k + i).wait_recv()
    return (land[6] + land[7]) + (land[8] + land[9])


def norm_back(values, gain, d_normed):
    inverse = lax.rsqrt(jnp.mean(values * values, axis=-1, keepdims=True) + EPSILON)
    scaled = d_normed * gain
    inner = jnp.mean(scaled * values, axis=-1, keepdims=True)
    grad = inverse * scaled - values * (inverse * inverse * inverse * inner)
    return grad, jnp.sum(d_normed * values * inverse, axis=0, keepdims=True)


def gate_parts(normed_rows, router, route):
    logits = nt(normed_rows, router)
    raised = jnp.exp(logits - jnp.max(logits, axis=1, keepdims=True))
    probs = raised / jnp.sum(raised, axis=1, keepdims=True)
    chosen = jnp.where(route == iota(logits.shape, 1), 1.0, 0.0)
    return probs, chosen, jnp.sum(probs * chosen, axis=1, keepdims=True)


def expert_dense(e, w, s, route_ref):
    model = s.x_rows.shape[1]

    @pl.loop(0, s.x_rows.shape[0] // ROWS)
    def _(t):
        at = pl.ds(pl.multiple_of(t * ROWS, ROWS), ROWS)
        here = route_ref[at, 0:1] == e
        inner = nn(s.x_rows[at], w[0])
        cubic = 0.044715 * inner * inner
        tanh = jnp.tanh(math.sqrt(2.0 / math.pi) * inner * (1.0 + cubic))
        half = 0.5 * (1.0 + tanh)
        active = jnp.where(here, inner * half, 0.0).astype(BF)
        slope = half + (0.5 * math.sqrt(2.0 / math.pi)) * inner * (1.0 - tanh * tanh) * (
            1.0 + 3.0 * cubic
        )
        d_inner = jnp.where(here, nn(s.d_rows[at], w[1]) * slope, 0.0).astype(BF)
        s.active[at] = active
        s.d_inner[at] = d_inner
        out = nt(active, w[1]).astype(BF)
        d_x = nt(d_inner, w[0]).astype(BF)
        if e == 0:
            s.terms[at, :model] = out
            s.terms[at, model:] = d_x
        else:
            s.terms[at, :model] = jnp.where(here, out, s.terms[at, :model])
            s.terms[at, model:] = jnp.where(here, d_x, s.terms[at, model:])


def layer_kernel(heads, names, *refs):
    s = Names()
    for name, ref in zip(names, refs):
        setattr(s, name, ref)
    h = Here()
    width = heads * HD
    seq, model = s.attn_rows.shape
    rows = s.tokens.shape[0]
    half = rows // 2
    shard = s.wq.shape[0]
    wire = Wire(s.t_send, s.t_recv)
    sources = [s.attn_shard]
    for e in range(E):
        sources += [s.w_in.at[e], s.w_out.at[e]]

    def target(p, at):
        return s.w_attn.at[at] if p == 0 else s.experts.at[p - 1, at]

    weights = Weights(h, Wire(s.w_send, s.w_recv), s.own_sem, sources, target)
    reduce = Reduce(
        h, Wire(s.g_send, s.g_recv), s.local_sem, s.mine, s.other, s.y_land, s.e_land, s.z_land,
        s.y_stage, s.e_stage, s.z_stage,
    )
    s.attn_shard[:, :width] = s.wq[...]
    s.attn_shard[:, width : 2 * width] = s.wk[...]
    s.attn_shard[:, 2 * width : 3 * width] = s.wv[...]
    s.attn_shard[:, 3 * width :] = jnp.transpose(s.wo[...])
    h.greet()
    weights.start(0)
    for p in Y_FIRST:
        weights.start(p)

    def block(part):
        return pl.ds(pl.multiple_of(h.t * rows + part * half, 16), half)

    gathers = [Rows(h, wire, s.attn_rows, rows, part, 2) for part in range(2)]
    gain_a = s.gain_a[...].astype(F32).reshape(1, model)
    for part in range(2):
        s.attn_rows[block(part)] = normed(
            s.tokens[part * half : (part + 1) * half], gain_a
        ).astype(BF)
        gathers[part].start()
    weights.start(1)
    s.d_rows[pl.ds(pl.multiple_of(h.t * rows, 16), rows)] = s.cot[...].astype(BF)
    s.tab[...] = s.table[...].astype(F32)
    fill_bias(s.bias, s.far, [s.tab[pl.ds(h.t * heads + hd, 1), :] for hd in range(heads)])
    s.route_col[...] = jnp.transpose(
        jnp.broadcast_to(s.routes[...].astype(F32), (8, seq))
    ).astype(jnp.int32)
    segments = s.segments[...]
    first = jnp.zeros(segments.shape, jnp.int32)
    for seg in range(1, 5):
        first = jnp.where(segments >= seg, jnp.sum(jnp.where(segments < seg, 1, 0)), first)
    s.first[...] = jnp.broadcast_to(first, s.first.shape)
    gathers[0].forward()
    gathers[1].forward()
    weights.forward(0)
    weights.start(2)
    weights.start(3)
    gathers[0].finish()
    gathers[1].finish()
    cots = Rows(h, wire, s.d_rows, rows, 0, 1)
    cots.start()
    weights.finish(0)

    project(heads, s.attn_rows[...], s.w_attn, s.qkv, s.q_t, s.v_t, s.kn)
    state = (s.first, s.q_t, s.v_t, s.kn, s.bias, s.far, s.acc, s.ctx_t, s.lse)
    attend_blocks(heads, *state, range(0, 3))
    cots.forward()
    weights.forward(1)
    weights.start(4)
    attend_blocks(heads, *state, range(3, seq // QT))
    s.ctx[...] = jnp.transpose(s.ctx_t[...])
    s.branch[...] = nt(s.ctx[...], s.w_attn[:, 3 * width :]).astype(BF)
    narrow = [ref.at[:, :, :, :model] for ref in (s.landed,)] + [
        ref.at[:, :, :model] for ref in (s.out, s.back)
    ]
    sums = [Sums(h, wire, s.branch, *narrow, rows, part, 2) for part in range(2)]
    for part in range(2):
        sums[part].start()
    for part in range(2):
        sums[part].cross()
    weights.forward(2)
    weights.start(5)

    gathers = [Rows(h, wire, s.x_rows, rows, part, 2) for part in range(2)]
    gain_f = s.gain_f[...].astype(F32).reshape(1, model)
    for part in range(2):
        at = slice(part * half, (part + 1) * half)
        attended = s.tokens[at] + sums[part].total()
        s.attended[at] = attended
        s.x_rows[block(part)] = normed(attended, gain_f).astype(BF)
        gathers[part].start()
    weights.forward(3)
    weights.start(6)
    for part in range(2):
        gathers[part].forward()
    cots.finish()
    for part in range(2):
        gathers[part].finish()
    wire.settle()
    gate = gate_parts(s.x_rows[...], s.router[...], s.route_col[:, 0:1])[2]
    s.d_rows[...] = (s.d_rows[...].astype(F32) * gate).astype(BF)
    s.x_t[...] = jnp.transpose(s.x_rows[...])
    s.d_t[...] = jnp.transpose(s.d_rows[...])

    def load_weights(e):
        copies = []
        for side in range(2):
            weights.finish(2 * e + 1 + side)
            copies.append(
                pltpu.make_async_copy(
                    s.experts.at[2 * e + side], s.w_buf.at[side], s.local_sem.at[3 + side]
                )
            )
            copies[-1].start()
        for copy in copies:
            copy.wait()

    def run_expert(e):
        load_weights(e)
        expert_dense(e, s.w_buf, s, s.route_col)
        s.acc[:, :model] = nn(s.x_t[...], s.d_inner[...])
        reduce.store(2 * e, s.acc, shard)
        s.acc[:, :model] = nn(s.d_t[...], s.active[...])
        reduce.store(2 * e + 1, s.acc, shard)

    run_expert(0)
    weights.forward(4)
    weights.pairs(7)
    weights.forward(5)
    weights.pairs(8)
    run_expert(1)
    weights.forward(6)
    weights.forward(7)
    reduce.start(2)
    reduce.start(3)
    run_expert(2)
    weights.forward(8)
    reduce.start(0)
    reduce.start(1)
    reduce.start(4)
    reduce.start(5)
    run_expert(3)
    reduce.start(6)
    reduce.start(7)

    sums = [
        Sums(h, wire, s.terms, s.landed, s.out, s.back, rows, part, 2) for part in range(2)
    ]
    for part in range(2):
        sums[part].start()
    for part in range(2):
        sums[part].cross()
    reduce.arrive(2)
    reduce.arrive(3)
    gathers = [Rows(h, wire, s.x_rows, rows, part, 2) for part in range(2)]
    router_rows = s.router[...].astype(F32)
    small = jnp.zeros((8, model), F32)
    row_id = iota((8, model), 0)
    for part in range(2):
        at = slice(part * half, (part + 1) * half)
        attended, cot = s.attended[at], s.cot[at]
        total = sums[part].total()
        expert_out, d_normed = total[:, :model], total[:, model:]
        ffn = normed(attended, gain_f).astype(BF)
        route = s.route_col[block(part), 0:1]
        probs, chosen, gate = gate_parts(ffn, s.router[...], route)
        s.output[at] = attended + gate * expert_out
        d_gate = jnp.sum(cot * expert_out, axis=1, keepdims=True)
        d_logits = d_gate * gate * (chosen - probs)
        for e in range(E):
            d_normed = d_normed + d_logits[:, e : e + 1] * router_rows[e : e + 1]
            grad = jnp.sum(d_logits[:, e : e + 1] * ffn.astype(F32), axis=0, keepdims=True)
            small = small + jnp.where(row_id == 2 + e, grad, 0.0)
        back, gain_grad = norm_back(attended, gain_f, d_normed)
        small = small + jnp.where(row_id == 1, gain_grad, 0.0)
        d_attended = cot + back
        s.attended[at] = d_attended
        s.x_rows[block(part)] = d_attended.astype(BF)
        gathers[part].start()
    s.small[...] = small
    for part in range(2):
        gathers[part].forward()
    for j in (0, Z_FIRST[0]):
        reduce.relay(j)
    for part in range(2):
        gathers[part].finish()

    scale = jnp.asarray(1.0 / math.sqrt(HD), BF)
    d_ctx = nn(s.x_rows[...], s.w_attn[:, 3 * width :]).astype(BF)
    d_ctx_t = jnp.transpose(d_ctx)
    s.dc_t[...] = d_ctx_t
    s.k_t[...] = jnp.transpose(s.qkv[:, width : 2 * width])
    product = d_ctx_t.astype(F32) * s.ctx_t[...].astype(F32)
    for hd in range(heads):
        band = slice(hd * HD, (hd + 1) * HD)
        s.qn[hd] = s.qkv[:, band] * scale
        s.vn[hd] = s.qkv[:, 2 * width + hd * HD : 2 * width + (hd + 1) * HD]
        s.dcn[hd] = d_ctx[:, band]
        s.delta[hd : hd + 1] = jnp.sum(product[band], axis=0, keepdims=True)
    s.dq_t[...] = jnp.zeros_like(s.dq_t)
    s.near[...] = jnp.zeros_like(s.near)
    for j in range(seq // QT):
        attend_back_block(heads, s, j, seq)
    reduce.arrive(4)
    for j in (1, Z_FIRST[1], 2, 3):
        reduce.relay(j)
    wire.settle()
    s.dqkv[:, :width] = jnp.transpose((s.dq_t[...] * (1.0 / math.sqrt(HD))).astype(BF))
    s.branch[...] = nt(s.dqkv[...], s.w_attn[:, : 3 * width]).astype(BF)
    sums = [Sums(h, wire, s.branch, *narrow, rows, part, 2) for part in range(2)]
    for part in range(2):
        sums[part].start()
    s.acc[:, : 3 * width] = tn(s.attn_rows[...], s.dqkv[...])
    s.acc[:, 3 * width : model] = tn(s.x_rows[...], s.ctx[...])
    reduce.store(2 * E, s.acc, shard)
    reduce.start(2 * E)
    for part in range(2):
        sums[part].cross()
    reduce.arrive(5)
    reduce.relay(4)
    reduce.cross(0)
    lines = diagonal_lines(heads, s.near)
    flat = jnp.concatenate(lines, axis=1)
    small = s.small[...]
    places = jnp.concatenate([flat, flat], axis=1)
    lane = iota((8, model), 1) // flat.shape[1]
    mine = (row_id == 6 + h.t // 2) & (lane == h.t % 2)
    small = small + jnp.where(mine, places, 0.0)

    for part in range(2):
        at = slice(part * half, (part + 1) * half)
        back, gain_grad = norm_back(s.tokens[at], gain_a, sums[part].total())
        s.grad_tokens[at] = s.attended[at] + back
        small = small + jnp.where(row_id == 0, gain_grad, 0.0)
    reduce.arrive(6)
    reduce.relay(5)
    reduce.cross(1)
    s.small[...] = add_everywhere(h, wire, small, s.small_land)
    reduce.arrive(7)
    reduce.relay(6)
    reduce.arrive(2 * E)
    reduce.relay(7)
    reduce.relay(2 * E)
    for e in range(E):
        s.grad_inner[e] = reduce.total(2 * e)
        s.grad_outer[e] = reduce.total(2 * e + 1)
    attn = reduce.total(2 * E)
    s.grad_q[...] = attn[:, :width]
    s.grad_k[...] = attn[:, width : 2 * width]
    s.grad_v[...] = attn[:, 2 * width : 3 * width]
    s.grad_o[...] = jnp.transpose(attn[:, 3 * width :])
    wire.settle()
    weights.close()
    reduce.close()


def layer(table, tokens, cot, segments, routes, gain_a, gain_f, router, wq, wk, wv, wo, w_in, w_out):
    rows, model = tokens.shape
    seq = segments.shape[1]
    shard, width = wq.shape
    heads = width // HD
    hidden = w_in.shape[2]
    vmem = pl.BlockSpec(memory_space=pltpu.VMEM)
    hbm = pl.BlockSpec(memory_space=pl.ANY)
    ins = [
        ("table", table, vmem), ("tokens", tokens, vmem), ("cot", cot, vmem),
        ("segments", segments, vmem), ("routes", routes, vmem), ("gain_a", gain_a, vmem),
        ("gain_f", gain_f, vmem), ("router", router, vmem), ("wq", wq, vmem), ("wk", wk, vmem),
        ("wv", wv, vmem), ("wo", wo, vmem), ("w_in", w_in, hbm), ("w_out", w_out, hbm),
    ]
    outs = [
        ("output", (rows, model), F32, vmem),
        ("grad_tokens", (rows, model), F32, vmem),
        ("grad_q", (shard, width), F32, vmem),
        ("grad_k", (shard, width), F32, vmem),
        ("grad_v", (shard, width), F32, vmem),
        ("grad_o", (width, shard), F32, vmem),
        ("small", (8, model), F32, vmem),
        ("grad_inner", (E, shard, hidden), F32, vmem),
        ("grad_outer", (E, shard, hidden), F32, vmem),
        ("experts", (2 * E, model, hidden), BF, hbm),
        ("y_land", (2 * E + 1, 4, shard, model), BF, hbm),
        ("e_land", (LEGS, 2, shard, model), BF, hbm),
        ("z_land", (LEGS, 2, shard, model), BF, hbm),
    ]
    scratch = [
        ("attn_shard", (shard, model), BF),
        ("attn_rows", (seq, model), BF),
        ("qkv", (seq, 3 * width), BF),
        ("ctx", (seq, width), BF),
        ("lse", (8, seq), F32),
        ("delta", (8, seq), F32),
        ("w_attn", (model, 4 * width), BF),
        ("first", (8, seq), jnp.int32),
        ("attended", (rows, model), F32),
        ("x_rows", (seq, model), BF),
        ("d_rows", (seq, model), BF),
        ("x_t", (model, seq), BF),
        ("d_t", (model, seq), BF),
        ("active", (seq, hidden), BF),
        ("d_inner", (seq, hidden), BF),
        ("terms", (seq, 2 * model), BF),
        ("w_buf", (2, model, hidden), BF),
        ("acc", (heads * QT, seq), F32),
        ("q_t", (width, seq), BF),
        ("k_t", (width, seq), BF),
        ("v_t", (width, seq), BF),
        ("dc_t", (width, seq), BF),
        ("ctx_t", (width, seq), BF),
        ("kn", (heads, seq, HD), BF),
        ("vn", (heads, seq, HD), BF),
        ("qn", (heads, seq, HD), BF),
        ("dcn", (heads, seq, HD), BF),
        ("bias", (heads, 2, HALF, HALF), F32),
        ("far", (8, QT), F32),
        ("tab", table.shape, F32),
        ("route_col", (seq, 8), jnp.int32),
        ("near", (heads, 2, HALF, HALF), F32),
        ("dq_t", (width, seq), F32),
        ("dqkv", (seq, 3 * width), BF),
        ("branch", (seq, model), BF),
        ("landed", (2, 2, rows // 2, 2 * model), BF),
        ("out", (2, rows // 2, 2 * model), BF),
        ("back", (2, rows // 2, 2 * model), BF),
        ("mine", (2 * E + 1, 4, shard, model), BF),
        ("other", (2 * E + 1, 4, shard, model), BF),
        ("y_stage", (4, shard, model), BF),
        ("e_stage", (2, shard, model), BF),
        ("z_stage", (2, shard, model), BF),
        ("small_land", (10, 8, model), F32),
    ]
    sems = [
        ("t_send", T_SEMS), ("t_recv", T_SEMS), ("w_send", W_SEMS), ("w_recv", W_SEMS),
        ("g_send", G_SEMS), ("g_recv", G_SEMS), ("own_sem", PIECES), ("local_sem", 5),
    ]
    names = [i[0] for i in ins] + [o[0] for o in outs] + [c[0] for c in scratch]
    names += [c[0] for c in sems]
    return pl.pallas_call(
        functools.partial(layer_kernel, heads, names),
        out_shape=tuple(jax.ShapeDtypeStruct(o[1], o[2]) for o in outs),
        in_specs=[i[2] for i in ins],
        out_specs=tuple(o[3] for o in outs),
        scratch_shapes=[pltpu.VMEM(c[1], c[2]) for c in scratch]
        + [pltpu.SemaphoreType.DMA((c[1],)) for c in sems],
        compiler_params=pltpu.CompilerParams(
            vmem_limit_bytes=VMEM_MAX, collective_id=1, has_side_effects=True
        ),
        cost_estimate=pl.CostEstimate(flops=4 * 10**10, bytes_accessed=10**8, transcendentals=10**7),
        name="layer",
    )(*[i[1] for i in ins])


def rms_apply(values, gain_vec):
    inverse = lax.rsqrt(jnp.mean(values * values, axis=-1, keepdims=True) + EPSILON)
    return values * inverse * gain_vec


def finish_kernel(heads_all, copies, *refs):
    small = refs[0]
    srcs, outs = refs[1 : 1 + copies], refs[1 + copies : 1 + 2 * copies]
    gain_a, gain_f, router, table = refs[1 + 2 * copies : 5 + 2 * copies]
    held, sem = refs[5 + 2 * copies : -1], refs[-1]
    loads = [pltpu.make_async_copy(a, v, sem.at[0, k]) for k, (a, v) in enumerate(zip(srcs, held))]
    moves = [pltpu.make_async_copy(v, b, sem.at[1, k]) for k, (v, b) in enumerate(zip(held, outs))]
    for load in loads:
        load.start()
    model = small.shape[1]
    gain_a[...] = small[0:1].reshape(model)
    gain_f[...] = small[1:2].reshape(model)
    router[...] = small[2 : 2 + E]
    per_row = model // HALF
    lines = [
        small[6 + k // per_row : 7 + k // per_row, (k % per_row) * HALF : (k % per_row + 1) * HALF]
        for k in range(heads_all)
    ]
    distance, bucket = iota((HALF, NBKT), 0), iota((HALF, NBKT), 1)
    pick = jnp.zeros((HALF, NBKT), F32)
    for b in range(NBKT - 1):
        inside = (distance >= FIRST[b]) & (distance < FIRST[b + 1]) & (bucket == b)
        pick = jnp.where(inside, 1.0, pick)
    pick = jnp.where((distance < NEAR) & (bucket == NBKT - 1), -1.0, pick)
    table[...] = lax.dot_general(
        jnp.concatenate(lines, axis=0), pick, (((1,), (0,)), ((), ())),
        precision=lax.Precision.HIGHEST, preferred_element_type=F32,
    )
    for load, move in zip(loads, moves):
        load.wait()
        move.start()
    for move in moves:
        move.wait()


def finish(small, arrays, heads_all):
    model = small.shape[1]
    vmem = pl.BlockSpec(memory_space=pltpu.VMEM)
    hbm = pl.BlockSpec(memory_space=pl.ANY)
    n = len(arrays)
    return pl.pallas_call(
        functools.partial(finish_kernel, heads_all, n),
        out_shape=tuple(jax.ShapeDtypeStruct(a.shape, a.dtype) for a in arrays)
        + (
            jax.ShapeDtypeStruct((model,), F32),
            jax.ShapeDtypeStruct((model,), F32),
            jax.ShapeDtypeStruct((E, model), F32),
            jax.ShapeDtypeStruct((heads_all, NBKT), F32),
        ),
        in_specs=[vmem] + [hbm] * n,
        out_specs=(hbm,) * n + (vmem,) * 4,
        scratch_shapes=[pltpu.VMEM(a.shape, a.dtype) for a in arrays]
        + [pltpu.SemaphoreType.DMA((2, n))],
        compiler_params=pltpu.CompilerParams(vmem_limit_bytes=VMEM_MAX),
        cost_estimate=pl.CostEstimate(flops=10**6, bytes_accessed=10**7, transcendentals=0),
        name="finish",
    )(small, *arrays)


def table_grad(diag):
    onehot = jnp.asarray((BUCKETS[:HALF, None] == np.arange(NBKT - 1)[None, :]).astype(np.float32))
    near_sums = jnp.dot(onehot.T, diag.T, precision=lax.Precision.HIGHEST)
    return jnp.concatenate([near_sums, -jnp.sum(near_sums, axis=0, keepdims=True)], axis=0)


def per_device_grid(
    tokens, segments, routes, cotangent, gain_attn, w_query, w_key, w_value, w_output, rel_table,
    gain_ffn, w_router, w_inner, w_outer,
):
    out = layer(
        jnp.transpose(rel_table), tokens, cotangent, segments[None, :], jnp.transpose(routes),
        gain_attn, gain_ffn, jnp.transpose(w_router), w_query, w_key, w_value, w_output, w_inner,
        jnp.transpose(w_outer, (0, 2, 1)),
    )
    small = out[6]
    done = finish(small, [*out[:6], out[7], out[8]], rel_table.shape[1])
    output, grad_tokens, grad_q, grad_k, grad_v, grad_o, grad_inner, grad_outer = done[:8]
    gain_a, gain_f, grad_router, grad_table = done[8:]
    return (
        output, grad_tokens, gain_a, grad_q, grad_k, grad_v, grad_o, jnp.transpose(grad_table),
        gain_f, jnp.transpose(grad_router), grad_inner, jnp.transpose(grad_outer, (0, 2, 1)),
    )


def per_device(
    tokens, segments, routes, cotangent, gain_attn, w_query, w_key, w_value, w_output, rel_table,
    gain_ffn, w_router, w_inner, w_outer,
):
    part_index = lax.axis_index("tensor")
    rows_local, model = tokens.shape
    seq_len = segments.shape[0]
    width = w_query.shape[1]
    heads = width // HD
    all_heads = rel_table.shape[1]
    hidden = w_inner.shape[2]

    attn_shard = jnp.concatenate([w_query, w_key, w_value, jnp.transpose(w_output)], axis=1)
    w_attn = gather_dp(attn_shard)
    both_shard = jnp.concatenate([w_inner, jnp.transpose(w_outer, (0, 2, 1))], axis=2)
    w_experts = [gather_dp(both_shard[e]) for e in range(E)]
    offs = jnp.zeros((1,), jnp.int32)
    slot_row, slot_col, plan = make_plan(jnp.reshape(routes, (1, seq_len)))
    counts = [jnp.sum((segments < s).astype(jnp.int32)) for s in range(1, 5)]
    first_key = jnp.zeros_like(segments)
    for s in range(1, 5):
        first_key = jnp.where(segments >= s, counts[s - 1], first_key)
    first_key = first_key[None, :]
    table = jnp.transpose(
        lax.dynamic_slice_in_dim(rel_table.astype(F32), part_index * heads, heads, 1)
    )

    normed_attn, norm_one_pull = jax.vjp(rms_apply, tokens, gain_attn.astype(F32))
    attn_rows = lax.all_gather(normed_attn.astype(BF), "tensor", axis=0, tiled=True)
    qkv, ctx, lse, branch = attend(attn_rows, w_attn, table, first_key, heads)
    attended = tokens + lax.psum_scatter(
        branch, "tensor", scatter_dimension=0, tiled=True
    ).astype(F32)

    normed_ffn, norm_two_pull = jax.vjp(rms_apply, attended, gain_ffn.astype(F32))
    ffn_in = normed_ffn.astype(BF)
    local_routes = lax.dynamic_slice_in_dim(routes[:, 0], part_index * rows_local, rows_local, 0)
    route_mask = (local_routes[:, None] == jnp.arange(E, dtype=jnp.int32)[None, :]).astype(F32)

    def gate_of(normed_values, router_values):
        logits = jnp.dot(normed_values, router_values, precision=lax.Precision.HIGHEST)
        return jnp.sum(jax.nn.softmax(logits, axis=-1) * route_mask, axis=-1)

    gate_weight, gate_pull = jax.vjp(gate_of, ffn_in.astype(F32), w_router.astype(F32))
    d_expert = (cotangent * gate_weight[:, None]).astype(BF)
    xd = lax.all_gather(jnp.concatenate([ffn_in, d_expert], axis=1), "tensor", axis=0, tiled=True)

    terms = None
    expert_sums = []
    for e in range(E):
        terms, part = expert(e, plan, offs, xd, slot_row, slot_col, terms, w_experts[e])
        expert_sums.append(reduce_dp(part[0]))
    sums = lax.psum_scatter(terms, "tensor", scatter_dimension=0, tiled=True).astype(F32)
    expert_out, d_ffn_local = sums[:, :model], sums[:, model:]
    output = attended + gate_weight[:, None] * expert_out
    d_gate = jnp.sum(cotangent * expert_out, axis=-1)

    d_ffn_router, grad_router_local = gate_pull(d_gate)
    d_attended_norm, grad_gain_two = norm_two_pull(d_ffn_local + d_ffn_router)
    d_attended = cotangent + d_attended_norm
    d_branch_rows = lax.all_gather(d_attended.astype(BF), "tensor", axis=0, tiled=True)

    total_rows, diag, attn_part = attend_back(
        d_branch_rows, w_attn, qkv, ctx, lse, first_key, attn_rows, table, offs, heads
    )
    attn_sum = reduce_dp(attn_part[0])
    d_attn_local = lax.psum_scatter(
        total_rows, "tensor", scatter_dimension=0, tiled=True
    ).astype(F32)
    d_tokens_norm, grad_gain_one = norm_one_pull(d_attn_local)
    grad_tokens = d_attended + d_tokens_norm
    grad_table_full = lax.dynamic_update_slice_in_dim(
        jnp.zeros((NBKT, all_heads), F32), table_grad(diag[:heads]), part_index * heads, 1
    )
    small_sums = lax.psum(
        (grad_gain_one, grad_gain_two, grad_router_local, grad_table_full), ("dp", "tensor")
    )
    return (
        output,
        grad_tokens,
        small_sums[0],
        attn_sum[:, :width],
        attn_sum[:, width : 2 * width],
        attn_sum[:, 2 * width : 3 * width],
        jnp.transpose(attn_sum[:, 3 * width :]),
        small_sums[3],
        small_sums[1],
        small_sums[2],
        jnp.stack([part[:, :hidden] for part in expert_sums]),
        jnp.stack([jnp.transpose(part[:, hidden:]) for part in expert_sums]),
    )


def solution(mesh):
    sizes = dict(mesh.shape)
    in_specs = (
        P(("dp", "tensor"), None),
        P("dp"),
        P("dp", None),
        P(("dp", "tensor"), None),
        P(),
        P("dp", "tensor"),
        P("dp", "tensor"),
        P("dp", "tensor"),
        P("tensor", "dp"),
        P(),
        P(),
        P(),
        P(None, "dp", "tensor"),
        P(None, "tensor", "dp"),
    )
    out_specs = (
        P(("dp", "tensor"), None),
        P(("dp", "tensor"), None),
        P(),
        P("dp", "tensor"),
        P("dp", "tensor"),
        P("dp", "tensor"),
        P("tensor", "dp"),
        P(),
        P(),
        P(),
        P(None, "dp", "tensor"),
        P(None, "tensor", "dp"),
    )
    return jax.shard_map(
        per_device_grid if sizes["dp"] == 8 and sizes["tensor"] == 4 else per_device,
        mesh=mesh,
        in_specs=in_specs,
        out_specs=out_specs,
        check_vma=False,
    )
```

```python
import functools
import math

import jax
import jax.numpy as jnp
import numpy as np
from jax import lax
from jax.experimental import pallas as pl
from jax.experimental.pallas import tpu as pltpu
from jax.sharding import PartitionSpec as P

HD = 64
NBKT = 32
MAXD = 128
E = 4
WIN = 1024
QT = 256
HALF = 128
ROWS = 256

EPSILON = 1e-06
NEG_LARGE = -1e30
BF = jnp.bfloat16
F32 = jnp.float32
VMEM_MAX = 63 * 1024 * 1024


def bucket_numbers(window, buckets, far_distance):
    distance = np.arange(window)
    exact_part = buckets // 2
    safe_distance = np.maximum(distance, 1) * 1.0
    log_part = exact_part + np.floor(
        np.log(safe_distance / exact_part)
        / np.log(far_distance / exact_part)
        * (buckets - exact_part)
    ).astype(np.int32)
    log_part = np.minimum(log_part, buckets - 1)
    return np.where(distance < exact_part, distance, log_part).astype(np.int32)


BUCKETS = bucket_numbers(WIN, NBKT, MAXD)
FIRST = [int(np.argmax(BUCKETS == b)) for b in range(NBKT)]
NEAR = FIRST[NBKT - 1]


def nn(a, b):
    return lax.dot_general(a, b, (((1,), (0,)), ((), ())), preferred_element_type=F32)


def nt(a, b):
    return lax.dot_general(a, b, (((1,), (1,)), ((), ())), preferred_element_type=F32)


def tn(a, b):
    return lax.dot_general(a, b, (((0,), (0,)), ((), ())), preferred_element_type=F32)


class Names:
    pass


def iota(shape, dim):
    return lax.broadcasted_iota(jnp.int32, shape, dim)


def gather_dp(shard):
    return lax.all_gather(shard, "dp", axis=0, tiled=True)


def reduce_dp(part):
    return lax.psum_scatter(part, "dp", scatter_dimension=0, tiled=True).astype(F32)


def plan_kernel(route_ref, slot_row_ref, slot_col_ref, plan_ref):
    length = route_ref.shape[1]
    route = route_ref[...]
    chosen = jnp.where(iota((8, length), 0) == route, 1.0, 0.0).astype(F32)
    upper = jnp.where(iota((length, length), 0) < iota((length, length), 1), 1.0, 0.0)
    before = nn(chosen.astype(BF), upper.astype(BF))
    rank = jnp.sum(chosen * before, axis=0, keepdims=True)
    start = jnp.int32(0)
    base = jnp.zeros((1, length), F32)
    for e in range(E):
        here = route == e
        count = jnp.sum(jnp.where(here, 1, 0))
        tiles = (count + (ROWS - 1)) // ROWS
        plan_ref[e] = tiles
        plan_ref[E + e] = start
        base = base + jnp.where(here, start.astype(F32), 0.0)
        start = start + tiles * ROWS
    slots = jnp.broadcast_to(rank + base, (8, length))
    slot_row_ref[...] = slots.astype(jnp.int32)
    slot_col_ref[...] = jnp.transpose(slots).astype(jnp.int32)


def make_plan(route_row):
    length = route_row.shape[1]
    return pl.pallas_call(
        plan_kernel,
        out_shape=(
            jax.ShapeDtypeStruct((8, length), jnp.int32),
            jax.ShapeDtypeStruct((length, 8), jnp.int32),
            jax.ShapeDtypeStruct((2 * E,), jnp.int32),
        ),
        in_specs=[pl.BlockSpec(memory_space=pltpu.VMEM)],
        out_specs=(
            pl.BlockSpec(memory_space=pltpu.VMEM),
            pl.BlockSpec(memory_space=pltpu.VMEM),
            pl.BlockSpec(memory_space=pltpu.SMEM),
        ),
        compiler_params=pltpu.CompilerParams(vmem_limit_bytes=VMEM_MAX),
        name="route_plan",
    )(route_row)


def fill_bias(bias_ref, far_ref, table_rows):
    step = iota((HALF, HALF), 1) - iota((HALF, HALF), 0)
    for h, row in enumerate(table_rows):
        far_ref[h : h + 1] = jnp.broadcast_to(row[:, NBKT - 1 :], (1, far_ref.shape[1]))
    for side in range(2):
        distance = step + side * HALF
        tiles = [jnp.broadcast_to(row[:, NBKT - 1 :], (HALF, HALF)) for row in table_rows]
        for b in reversed(range(NBKT - 1)):
            below = distance < FIRST[b + 1]
            for h, row in enumerate(table_rows):
                tiles[h] = jnp.where(below, row[:, b : b + 1], tiles[h])
        for h, tile in enumerate(tiles):
            bias_ref[h, side] = tile


def biased_scores(raw, gap, h, bias_ref, far_ref, first_key, key_start):
    far = far_ref[h : h + 1]
    keys = key_start + iota((QT, QT), 0)
    if gap >= 2:
        return jnp.where(keys >= first_key, raw + far, NEG_LARGE)
    diag, near = bias_ref[h, 0], bias_ref[h, 1]
    const = jnp.broadcast_to(far[:, :HALF], (HALF, HALF))
    if gap == 1:
        tile = jnp.concatenate(
            [
                jnp.concatenate([const, const], axis=1),
                jnp.concatenate([near, const], axis=1),
            ],
            axis=0,
        )
        return jnp.where(keys >= first_key, raw + tile, NEG_LARGE)
    tile = jnp.concatenate(
        [jnp.concatenate([diag, near], axis=1), jnp.concatenate([const, diag], axis=1)], axis=0
    )
    causal = iota((QT, QT), 0) <= iota((QT, QT), 1)
    return jnp.where((keys >= first_key) & causal, raw + tile, NEG_LARGE)


def attend_blocks(heads, first_ref, q_t, v_t, kn, bias_ref, far_ref, s_ref, ctx_t, lse_ref, blocks):
    for i in blocks:
        cols = slice(i * QT, (i + 1) * QT)
        first_key = first_ref[0:1, cols]
        for h in range(heads):
            band = slice(h * HD, (h + 1) * HD)
            q_blk = q_t[band, cols]
            peak = None
            for j in range(i + 1):
                raw = nn(kn[h, j * QT : (j + 1) * QT], q_blk)
                s = biased_scores(raw, i - j, h, bias_ref, far_ref, first_key, j * QT)
                s_ref[h * QT : (h + 1) * QT, j * QT : (j + 1) * QT] = s
                top = jnp.max(s, axis=0, keepdims=True)
                peak = top if peak is None else jnp.maximum(peak, top)
            total = jnp.zeros((1, QT), F32)
            acc = jnp.zeros((HD, QT), F32)
            for j in range(i + 1):
                p = jnp.exp(s_ref[h * QT : (h + 1) * QT, j * QT : (j + 1) * QT] - peak)
                total = total + jnp.sum(p, axis=0, keepdims=True)
                acc = acc + nn(v_t[band, j * QT : (j + 1) * QT], p.astype(BF))
            ctx_t[band, cols] = (acc / total).astype(BF)
            lse_ref[h : h + 1, cols] = peak + jnp.log(total)


def project(heads, x, w_ref, qkv_ref, q_t, v_t, kn):
    width = heads * HD
    qkv = nn(x, w_ref[:, : 3 * width]).astype(BF)
    qkv_ref[...] = qkv
    q_t[...] = jnp.transpose(qkv[:, :width]) * jnp.asarray(1.0 / math.sqrt(HD), BF)
    v_t[...] = jnp.transpose(qkv[:, 2 * width :])
    for h in range(heads):
        kn[h] = qkv[:, width + h * HD : width + (h + 1) * HD]


def attend_kernel(heads, table_ref, x_ref, first_ref, w_ref, *refs):
    qkv_ref, ctx_ref, lse_ref, branch_ref, q_t, v_t, kn, bias_ref, far_ref, s_ref, ctx_t = refs
    width = heads * HD
    seq = x_ref.shape[0]
    fill_bias(bias_ref, far_ref, [table_ref[hd : hd + 1, :] for hd in range(heads)])
    project(heads, x_ref[...], w_ref, qkv_ref, q_t, v_t, kn)
    blocks = range(seq // QT)
    attend_blocks(
        heads, first_ref, q_t, v_t, kn, bias_ref, far_ref, s_ref, ctx_t, lse_ref, blocks
    )
    ctx = jnp.transpose(ctx_t[...])
    ctx_ref[...] = ctx
    branch_ref[...] = nt(ctx, w_ref[:, 3 * width :]).astype(BF)


def attend(x, w, table, first_key, heads):
    seq, model = x.shape
    width = heads * HD
    vmem = pl.BlockSpec(memory_space=pltpu.VMEM)
    return pl.pallas_call(
        functools.partial(attend_kernel, heads),
        out_shape=(
            jax.ShapeDtypeStruct((seq, 3 * width), BF),
            jax.ShapeDtypeStruct((seq, width), BF),
            jax.ShapeDtypeStruct((8, seq), F32),
            jax.ShapeDtypeStruct((seq, model), BF),
        ),
        in_specs=[vmem] * 4,
        out_specs=(vmem,) * 4,
        scratch_shapes=[
            pltpu.VMEM((width, seq), BF),
            pltpu.VMEM((width, seq), BF),
            pltpu.VMEM((heads, seq, HD), BF),
            pltpu.VMEM((heads, 2, HALF, HALF), F32),
            pltpu.VMEM((8, QT), F32),
            pltpu.VMEM((heads * QT, seq), F32),
            pltpu.VMEM((width, seq), BF),
        ],
        compiler_params=pltpu.CompilerParams(vmem_limit_bytes=VMEM_MAX),
        cost_estimate=pl.CostEstimate(flops=4 * 10**9, bytes_accessed=10**7, transcendentals=2 * 10**6),
        name="attend",
    )(table, x, first_key, w)


def attend_back_block(heads, s, j, seq):
    width = heads * HD
    keys = slice(j * QT, (j + 1) * QT)
    for h in range(heads):
        band = slice(h * HD, (h + 1) * HD)
        dk = jnp.zeros((QT, HD), F32)
        dv = jnp.zeros((QT, HD), F32)
        for i in range(j, seq // QT):
            cols = slice(i * QT, (i + 1) * QT)
            raw = nn(s.kn[h, keys], s.q_t[band, cols])
            scores = biased_scores(raw, i - j, h, s.bias, s.far, s.first[0:1, cols], j * QT)
            p = jnp.exp(scores - s.lse[h : h + 1, cols])
            dp = nn(s.vn[h, keys], s.dc_t[band, cols])
            ds = p * (dp - s.delta[h : h + 1, cols])
            if i == j:
                s.near[h, 0] += ds[:HALF, :HALF] + ds[HALF:, HALF:]
                s.near[h, 1] += ds[:HALF, HALF:]
            elif i == j + 1:
                s.near[h, 1] += ds[HALF:, :HALF]
            ds = ds.astype(BF)
            dv = dv + nn(p.astype(BF), s.dcn[h, cols])
            dk = dk + nn(ds, s.qn[h, cols])
            s.dq_t[band, cols] += nn(s.k_t[band, keys], ds)
        s.dqkv[keys, width + h * HD : width + (h + 1) * HD] = dk.astype(BF)
        s.dqkv[keys, 2 * width + h * HD : 2 * width + (h + 1) * HD] = dv.astype(BF)


def diagonal_lines(heads, near):
    key, query = iota((HALF, HALF), 0), iota((HALF, HALF), 1)
    lines = []
    for h in range(heads):
        both = near[h, 0] + jnp.where(query < key, near[h, 1], 0.0)
        for bit in range(7):
            turned = pltpu.roll(both, HALF - (1 << bit), 1)
            both = jnp.where((key >> bit) & 1 == 1, turned, both)
        lines.append(jnp.sum(both, axis=0, keepdims=True))
    return lines


def attend_back_kernel(heads, blocks, names, *refs):
    s = Names()
    for name, ref in zip(names, refs):
        setattr(s, name, ref)
    grads = refs[len(names) :]
    width = heads * HD
    seq = s.d.shape[0]
    scale = jnp.asarray(1.0 / math.sqrt(HD), BF)
    fill_bias(s.bias, s.far, [s.tab[hd : hd + 1, :] for hd in range(heads)])
    d_rows = s.d[...]
    ctx = s.ctx[...]
    dc = nn(d_rows, s.w[:, 3 * width :]).astype(BF)
    s.acc[:, 3 * width :] = tn(d_rows, ctx)
    dct = jnp.transpose(dc)
    s.dc_t[...] = dct
    qkv = s.qkv[...]
    s.q_t[...] = jnp.transpose(qkv[:, :width]) * scale
    s.k_t[...] = jnp.transpose(qkv[:, width : 2 * width])
    product = dct.astype(F32) * jnp.transpose(ctx).astype(F32)
    for h in range(heads):
        band = slice(h * HD, (h + 1) * HD)
        s.qn[h] = qkv[:, band] * scale
        s.kn[h] = qkv[:, width + h * HD : width + (h + 1) * HD]
        s.vn[h] = qkv[:, 2 * width + h * HD : 2 * width + (h + 1) * HD]
        s.dcn[h] = dc[:, band]
        s.delta[h : h + 1] = jnp.sum(product[band], axis=0, keepdims=True)
    s.dq_t[...] = jnp.zeros_like(s.dq_t)
    s.near[...] = jnp.zeros_like(s.near)
    for j in range(seq // QT):
        attend_back_block(heads, s, j, seq)
    s.dqkv[:, :width] = jnp.transpose((s.dq_t[...] * (1.0 / math.sqrt(HD))).astype(BF))
    d_qkv = s.dqkv[...]
    s.rows[...] = nt(d_qkv, s.w[:, : 3 * width]).astype(BF)
    s.acc[:, : 3 * width] = tn(s.x[...], d_qkv)
    scatter_rows(s.acc, s.offs, grads, blocks)
    lines = diagonal_lines(heads, s.near) + [jnp.zeros((8 - heads, HALF), F32)]
    s.diag[...] = jnp.concatenate(lines, axis=0)


def scatter_rows(acc_ref, offs_ref, outs, blocks):
    k = 0
    for out, count in zip(outs, blocks):
        rows = out.shape[1]
        for b in range(count):
            at = pl.ds(pl.multiple_of(offs_ref[k], rows), rows)
            out[b] = acc_ref[at, :].astype(BF)
            k += 1


def attend_back(d_rows, w, qkv, ctx, lse, first_key, x, table, offs, heads):
    seq, model = x.shape
    width = heads * HD
    vmem = pl.BlockSpec(memory_space=pltpu.VMEM)
    smem = pl.BlockSpec(memory_space=pltpu.SMEM)
    scratch = [
        ("q_t", (width, seq), BF),
        ("k_t", (width, seq), BF),
        ("dc_t", (width, seq), BF),
        ("kn", (heads, seq, HD), BF),
        ("vn", (heads, seq, HD), BF),
        ("qn", (heads, seq, HD), BF),
        ("dcn", (heads, seq, HD), BF),
        ("bias", (heads, 2, HALF, HALF), F32),
        ("far", (8, QT), F32),
        ("dq_t", (width, seq), F32),
        ("dqkv", (seq, 3 * width), BF),
        ("near", (heads, 2, HALF, HALF), F32),
        ("delta", (8, seq), F32),
        ("acc", (model, 4 * width), F32),
    ]
    ins = ["offs", "tab", "d", "w", "qkv", "ctx", "lse", "first", "x"]
    names = ins + ["rows", "diag", "grads"] + [c[0] for c in scratch]

    def kernel(*refs):
        at = len(ins) + 2
        plain = refs[:at] + refs[at + 1 :]
        attend_back_kernel(
            heads, (1,), names[:at] + names[at + 1 :], *plain, refs[at]
        )

    out = pl.pallas_call(
        kernel,
        out_shape=(
            jax.ShapeDtypeStruct((seq, model), BF),
            jax.ShapeDtypeStruct((8, HALF), F32),
            jax.ShapeDtypeStruct((1, model, 4 * width), BF),
        ),
        in_specs=[smem] + [vmem] * 8,
        out_specs=(vmem,) * 3,
        scratch_shapes=[pltpu.VMEM(c[1], c[2]) for c in scratch],
        compiler_params=pltpu.CompilerParams(vmem_limit_bytes=VMEM_MAX),
        cost_estimate=pl.CostEstimate(flops=10**10, bytes_accessed=10**7, transcendentals=2 * 10**6),
        name="attend_back",
    )(offs, table, d_rows, w, qkv, ctx, lse, first_key, x)
    return out[0], out[1], out[2]


def expert_kernel(e, plan_ref, offs_ref, xd_ref, row_ref, col_ref, w_ref, *refs):
    terms_in = refs[0] if e > 0 else None
    terms_ref, grad, acc_ref = refs[-3:]
    model = xd_ref.shape[1] // 2
    hidden = w_ref.shape[1] // 2
    length = xd_ref.shape[0]
    terms_ref[...] = jnp.zeros_like(terms_ref) if terms_in is None else terms_in[...]
    acc_ref[...] = jnp.zeros_like(acc_ref)
    base = plan_ref[E + e]

    @pl.loop(0, plan_ref[e])
    def _(t):
        start = base + t * ROWS
        pick = jnp.where(row_ref[0:1, :] == start + iota((ROWS, length), 0), 1.0, 0.0).astype(BF)
        xd = nn(pick, xd_ref[...]).astype(BF)
        x, d = xd[:, :model], xd[:, model:]
        inner = nn(x, w_ref[:, :hidden])
        cubic = 0.044715 * inner * inner
        tanh = jnp.tanh(math.sqrt(2.0 / math.pi) * inner * (1.0 + cubic))
        half = 0.5 * (1.0 + tanh)
        active = (inner * half).astype(BF)
        slope = half + (0.5 * math.sqrt(2.0 / math.pi)) * inner * (1.0 - tanh * tanh) * (1.0 + 3.0 * cubic)
        out = nt(active, w_ref[:, hidden:]).astype(BF)
        d_inner = (nn(d, w_ref[:, hidden:]) * slope).astype(BF)
        acc_ref[:, :hidden] += tn(x, d_inner)
        acc_ref[:, hidden:] += tn(d, active)
        d_x = nt(d_inner, w_ref[:, :hidden]).astype(BF)
        place = jnp.where(col_ref[:, 0:1] == start + iota((length, ROWS), 1), 1.0, 0.0).astype(BF)
        terms_ref[:, :model] = (terms_ref[:, :model].astype(F32) + nn(place, out)).astype(BF)
        terms_ref[:, model:] = (terms_ref[:, model:].astype(F32) + nn(place, d_x)).astype(BF)

    scatter_rows(acc_ref, offs_ref, [grad], (1,))


def expert(e, plan, offs, xd, slot_row, slot_col, terms, w):
    length, both = xd.shape
    model, hidden2 = w.shape
    vmem = pl.BlockSpec(memory_space=pltpu.VMEM)
    smem = pl.BlockSpec(memory_space=pltpu.SMEM)
    extra = [] if terms is None else [terms]
    return pl.pallas_call(
        functools.partial(expert_kernel, e),
        out_shape=(
            jax.ShapeDtypeStruct((length, both), BF),
            jax.ShapeDtypeStruct((1, model, hidden2), BF),
        ),
        in_specs=[smem] * 2 + [vmem] * (4 + len(extra)),
        out_specs=(vmem,) * 2,
        scratch_shapes=[pltpu.VMEM((model, hidden2), F32)],
        compiler_params=pltpu.CompilerParams(vmem_limit_bytes=VMEM_MAX),
        cost_estimate=pl.CostEstimate(flops=3 * 10**9, bytes_accessed=10**7, transcendentals=10**6),
        name=f"expert_{e}",
    )(plan, offs, xd, slot_row, slot_col, w, *extra)


MESH = pl.DeviceIdType.MESH
PIECES = 2 + 2 * E
LAST = PIECES - 1
T_SEMS = 48
W_SEMS = 9 * PIECES
Y_FIRST = (7, 8, LAST,)
Z_FIRST = {8: 9}
LEGS = 2 * E + 1 + len(Z_FIRST)
G_SEMS = 6 * LEGS


class Here:
    def __init__(self):
        self.d = lax.axis_index("dp")
        self.t = lax.axis_index("tensor")
        self.z, self.y = self.d // 2, self.d % 2
        self.x, self.c = self.t // 2, self.t % 2
        self.core = {"dp": self.d, "tensor": 2 * self.x + 1 - self.c}
        self.side = {"dp": self.d, "tensor": 2 * (1 - self.x) + self.c}
        self.over = {"dp": 2 * self.z + 1 - self.y, "tensor": self.t}

        self.low = self.z // 2
        self.middle = (self.z == 1) | (self.z == 2)
        self.pair_z = self.z + 1 - 2 * (self.z % 2)
        self.mid_z = 2 - self.low
        self.end_z = 3 - 3 * self.low
        self.order = [self.z, self.pair_z, self.mid_z, self.end_z]
        self.pair, self.far_mid, self.far_end = (self.at_z(z) for z in self.order[1:])

    def at_z(self, z):
        return {"dp": 2 * z + self.y, "tensor": self.t}

    def greet(self):
        barrier = pltpu.get_barrier_semaphore()
        peers = [self.core, self.side, self.over, self.pair, self.far_mid, self.far_end]
        for peer in peers:
            pl.semaphore_signal(barrier, inc=1, device_id=peer, device_id_type=MESH)
        pl.semaphore_wait(barrier, len(peers))


class Wire:
    def __init__(self, send, recv):
        self.send, self.recv, self.sent, self.count = send, recv, [], 0

    def take(self, number):
        self.count += number
        return self.count - number

    def plan(self, src, dst, peer, send, recv):
        return pltpu.make_async_remote_copy(
            src_ref=src, dst_ref=dst, send_sem=self.send.at[send], recv_sem=self.recv.at[recv],
            device_id=peer, device_id_type=MESH,
        )

    def __call__(self, src, dst, peer):
        k = self.take(1)
        copy = self.plan(src, dst, peer, k, k)
        copy.start()
        self.sent.append(copy)
        return copy

    def settle(self):
        for copy in self.sent:
            copy.wait_send()
        self.sent = []


class Rows:
    def __init__(self, here, wire, buf, rows, part, parts):
        self.here, self.wire, self.buf = here, wire, buf
        self.rows, self.size = rows, rows // parts
        self.shift = part * self.size

    def at(self, t):
        return self.buf.at[pl.ds(pl.multiple_of(t * self.rows + self.shift, 16), self.size)]

    def start(self):
        mine = self.at(self.here.t)
        self.far = self.wire(mine, mine, self.here.side)
        self.near = self.wire(mine, mine, self.here.core)

    def forward(self):
        self.far.wait_recv()
        theirs = self.at(2 * (1 - self.here.x) + self.here.c)
        self.last = self.wire(theirs, theirs, self.here.core)

    def finish(self):
        self.near.wait_recv()
        self.last.wait_recv()


class Sums:
    def __init__(self, here, wire, src, landed, out, back, rows, part, parts):
        self.here, self.wire, self.src = here, wire, src
        self.landed, self.out, self.back = landed, out, back
        self.rows, self.size = rows, rows // parts
        self.shift = part * self.size
        self.part = part

    def at(self, t):
        return pl.ds(pl.multiple_of(t * self.rows + self.shift, 16), self.size)

    def start(self):
        h = self.here
        self.copies = []
        for slot, x in ((0, 1 - h.x), (1, h.x)):
            src = self.src.at[self.at(2 * x + 1 - h.c)]
            self.copies.append(self.wire(src, self.landed.at[slot, self.part], h.core))

    def cross(self):
        h = self.here
        self.copies[0].wait_recv()
        mine = self.src[self.at(2 * (1 - h.x) + h.c)].astype(F32)
        self.out[self.part] = (mine + self.landed[0, self.part].astype(F32)).astype(BF)
        self.last = self.wire(self.out.at[self.part], self.back.at[self.part], h.side)

    def total(self):
        h = self.here
        self.copies[1].wait_recv()
        near = self.src[self.at(2 * h.x + h.c)].astype(F32) + self.landed[1, self.part].astype(F32)
        self.last.wait_recv()
        return near + self.back[self.part].astype(F32)


class Weights:
    def __init__(self, here, wire, own_sem, sources, target):
        self.here, self.wire, self.own_sem = here, wire, own_sem
        self.sources, self.target = sources, target
        self.over, self.own, self.z, self.relays = {}, {}, {}, []

    def at(self, p, z):
        rows = self.sources[p].shape[0]
        if p in Y_FIRST:
            return self.target(p, pl.ds(pl.multiple_of(2 * z * rows, 16), 2 * rows))
        return self.target(p, pl.ds(pl.multiple_of((2 * z + self.here.y) * rows, 16), rows))

    def start(self, p):
        h, src = self.here, self.sources[p]
        rows = src.shape[0]
        dst = self.target(p, pl.ds(pl.multiple_of(h.d * rows, 16), rows))
        self.own[p] = pltpu.make_async_copy(src, dst, self.own_sem.at[p])
        self.own[p].start()
        if p not in Y_FIRST:
            self.spread(p, src)
        self.over[p] = [self.wire(src, dst, h.over)]

    def pairs(self, p):
        self.over[p][0].wait_recv()
        self.own[p].wait()
        self.spread(p, self.at(p, self.here.z))

    def spread(self, p, src):
        h, wire = self.here, self.wire
        dst = self.at(p, h.z)
        k = wire.take(5)
        end = jnp.where(h.middle, 0, 1)
        near = wire.plan(src, dst, h.pair, k, k)
        far = wire.plan(src, dst, h.far_mid, k + 1, k + 1 + end)
        near.start()
        far.start()
        wire.sent += [near, far]
        relays = []
        for j, z in ((1, h.mid_z), (2, h.end_z)):
            block = self.at(p, z)
            relays.append(wire.plan(block, block, h.pair, k + 2 + j, k + j))
        self.z[p] = [near] + relays
        self.relays += relays

    def forward(self, p):
        h = self.here
        near, *relays = self.z[p]
        for copy, z in zip(self.z[p], h.order[1:]):
            copy.wait_recv()
            if copy is not near:
                pl.when(h.middle)(copy.start)
            if p not in Y_FIRST:
                block = self.at(p, z)
                self.over[p].append(self.wire(block, block, h.over))

    def finish(self, p):
        if p in Y_FIRST:
            return
        for copy in self.over[p]:
            copy.wait_recv()
        self.own[p].wait()

    def close(self):
        self.wire.settle()
        for copy in self.relays:
            pl.when(self.here.middle)(copy.wait_send)


def normed(values, gain):
    inverse = lax.rsqrt(jnp.mean(values * values, axis=-1, keepdims=True) + EPSILON)
    return values * inverse * gain


class Reduce:
    def __init__(self, here, wire, local, mine, other, y_land, e_land, z_land, e_stage):
        self.here, self.wire, self.local = here, wire, local
        self.mine, self.other = mine, other
        self.y_land, self.e_land, self.z_land = y_land, e_land, z_land
        self.e_stage = e_stage
        self.y, self.legs = {}, {}

    def fetch(self, src, dst, sem):
        copy = pltpu.make_async_copy(src, dst, self.local.at[sem])
        copy.start()
        copy.wait()

    def store(self, q, acc, shard):
        h = self.here
        for k, z in enumerate(h.order):
            for side, target in ((h.y, self.mine.at[q]), (1 - h.y, self.other.at[q])):
                at = pl.ds(pl.multiple_of((2 * z + side) * shard, 16), shard)
                target[k] = acc[at, : target.shape[2]].astype(BF)

    def start(self, q):
        if q in Z_FIRST:
            self.leg(q, self.mine.at[q])
            self.leg(Z_FIRST[q], self.other.at[q])
        else:
            self.y[q] = self.wire(self.other.at[q], self.y_land.at[q], self.here.over)

    def arrive(self, q):
        self.y[q].wait_recv()
        for k in range(4):
            pair = self.mine[q, k].astype(F32) + self.y_land[q, k].astype(F32)
            self.mine[q, k] = pair.astype(BF)
        self.leg(q, self.mine.at[q])

    def leg(self, j, blocks):
        h, wire = self.here, self.wire
        k = wire.take(5)
        near = wire.plan(blocks.at[1], self.z_land.at[j, 0], h.pair, k, k)
        hand = [
            wire.plan(blocks.at[2 + i], self.e_land.at[j, i], h.pair, k + 1 + i, k + 2 + i)
            for i in range(2)
        ]
        on = [
            wire.plan(blocks.at[2 + i], self.z_land.at[j, 1], peer, k + 3 + i, k + 1)
            for i, peer in enumerate((h.far_mid, h.far_end))
        ]

        @pl.when(jnp.logical_not(h.middle))
        def _():
            for copy in hand:
                copy.start()

        near.start()
        self.legs[j] = (blocks, near, hand, on)

    def relay(self, j):
        blocks, _, hand, on = self.legs[j]

        @pl.when(self.here.middle)
        def _():
            for copy in hand:
                copy.wait_recv()
            self.fetch(self.e_land.at[j], self.e_stage, 0)
            for i in range(2):
                both = blocks[2 + i].astype(F32) + self.e_stage[i].astype(F32)
                blocks[2 + i] = both.astype(BF)
                on[i].start()

    def along_z(self, j):
        blocks, near, _, on = self.legs[j]
        near.wait_recv()
        on[0].wait_recv()
        both = self.z_land[j, 0].astype(F32) + self.z_land[j, 1].astype(F32)
        return blocks[0].astype(F32) + both

    def cross(self, q):
        self.other[q, 0] = self.along_z(Z_FIRST[q]).astype(BF)
        self.y[q] = self.wire(self.other.at[q, 0], self.y_land.at[q, 0], self.here.over)

    def total(self, q):
        result = self.along_z(q)
        if q in Z_FIRST:
            self.y[q].wait_recv()
            result = result + self.y_land[q, 0].astype(F32)
        return result

    def close(self):
        self.wire.settle()
        for _, near, hand, on in self.legs.values():
            near.wait_send()
            for copy in on:
                pl.when(self.here.middle)(copy.wait_send)
            for copy in hand:
                pl.when(jnp.logical_not(self.here.middle))(copy.wait_send)


class SmallSum:
    def __init__(self, here, wire, value, land):
        self.here, self.wire, self.value, self.land = here, wire, value, land

    def start(self, step):
        h, wire, land = self.here, self.wire, self.land
        if step < 3:
            peer = (h.core, h.side, h.over)[step]
            land[2 * step] = self.value[...]
            self.copy = wire(land.at[2 * step], land.at[2 * step + 1], peer)
            return
        land[6 + h.z] = self.value[...]
        self.k = wire.take(3)
        own = land.at[6 + h.z]
        for i, peer in enumerate((h.pair, h.far_mid, h.far_end)):
            back = self.k if i == 0 else self.k + 1 + jnp.where(h.middle, 0, 1)
            copy = wire.plan(own, own, peer, self.k + i, back)
            copy.start()
            wire.sent.append(copy)

    def finish(self, step):
        h, land = self.here, self.land
        if step < 3:
            self.copy.wait_recv()
            self.value[...] += land[2 * step + 1]
            return
        own = land.at[6 + h.z]
        for i, z in enumerate(h.order[1:]):
            self.wire.plan(own, land.at[6 + z], h.pair, self.k + i, self.k + i).wait_recv()
        self.value[...] = (land[6] + land[7]) + (land[8] + land[9])


class Results:
    def __init__(self, s, reduce, width):
        self.s, self.reduce, self.width, self.moves = s, reduce, width, []

    def put(self, q):
        s, width = self.s, self.width
        total = self.reduce.total(q)
        if q == 2 * E:
            s.grad_q[...] = total[:, :width]
            s.grad_k[...] = total[:, width : 2 * width]
            s.grad_v[...] = total[:, 2 * width : 3 * width]
            s.grad_o[...] = jnp.transpose(total[:, 3 * width :])
            return
        slot = len(self.moves) % 2
        if len(self.moves) >= 2:
            self.moves[-2].wait()
        s.held[slot] = total
        target = (s.grad_inner, s.grad_outer)[q % 2].at[q // 2]
        self.moves.append(pltpu.make_async_copy(s.held.at[slot], target, s.local_sem.at[3 + slot]))
        self.moves[-1].start()

    def close(self):
        for move in self.moves[-2:]:
            move.wait()


def norm_back(values, gain, d_normed):
    inverse = lax.rsqrt(jnp.mean(values * values, axis=-1, keepdims=True) + EPSILON)
    scaled = d_normed * gain
    inner = jnp.mean(scaled * values, axis=-1, keepdims=True)
    grad = inverse * scaled - values * (inverse * inverse * inverse * inner)
    return grad, jnp.sum(d_normed * values * inverse, axis=0, keepdims=True)


def gate_parts(normed_rows, router, route):
    logits = nt(normed_rows, router)
    raised = jnp.exp(logits - jnp.max(logits, axis=1, keepdims=True))
    probs = raised / jnp.sum(raised, axis=1, keepdims=True)
    chosen = jnp.where(route == iota(logits.shape, 1), 1.0, 0.0)
    return probs, chosen, jnp.sum(probs * chosen, axis=1, keepdims=True)


def expert_dense(e, w, s, route_ref):
    model = s.x_rows.shape[1]

    @pl.loop(0, s.x_rows.shape[0] // ROWS)
    def _(t):
        at = pl.ds(pl.multiple_of(t * ROWS, ROWS), ROWS)
        here = route_ref[at, 0:1] == e
        inner = nn(s.x_rows[at], w[0])
        cubic = 0.044715 * inner * inner
        tanh = jnp.tanh(math.sqrt(2.0 / math.pi) * inner * (1.0 + cubic))
        half = 0.5 * (1.0 + tanh)
        active = jnp.where(here, inner * half, 0.0).astype(BF)
        slope = half + (0.5 * math.sqrt(2.0 / math.pi)) * inner * (1.0 - tanh * tanh) * (
            1.0 + 3.0 * cubic
        )
        d_inner = jnp.where(here, nn(s.d_rows[at], w[1]) * slope, 0.0).astype(BF)
        s.active[at] = active
        s.d_inner[at] = d_inner
        out = nt(active, w[1]).astype(BF)
        d_x = nt(d_inner, w[0]).astype(BF)
        if e == 0:
            s.terms[at, :model] = out
            s.terms[at, model:] = d_x
        else:
            s.terms[at, :model] = jnp.where(here, out, s.terms[at, :model])
            s.terms[at, model:] = jnp.where(here, d_x, s.terms[at, model:])


def layer_kernel(heads, names, *refs):
    s = Names()
    for name, ref in zip(names, refs):
        setattr(s, name, ref)
    h = Here()
    width = heads * HD
    seq, model = s.attn_rows.shape
    rows = s.tokens.shape[0]
    half = rows // 2
    shard = s.wq.shape[0]
    wire = Wire(s.t_send, s.t_recv)
    split = model // 2
    sources = [s.attn_shard.at[0]]
    for e in range(E):
        sources += [s.w_in.at[e], s.w_out.at[e]]
    sources += [s.attn_shard.at[1]]

    def target(p, at):
        if p in (0, LAST):
            return s.w_attn.at[at, pl.ds(split if p else 0, split)]
        return s.experts.at[p - 1, at]

    weights = Weights(h, Wire(s.w_send, s.w_recv), s.own_sem, sources, target)
    reduce = Reduce(
        h, Wire(s.g_send, s.g_recv), s.local_sem, s.mine, s.other, s.y_land, s.e_land, s.z_land,
        s.e_stage,
    )
    results = Results(s, reduce, width)
    row_id = iota((8, model), 0)

    def block(part):
        return pl.ds(pl.multiple_of(h.t * rows + part * half, 16), half)

    def span(part):
        return slice(part * half, (part + 1) * half)

    def norm_rows(part):
        s.attn_rows[block(part)] = normed(s.tokens[span(part)], gain_a).astype(BF)

    def fill_first():
        segments = s.segments[...]
        first = jnp.zeros(segments.shape, jnp.int32)
        for seg in range(1, 5):
            first = jnp.where(segments >= seg, jnp.sum(jnp.where(segments < seg, 1, 0)), first)
        s.first[...] = jnp.broadcast_to(first, s.first.shape)

    def norm_attended(part, total, gather):
        attended = s.tokens[span(part)] + total.total()
        s.grad_tokens[span(part)] = attended
        s.x_rows[block(part)] = normed(attended, gain_f).astype(BF)
        gather.start()

    def load_weights(e):
        copies = []
        for side in range(2):
            copies.append(
                pltpu.make_async_copy(
                    s.experts.at[2 * e + side], s.w_buf.at[side], s.local_sem.at[1 + side]
                )
            )
            copies[-1].start()
        for copy in copies:
            copy.wait()

    def run_expert(e):
        expert_dense(e, s.w_buf, s, s.route_col)
        s.acc[:, :model] = nn(s.x_t[...], s.d_inner[...])
        reduce.store(2 * e, s.acc, shard)
        s.acc[:, :model] = nn(s.d_t[...], s.active[...])
        reduce.store(2 * e + 1, s.acc, shard)

    def expert_back(part, total, gather):
        router_rows = s.router[...].astype(F32)
        attended, cot = s.grad_tokens[span(part)], s.cot[span(part)]
        expert_out, d_normed = total[:, :model], total[:, model:]
        ffn = normed(attended, gain_f).astype(BF)
        route = s.route_col[block(part), 0:1]
        probs, chosen, gate = gate_parts(ffn, s.router[...], route)
        s.output[span(part)] = attended + gate * expert_out
        d_gate = jnp.sum(cot * expert_out, axis=1, keepdims=True)
        d_logits = d_gate * gate * (chosen - probs)
        small = s.small[...]
        for e in range(E):
            d_normed = d_normed + d_logits[:, e : e + 1] * router_rows[e : e + 1]
            grad = jnp.sum(d_logits[:, e : e + 1] * ffn.astype(F32), axis=0, keepdims=True)
            small = small + jnp.where(row_id == 2 + e, grad, 0.0)
        back, gain_grad = norm_back(attended, gain_f, d_normed)
        s.small[...] = small + jnp.where(row_id == 1, gain_grad, 0.0)
        d_attended = cot + back
        s.grad_tokens[span(part)] = d_attended
        s.x_rows[block(part)] = d_attended.astype(BF)
        gather.start()

    def keep_lines():
        flat = jnp.concatenate(diagonal_lines(heads, s.near), axis=1)
        places = jnp.concatenate([flat, flat], axis=1)
        lane = iota((8, model), 1) // flat.shape[1]
        mine = (row_id == 6 + h.t // 2) & (lane == h.t % 2)
        s.small[...] += jnp.where(mine, places, 0.0)

    def first_norm_back(part, total):
        back, gain_grad = norm_back(s.tokens[span(part)], gain_a, total)
        s.grad_tokens[span(part)] += back
        s.small[...] += jnp.where(row_id == 0, gain_grad, 0.0)

    s.attn_shard[0, :, :width] = s.wq[...]
    s.attn_shard[0, :, width:] = s.wk[...]
    s.attn_shard[1, :, :width] = s.wv[...]
    s.attn_shard[1, :, width:] = jnp.transpose(s.wo[...])
    h.greet()
    weights.start(0)

    gathers = [Rows(h, wire, s.attn_rows, rows, part, 2) for part in range(2)]
    gain_a = s.gain_a[...].astype(F32).reshape(1, model)
    norm_rows(0)
    gathers[0].start()
    weights.start(LAST)
    weights.start(2)
    norm_rows(1)
    gathers[1].start()
    s.d_rows[pl.ds(pl.multiple_of(h.t * rows, 16), rows)] = s.cot[...].astype(BF)
    s.tab[...] = s.table[...].astype(F32)
    fill_bias(s.bias, s.far, [s.tab[pl.ds(h.t * heads + hd, 1), :] for hd in range(heads)])
    s.route_col[...] = jnp.transpose(
        jnp.broadcast_to(s.routes[...].astype(F32), (8, seq))
    ).astype(jnp.int32)
    fill_first()
    weights.pairs(LAST)
    weights.forward(0)
    gathers[0].forward()
    weights.start(6)
    gathers[1].forward()
    weights.start(1)
    gathers[0].finish()
    gathers[1].finish()
    weights.start(7)
    weights.start(3)
    weights.forward(2)
    cots = Rows(h, wire, s.d_rows, rows, 0, 1)
    cots.start()
    weights.finish(0)
    weights.forward(LAST)
    weights.finish(LAST)

    project(heads, s.attn_rows[...], s.w_attn, s.qkv, s.q_t, s.v_t, s.kn)
    state = (s.first, s.q_t, s.v_t, s.kn, s.bias, s.far, s.acc, s.ctx_t, s.lse)
    weights.start(4)
    attend_blocks(heads, *state, range(0, 3))
    attend_blocks(heads, *state, range(3, seq // QT))
    s.ctx[...] = jnp.transpose(s.ctx_t[...])
    s.branch[...] = nt(s.ctx[...], s.w_attn[:, 3 * width :]).astype(BF)
    narrow = [s.landed.at[:, :, :, :model], s.out.at[:, :, :model], s.back.at[:, :, :model]]
    sums = [Sums(h, wire, s.branch, *narrow, rows, part, 2) for part in range(2)]
    sums[0].start()
    sums[1].start()
    weights.forward(6)
    sums[0].cross()
    weights.start(8)
    sums[1].cross()
    weights.forward(1)
    cots.forward()

    gathers = [Rows(h, wire, s.x_rows, rows, part, 2) for part in range(2)]
    gain_f = s.gain_f[...].astype(F32).reshape(1, model)
    norm_attended(0, sums[0], gathers[0])
    weights.pairs(7)
    norm_attended(1, sums[1], gathers[1])
    weights.forward(4)
    gathers[0].forward()
    gathers[1].forward()
    weights.forward(3)
    cots.finish()
    gathers[0].finish()
    gathers[1].finish()
    weights.start(5)
    wire.settle()
    gate = gate_parts(s.x_rows[...], s.router[...], s.route_col[:, 0:1])[2]
    s.d_rows[...] = (s.d_rows[...].astype(F32) * gate).astype(BF)
    s.x_t[...] = jnp.transpose(s.x_rows[...])
    s.d_t[...] = jnp.transpose(s.d_rows[...])

    weights.finish(1)
    weights.finish(2)
    load_weights(0)
    run_expert(0)
    weights.pairs(8)
    weights.forward(5)
    weights.finish(3)
    weights.finish(4)
    load_weights(1)
    run_expert(1)
    reduce.start(2)
    weights.forward(7)
    weights.finish(5)
    weights.finish(6)
    load_weights(2)
    run_expert(2)
    reduce.start(0)
    weights.finish(7)
    weights.forward(8)
    weights.finish(8)
    load_weights(3)
    run_expert(3)
    reduce.start(4)

    s.small[...] = jnp.zeros_like(s.small)
    sums = [
        Sums(h, wire, s.terms, s.landed, s.out, s.back, rows, part, 2) for part in range(2)
    ]
    sums[0].start()
    sums[1].start()
    reduce.arrive(2)
    sums[0].cross()
    sums[1].cross()
    reduce.arrive(4)
    reduce.start(6)
    gathers = [Rows(h, wire, s.x_rows, rows, part, 2) for part in range(2)]
    expert_back(0, sums[0].total(), gathers[0])
    reduce.relay(2)
    reduce.arrive(0)
    reduce.start(1)
    expert_back(1, sums[1].total(), gathers[1])
    reduce.arrive(6)
    gathers[0].forward()
    reduce.relay(4)
    gathers[1].forward()
    gathers[0].finish()
    gathers[1].finish()
    results.put(4)

    scale = jnp.asarray(1.0 / math.sqrt(HD), BF)
    d_ctx = nn(s.x_rows[...], s.w_attn[:, 3 * width :]).astype(BF)
    d_ctx_t = jnp.transpose(d_ctx)
    s.dc_t[...] = d_ctx_t
    s.k_t[...] = jnp.transpose(s.qkv[:, width : 2 * width])
    product = d_ctx_t.astype(F32) * s.ctx_t[...].astype(F32)
    for hd in range(heads):
        band = slice(hd * HD, (hd + 1) * HD)
        s.qn[hd] = s.qkv[:, band] * scale
        s.vn[hd] = s.qkv[:, 2 * width + hd * HD : 2 * width + (hd + 1) * HD]
        s.dcn[hd] = d_ctx[:, band]
        s.delta[hd : hd + 1] = jnp.sum(product[band], axis=0, keepdims=True)
    s.dq_t[...] = jnp.zeros_like(s.dq_t)
    s.near[...] = jnp.zeros_like(s.near)
    attend_back_block(heads, s, 0, seq)
    reduce.arrive(1)
    for j in range(1, seq // QT):
        attend_back_block(heads, s, j, seq)
    wire.settle()
    s.dqkv[:, :width] = jnp.transpose((s.dq_t[...] * (1.0 / math.sqrt(HD))).astype(BF))
    s.branch[...] = nt(s.dqkv[...], s.w_attn[:, : 3 * width]).astype(BF)
    reduce.relay(0)
    sums = [Sums(h, wire, s.branch, *narrow, rows, part, 2) for part in range(2)]
    sums[0].start()
    sums[1].start()
    reduce.start(3)
    s.acc[:, : 3 * width] = tn(s.attn_rows[...], s.dqkv[...])
    s.acc[:, 3 * width : model] = tn(s.x_rows[...], s.ctx[...])
    reduce.store(2 * E, s.acc, shard)
    reduce.relay(1)
    sums[0].cross()
    reduce.start(8)
    sums[1].cross()
    reduce.relay(6)
    keep_lines()
    reduce.start(7)

    first_norm_back(0, sums[0].total())
    first_norm_back(1, sums[1].total())
    reduce.arrive(3)
    everywhere = SmallSum(h, wire, s.small, s.small_land)
    results.put(1)
    reduce.start(5)
    reduce.relay(Z_FIRST[8])
    everywhere.start(0)
    reduce.arrive(7)
    reduce.relay(8)
    reduce.arrive(5)
    reduce.relay(3)
    everywhere.finish(0)
    reduce.cross(8)
    results.put(0)
    reduce.relay(7)
    reduce.relay(5)
    everywhere.start(1)
    everywhere.finish(1)
    results.put(2)
    results.put(3)
    results.put(8)
    everywhere.start(2)
    everywhere.finish(2)
    results.put(6)
    everywhere.start(3)
    results.put(7)
    results.put(5)
    everywhere.finish(3)
    results.close()
    wire.settle()
    weights.close()
    reduce.close()


def layer(table, tokens, cot, segments, routes, gain_a, gain_f, router, wq, wk, wv, wo, w_in, w_out):
    rows, model = tokens.shape
    seq = segments.shape[1]
    shard, width = wq.shape
    heads = width // HD
    hidden = w_in.shape[2]
    vmem = pl.BlockSpec(memory_space=pltpu.VMEM)
    hbm = pl.BlockSpec(memory_space=pl.ANY)
    ins = [
        ("table", table, vmem), ("tokens", tokens, vmem), ("cot", cot, vmem),
        ("segments", segments, vmem), ("routes", routes, vmem), ("gain_a", gain_a, vmem),
        ("gain_f", gain_f, vmem), ("router", router, vmem), ("wq", wq, vmem), ("wk", wk, vmem),
        ("wv", wv, vmem), ("wo", wo, vmem), ("w_in", w_in, hbm), ("w_out", w_out, hbm),
    ]
    outs = [
        ("output", (rows, model), F32, vmem),
        ("grad_tokens", (rows, model), F32, vmem),
        ("grad_q", (shard, width), F32, vmem),
        ("grad_k", (shard, width), F32, vmem),
        ("grad_v", (shard, width), F32, vmem),
        ("grad_o", (width, shard), F32, vmem),
        ("small", (8, model), F32, vmem),
        ("grad_inner", (E, shard, hidden), F32, hbm),
        ("grad_outer", (E, shard, hidden), F32, hbm),
        ("experts", (2 * E, model, hidden), BF, hbm),
        ("e_land", (LEGS, 2, shard, model), BF, hbm),
    ]
    scratch = [
        ("attn_shard", (2, shard, 2 * width), BF),
        ("attn_rows", (seq, model), BF),
        ("qkv", (seq, 3 * width), BF),
        ("ctx", (seq, width), BF),
        ("lse", (8, seq), F32),
        ("delta", (8, seq), F32),
        ("w_attn", (model, 4 * width), BF),
        ("first", (8, seq), jnp.int32),
        ("x_rows", (seq, model), BF),
        ("d_rows", (seq, model), BF),
        ("x_t", (model, seq), BF),
        ("d_t", (model, seq), BF),
        ("active", (seq, hidden), BF),
        ("d_inner", (seq, hidden), BF),
        ("terms", (seq, 2 * model), BF),
        ("w_buf", (2, model, hidden), BF),
        ("acc", (heads * QT, seq), F32),
        ("q_t", (width, seq), BF),
        ("k_t", (width, seq), BF),
        ("v_t", (width, seq), BF),
        ("dc_t", (width, seq), BF),
        ("ctx_t", (width, seq), BF),
        ("kn", (heads, seq, HD), BF),
        ("vn", (heads, seq, HD), BF),
        ("qn", (heads, seq, HD), BF),
        ("dcn", (heads, seq, HD), BF),
        ("bias", (heads, 2, HALF, HALF), F32),
        ("far", (8, QT), F32),
        ("tab", table.shape, F32),
        ("route_col", (seq, 8), jnp.int32),
        ("near", (heads, 2, HALF, HALF), F32),
        ("dq_t", (width, seq), F32),
        ("dqkv", (seq, 3 * width), BF),
        ("branch", (seq, model), BF),
        ("landed", (2, 2, rows // 2, 2 * model), BF),
        ("out", (2, rows // 2, 2 * model), BF),
        ("back", (2, rows // 2, 2 * model), BF),
        ("mine", (2 * E + 1, 4, shard, model), BF),
        ("other", (2 * E + 1, 4, shard, model), BF),
        ("y_land", (2 * E + 1, 4, shard, model), BF),
        ("z_land", (LEGS, 2, shard, model), BF),
        ("e_stage", (2, shard, model), BF),
        ("held", (2, shard, hidden), F32),
        ("small_land", (10, 8, model), F32),
    ]
    sems = [
        ("t_send", T_SEMS), ("t_recv", T_SEMS), ("w_send", W_SEMS), ("w_recv", W_SEMS),
        ("g_send", G_SEMS), ("g_recv", G_SEMS), ("own_sem", PIECES), ("local_sem", 5),
    ]
    names = [i[0] for i in ins] + [o[0] for o in outs] + [c[0] for c in scratch]
    names += [c[0] for c in sems]
    return pl.pallas_call(
        functools.partial(layer_kernel, heads, names),
        out_shape=tuple(jax.ShapeDtypeStruct(o[1], o[2]) for o in outs),
        in_specs=[i[2] for i in ins],
        out_specs=tuple(o[3] for o in outs),
        scratch_shapes=[pltpu.VMEM(c[1], c[2]) for c in scratch]
        + [pltpu.SemaphoreType.DMA((c[1],)) for c in sems],
        compiler_params=pltpu.CompilerParams(
            vmem_limit_bytes=VMEM_MAX, collective_id=1, has_side_effects=True
        ),
        cost_estimate=pl.CostEstimate(flops=4 * 10**10, bytes_accessed=10**8, transcendentals=10**7),
        name="layer",
    )(*[i[1] for i in ins])


def rms_apply(values, gain_vec):
    inverse = lax.rsqrt(jnp.mean(values * values, axis=-1, keepdims=True) + EPSILON)
    return values * inverse * gain_vec


def finish_kernel(heads_all, copies, *refs):
    small = refs[0]
    srcs, outs = refs[1 : 1 + copies], refs[1 + copies : 1 + 2 * copies]
    gain_a, gain_f, router, table = refs[1 + 2 * copies : 5 + 2 * copies]
    held, sem = refs[5 + 2 * copies : -1], refs[-1]
    loads = [pltpu.make_async_copy(a, v, sem.at[0, k]) for k, (a, v) in enumerate(zip(srcs, held))]
    moves = [pltpu.make_async_copy(v, b, sem.at[1, k]) for k, (v, b) in enumerate(zip(held, outs))]
    for load in loads:
        load.start()
    model = small.shape[1]
    gain_a[...] = small[0:1].reshape(model)
    gain_f[...] = small[1:2].reshape(model)
    router[...] = small[2 : 2 + E]
    per_row = model // HALF
    lines = [
        small[6 + k // per_row : 7 + k // per_row, (k % per_row) * HALF : (k % per_row + 1) * HALF]
        for k in range(heads_all)
    ]
    distance, bucket = iota((HALF, NBKT), 0), iota((HALF, NBKT), 1)
    pick = jnp.zeros((HALF, NBKT), F32)
    for b in range(NBKT - 1):
        inside = (distance >= FIRST[b]) & (distance < FIRST[b + 1]) & (bucket == b)
        pick = jnp.where(inside, 1.0, pick)
    pick = jnp.where((distance < NEAR) & (bucket == NBKT - 1), -1.0, pick)
    table[...] = lax.dot_general(
        jnp.concatenate(lines, axis=0), pick, (((1,), (0,)), ((), ())),
        precision=lax.Precision.HIGHEST, preferred_element_type=F32,
    )
    for load, move in zip(loads, moves):
        load.wait()
        move.start()
    for move in moves:
        move.wait()


def finish(small, arrays, heads_all):
    model = small.shape[1]
    vmem = pl.BlockSpec(memory_space=pltpu.VMEM)
    hbm = pl.BlockSpec(memory_space=pl.ANY)
    n = len(arrays)
    return pl.pallas_call(
        functools.partial(finish_kernel, heads_all, n),
        out_shape=tuple(jax.ShapeDtypeStruct(a.shape, a.dtype) for a in arrays)
        + (
            jax.ShapeDtypeStruct((model,), F32),
            jax.ShapeDtypeStruct((model,), F32),
            jax.ShapeDtypeStruct((E, model), F32),
            jax.ShapeDtypeStruct((heads_all, NBKT), F32),
        ),
        in_specs=[vmem] + [hbm] * n,
        out_specs=(hbm,) * n + (vmem,) * 4,
        scratch_shapes=[pltpu.VMEM(a.shape, a.dtype) for a in arrays]
        + [pltpu.SemaphoreType.DMA((2, n))],
        compiler_params=pltpu.CompilerParams(vmem_limit_bytes=VMEM_MAX),
        cost_estimate=pl.CostEstimate(flops=10**6, bytes_accessed=10**7, transcendentals=0),
        name="finish",
    )(small, *arrays)


def table_grad(diag):
    onehot = jnp.asarray((BUCKETS[:HALF, None] == np.arange(NBKT - 1)[None, :]).astype(np.float32))
    near_sums = jnp.dot(onehot.T, diag.T, precision=lax.Precision.HIGHEST)
    return jnp.concatenate([near_sums, -jnp.sum(near_sums, axis=0, keepdims=True)], axis=0)


def per_device_grid(
    tokens, segments, routes, cotangent, gain_attn, w_query, w_key, w_value, w_output, rel_table,
    gain_ffn, w_router, w_inner, w_outer,
):
    out = layer(
        jnp.transpose(rel_table), tokens, cotangent, segments[None, :], jnp.transpose(routes),
        gain_attn, gain_ffn, jnp.transpose(w_router), w_query, w_key, w_value, w_output, w_inner,
        jnp.transpose(w_outer, (0, 2, 1)),
    )
    small = out[6]
    done = finish(small, [*out[:6], out[7], out[8]], rel_table.shape[1])
    output, grad_tokens, grad_q, grad_k, grad_v, grad_o, grad_inner, grad_outer = done[:8]
    gain_a, gain_f, grad_router, grad_table = done[8:]
    return (
        output, grad_tokens, gain_a, grad_q, grad_k, grad_v, grad_o, jnp.transpose(grad_table),
        gain_f, jnp.transpose(grad_router), grad_inner, jnp.transpose(grad_outer, (0, 2, 1)),
    )


def per_device(
    tokens, segments, routes, cotangent, gain_attn, w_query, w_key, w_value, w_output, rel_table,
    gain_ffn, w_router, w_inner, w_outer,
):
    part_index = lax.axis_index("tensor")
    rows_local, model = tokens.shape
    seq_len = segments.shape[0]
    width = w_query.shape[1]
    heads = width // HD
    all_heads = rel_table.shape[1]
    hidden = w_inner.shape[2]

    attn_shard = jnp.concatenate([w_query, w_key, w_value, jnp.transpose(w_output)], axis=1)
    w_attn = gather_dp(attn_shard)
    both_shard = jnp.concatenate([w_inner, jnp.transpose(w_outer, (0, 2, 1))], axis=2)
    w_experts = [gather_dp(both_shard[e]) for e in range(E)]
    offs = jnp.zeros((1,), jnp.int32)
    slot_row, slot_col, plan = make_plan(jnp.reshape(routes, (1, seq_len)))
    counts = [jnp.sum((segments < s).astype(jnp.int32)) for s in range(1, 5)]
    first_key = jnp.zeros_like(segments)
    for s in range(1, 5):
        first_key = jnp.where(segments >= s, counts[s - 1], first_key)
    first_key = first_key[None, :]
    table = jnp.transpose(
        lax.dynamic_slice_in_dim(rel_table.astype(F32), part_index * heads, heads, 1)
    )

    normed_attn, norm_one_pull = jax.vjp(rms_apply, tokens, gain_attn.astype(F32))
    attn_rows = lax.all_gather(normed_attn.astype(BF), "tensor", axis=0, tiled=True)
    qkv, ctx, lse, branch = attend(attn_rows, w_attn, table, first_key, heads)
    attended = tokens + lax.psum_scatter(
        branch, "tensor", scatter_dimension=0, tiled=True
    ).astype(F32)

    normed_ffn, norm_two_pull = jax.vjp(rms_apply, attended, gain_ffn.astype(F32))
    ffn_in = normed_ffn.astype(BF)
    local_routes = lax.dynamic_slice_in_dim(routes[:, 0], part_index * rows_local, rows_local, 0)
    route_mask = (local_routes[:, None] == jnp.arange(E, dtype=jnp.int32)[None, :]).astype(F32)

    def gate_of(normed_values, router_values):
        logits = jnp.dot(normed_values, router_values, precision=lax.Precision.HIGHEST)
        return jnp.sum(jax.nn.softmax(logits, axis=-1) * route_mask, axis=-1)

    gate_weight, gate_pull = jax.vjp(gate_of, ffn_in.astype(F32), w_router.astype(F32))
    d_expert = (cotangent * gate_weight[:, None]).astype(BF)
    xd = lax.all_gather(jnp.concatenate([ffn_in, d_expert], axis=1), "tensor", axis=0, tiled=True)

    terms = None
    expert_sums = []
    for e in range(E):
        terms, part = expert(e, plan, offs, xd, slot_row, slot_col, terms, w_experts[e])
        expert_sums.append(reduce_dp(part[0]))
    sums = lax.psum_scatter(terms, "tensor", scatter_dimension=0, tiled=True).astype(F32)
    expert_out, d_ffn_local = sums[:, :model], sums[:, model:]
    output = attended + gate_weight[:, None] * expert_out
    d_gate = jnp.sum(cotangent * expert_out, axis=-1)

    d_ffn_router, grad_router_local = gate_pull(d_gate)
    d_attended_norm, grad_gain_two = norm_two_pull(d_ffn_local + d_ffn_router)
    d_attended = cotangent + d_attended_norm
    d_branch_rows = lax.all_gather(d_attended.astype(BF), "tensor", axis=0, tiled=True)

    total_rows, diag, attn_part = attend_back(
        d_branch_rows, w_attn, qkv, ctx, lse, first_key, attn_rows, table, offs, heads
    )
    attn_sum = reduce_dp(attn_part[0])
    d_attn_local = lax.psum_scatter(
        total_rows, "tensor", scatter_dimension=0, tiled=True
    ).astype(F32)
    d_tokens_norm, grad_gain_one = norm_one_pull(d_attn_local)
    grad_tokens = d_attended + d_tokens_norm
    grad_table_full = lax.dynamic_update_slice_in_dim(
        jnp.zeros((NBKT, all_heads), F32), table_grad(diag[:heads]), part_index * heads, 1
    )
    small_sums = lax.psum(
        (grad_gain_one, grad_gain_two, grad_router_local, grad_table_full), ("dp", "tensor")
    )
    return (
        output,
        grad_tokens,
        small_sums[0],
        attn_sum[:, :width],
        attn_sum[:, width : 2 * width],
        attn_sum[:, 2 * width : 3 * width],
        jnp.transpose(attn_sum[:, 3 * width :]),
        small_sums[3],
        small_sums[1],
        small_sums[2],
        jnp.stack([part[:, :hidden] for part in expert_sums]),
        jnp.stack([jnp.transpose(part[:, hidden:]) for part in expert_sums]),
    )


def solution(mesh):
    sizes = dict(mesh.shape)
    in_specs = (
        P(("dp", "tensor"), None),
        P("dp"),
        P("dp", None),
        P(("dp", "tensor"), None),
        P(),
        P("dp", "tensor"),
        P("dp", "tensor"),
        P("dp", "tensor"),
        P("tensor", "dp"),
        P(),
        P(),
        P(),
        P(None, "dp", "tensor"),
        P(None, "tensor", "dp"),
    )
    out_specs = (
        P(("dp", "tensor"), None),
        P(("dp", "tensor"), None),
        P(),
        P("dp", "tensor"),
        P("dp", "tensor"),
        P("dp", "tensor"),
        P("tensor", "dp"),
        P(),
        P(),
        P(),
        P(None, "dp", "tensor"),
        P(None, "tensor", "dp"),
    )
    return jax.shard_map(
        per_device_grid if sizes["dp"] == 8 and sizes["tensor"] == 4 else per_device,
        mesh=mesh,
        in_specs=in_specs,
        out_specs=out_specs,
        check_vma=False,
    )
```

```python
import functools
import math

import jax
import jax.numpy as jnp
import numpy as np
from jax import lax
from jax.experimental import pallas as pl
from jax.experimental.pallas import tpu as pltpu
from jax.sharding import PartitionSpec as P

HD = 64
NBKT = 32
MAXD = 128
E = 4
WIN = 1024
QT = 256
HALF = 128
ROWS = 256

EPSILON = 1e-06
NEG_LARGE = -1e30
BF = jnp.bfloat16
F32 = jnp.float32
VMEM_MAX = 65000 * 1024


def bucket_numbers(window, buckets, far_distance):
    distance = np.arange(window)
    exact_part = buckets // 2
    safe_distance = np.maximum(distance, 1) * 1.0
    log_part = exact_part + np.floor(
        np.log(safe_distance / exact_part)
        / np.log(far_distance / exact_part)
        * (buckets - exact_part)
    ).astype(np.int32)
    log_part = np.minimum(log_part, buckets - 1)
    return np.where(distance < exact_part, distance, log_part).astype(np.int32)


BUCKETS = bucket_numbers(WIN, NBKT, MAXD)
FIRST = [int(np.argmax(BUCKETS == b)) for b in range(NBKT)]
NEAR = FIRST[NBKT - 1]


def nn(a, b):
    return lax.dot_general(a, b, (((1,), (0,)), ((), ())), preferred_element_type=F32)


def nt(a, b):
    return lax.dot_general(a, b, (((1,), (1,)), ((), ())), preferred_element_type=F32)


def tn(a, b):
    return lax.dot_general(a, b, (((0,), (0,)), ((), ())), preferred_element_type=F32)


class Names:
    pass


def iota(shape, dim):
    return lax.broadcasted_iota(jnp.int32, shape, dim)


def gather_dp(shard):
    return lax.all_gather(shard, "dp", axis=0, tiled=True)


def reduce_dp(part):
    return lax.psum_scatter(part, "dp", scatter_dimension=0, tiled=True).astype(F32)


def plan_kernel(route_ref, slot_row_ref, slot_col_ref, plan_ref):
    length = route_ref.shape[1]
    route = route_ref[...]
    chosen = jnp.where(iota((8, length), 0) == route, 1.0, 0.0).astype(F32)
    upper = jnp.where(iota((length, length), 0) < iota((length, length), 1), 1.0, 0.0)
    before = nn(chosen.astype(BF), upper.astype(BF))
    rank = jnp.sum(chosen * before, axis=0, keepdims=True)
    start = jnp.int32(0)
    base = jnp.zeros((1, length), F32)
    for e in range(E):
        here = route == e
        count = jnp.sum(jnp.where(here, 1, 0))
        tiles = (count + (ROWS - 1)) // ROWS
        plan_ref[e] = tiles
        plan_ref[E + e] = start
        base = base + jnp.where(here, start.astype(F32), 0.0)
        start = start + tiles * ROWS
    slots = jnp.broadcast_to(rank + base, (8, length))
    slot_row_ref[...] = slots.astype(jnp.int32)
    slot_col_ref[...] = jnp.transpose(slots).astype(jnp.int32)


def make_plan(route_row):
    length = route_row.shape[1]
    return pl.pallas_call(
        plan_kernel,
        out_shape=(
            jax.ShapeDtypeStruct((8, length), jnp.int32),
            jax.ShapeDtypeStruct((length, 8), jnp.int32),
            jax.ShapeDtypeStruct((2 * E,), jnp.int32),
        ),
        in_specs=[pl.BlockSpec(memory_space=pltpu.VMEM)],
        out_specs=(
            pl.BlockSpec(memory_space=pltpu.VMEM),
            pl.BlockSpec(memory_space=pltpu.VMEM),
            pl.BlockSpec(memory_space=pltpu.SMEM),
        ),
        compiler_params=pltpu.CompilerParams(vmem_limit_bytes=VMEM_MAX),
        name="route_plan",
    )(route_row)


def fill_bias(bias_ref, far_ref, table_rows):
    step = iota((HALF, HALF), 1) - iota((HALF, HALF), 0)
    for h, row in enumerate(table_rows):
        far_ref[h : h + 1] = jnp.broadcast_to(row[:, NBKT - 1 :], (1, far_ref.shape[1]))
    for side in range(2):
        distance = step + side * HALF
        tiles = [jnp.broadcast_to(row[:, NBKT - 1 :], (HALF, HALF)) for row in table_rows]
        for b in reversed(range(NBKT - 1)):
            below = distance < FIRST[b + 1]
            for h, row in enumerate(table_rows):
                tiles[h] = jnp.where(below, row[:, b : b + 1], tiles[h])
        for h, tile in enumerate(tiles):
            bias_ref[h, side] = tile


def biased_scores(raw, gap, h, bias_ref, far_ref, first_key, key_start):
    far = far_ref[h : h + 1]
    keys = key_start + iota((QT, QT), 0)
    if gap >= 2:
        return jnp.where(keys >= first_key, raw + far, NEG_LARGE)
    diag, near = bias_ref[h, 0], bias_ref[h, 1]
    const = jnp.broadcast_to(far[:, :HALF], (HALF, HALF))
    if gap == 1:
        tile = jnp.concatenate(
            [
                jnp.concatenate([const, const], axis=1),
                jnp.concatenate([near, const], axis=1),
            ],
            axis=0,
        )
        return jnp.where(keys >= first_key, raw + tile, NEG_LARGE)
    tile = jnp.concatenate(
        [jnp.concatenate([diag, near], axis=1), jnp.concatenate([const, diag], axis=1)], axis=0
    )
    causal = iota((QT, QT), 0) <= iota((QT, QT), 1)
    return jnp.where((keys >= first_key) & causal, raw + tile, NEG_LARGE)


def attend_blocks(heads, first_ref, q_t, v_t, kn, bias_ref, far_ref, s_ref, ctx_t, lse_ref, blocks):
    for i in blocks:
        cols = slice(i * QT, (i + 1) * QT)
        first_key = first_ref[0:1, cols]
        for h in range(heads):
            band = slice(h * HD, (h + 1) * HD)
            q_blk = q_t[band, cols]
            peak = None
            for j in range(i + 1):
                raw = nn(kn[h, j * QT : (j + 1) * QT], q_blk)
                s = biased_scores(raw, i - j, h, bias_ref, far_ref, first_key, j * QT)
                s_ref[h * QT : (h + 1) * QT, j * QT : (j + 1) * QT] = s
                top = jnp.max(s, axis=0, keepdims=True)
                peak = top if peak is None else jnp.maximum(peak, top)
            total = jnp.zeros((1, QT), F32)
            acc = jnp.zeros((HD, QT), F32)
            for j in range(i + 1):
                p = jnp.exp(s_ref[h * QT : (h + 1) * QT, j * QT : (j + 1) * QT] - peak)
                total = total + jnp.sum(p, axis=0, keepdims=True)
                acc = acc + nn(v_t[band, j * QT : (j + 1) * QT], p.astype(BF))
            ctx_t[band, cols] = (acc / total).astype(BF)
            lse_ref[h : h + 1, cols] = peak + jnp.log(total)


def project(heads, x, w_ref, qkv_ref, q_t, v_t, kn):
    width = heads * HD
    qkv = nn(x, w_ref[:, : 3 * width]).astype(BF)
    qkv_ref[...] = qkv
    q_t[...] = jnp.transpose(qkv[:, :width]) * jnp.asarray(1.0 / math.sqrt(HD), BF)
    v_t[...] = jnp.transpose(qkv[:, 2 * width :])
    for h in range(heads):
        kn[h] = qkv[:, width + h * HD : width + (h + 1) * HD]


def attend_kernel(heads, table_ref, x_ref, first_ref, w_ref, *refs):
    qkv_ref, ctx_ref, lse_ref, branch_ref, q_t, v_t, kn, bias_ref, far_ref, s_ref, ctx_t = refs
    width = heads * HD
    seq = x_ref.shape[0]
    fill_bias(bias_ref, far_ref, [table_ref[hd : hd + 1, :] for hd in range(heads)])
    project(heads, x_ref[...], w_ref, qkv_ref, q_t, v_t, kn)
    blocks = range(seq // QT)
    attend_blocks(
        heads, first_ref, q_t, v_t, kn, bias_ref, far_ref, s_ref, ctx_t, lse_ref, blocks
    )
    ctx = jnp.transpose(ctx_t[...])
    ctx_ref[...] = ctx
    branch_ref[...] = nt(ctx, w_ref[:, 3 * width :]).astype(BF)


def attend(x, w, table, first_key, heads):
    seq, model = x.shape
    width = heads * HD
    vmem = pl.BlockSpec(memory_space=pltpu.VMEM)
    return pl.pallas_call(
        functools.partial(attend_kernel, heads),
        out_shape=(
            jax.ShapeDtypeStruct((seq, 3 * width), BF),
            jax.ShapeDtypeStruct((seq, width), BF),
            jax.ShapeDtypeStruct((8, seq), F32),
            jax.ShapeDtypeStruct((seq, model), BF),
        ),
        in_specs=[vmem] * 4,
        out_specs=(vmem,) * 4,
        scratch_shapes=[
            pltpu.VMEM((width, seq), BF),
            pltpu.VMEM((width, seq), BF),
            pltpu.VMEM((heads, seq, HD), BF),
            pltpu.VMEM((heads, 2, HALF, HALF), F32),
            pltpu.VMEM((8, QT), F32),
            pltpu.VMEM((heads * QT, seq), F32),
            pltpu.VMEM((width, seq), BF),
        ],
        compiler_params=pltpu.CompilerParams(vmem_limit_bytes=VMEM_MAX),
        cost_estimate=pl.CostEstimate(flops=4 * 10**9, bytes_accessed=10**7, transcendentals=2 * 10**6),
        name="attend",
    )(table, x, first_key, w)


def attend_back_block(heads, s, j, seq):
    width = heads * HD
    keys = slice(j * QT, (j + 1) * QT)
    for h in range(heads):
        band = slice(h * HD, (h + 1) * HD)
        dk = jnp.zeros((QT, HD), F32)
        dv = jnp.zeros((QT, HD), F32)
        for i in range(j, seq // QT):
            cols = slice(i * QT, (i + 1) * QT)
            raw = nn(s.kn[h, keys], s.q_t[band, cols])
            scores = biased_scores(raw, i - j, h, s.bias, s.far, s.first[0:1, cols], j * QT)
            p = jnp.exp(scores - s.lse[h : h + 1, cols])
            dp = nn(s.vn[h, keys], s.dc_t[band, cols])
            ds = p * (dp - s.delta[h : h + 1, cols])
            if i == j:
                s.near[h, 0] += ds[:HALF, :HALF] + ds[HALF:, HALF:]
                s.near[h, 1] += ds[:HALF, HALF:]
            elif i == j + 1:
                s.near[h, 1] += ds[HALF:, :HALF]
            ds = ds.astype(BF)
            dv = dv + nn(p.astype(BF), s.dcn[h, cols])
            dk = dk + nn(ds, s.qn[h, cols])
            s.dq_t[band, cols] += nn(s.k_t[band, keys], ds)
        s.dqkv[keys, width + h * HD : width + (h + 1) * HD] = dk.astype(BF)
        s.dqkv[keys, 2 * width + h * HD : 2 * width + (h + 1) * HD] = dv.astype(BF)


def diagonal_lines(heads, near):
    key, query = iota((HALF, HALF), 0), iota((HALF, HALF), 1)
    lines = []
    for h in range(heads):
        both = near[h, 0] + jnp.where(query < key, near[h, 1], 0.0)
        for bit in range(7):
            turned = pltpu.roll(both, HALF - (1 << bit), 1)
            both = jnp.where((key >> bit) & 1 == 1, turned, both)
        lines.append(jnp.sum(both, axis=0, keepdims=True))
    return lines


def attend_back_kernel(heads, blocks, names, *refs):
    s = Names()
    for name, ref in zip(names, refs):
        setattr(s, name, ref)
    grads = refs[len(names) :]
    width = heads * HD
    seq = s.d.shape[0]
    scale = jnp.asarray(1.0 / math.sqrt(HD), BF)
    fill_bias(s.bias, s.far, [s.tab[hd : hd + 1, :] for hd in range(heads)])
    d_rows = s.d[...]
    ctx = s.ctx[...]
    dc = nn(d_rows, s.w[:, 3 * width :]).astype(BF)
    s.acc[:, 3 * width :] = tn(d_rows, ctx)
    dct = jnp.transpose(dc)
    s.dc_t[...] = dct
    qkv = s.qkv[...]
    s.q_t[...] = jnp.transpose(qkv[:, :width]) * scale
    s.k_t[...] = jnp.transpose(qkv[:, width : 2 * width])
    product = dct.astype(F32) * jnp.transpose(ctx).astype(F32)
    for h in range(heads):
        band = slice(h * HD, (h + 1) * HD)
        s.qn[h] = qkv[:, band] * scale
        s.kn[h] = qkv[:, width + h * HD : width + (h + 1) * HD]
        s.vn[h] = qkv[:, 2 * width + h * HD : 2 * width + (h + 1) * HD]
        s.dcn[h] = dc[:, band]
        s.delta[h : h + 1] = jnp.sum(product[band], axis=0, keepdims=True)
    s.dq_t[...] = jnp.zeros_like(s.dq_t)
    s.near[...] = jnp.zeros_like(s.near)
    for j in range(seq // QT):
        attend_back_block(heads, s, j, seq)
    s.dqkv[:, :width] = jnp.transpose((s.dq_t[...] * (1.0 / math.sqrt(HD))).astype(BF))
    d_qkv = s.dqkv[...]
    s.rows[...] = nt(d_qkv, s.w[:, : 3 * width]).astype(BF)
    s.acc[:, : 3 * width] = tn(s.x[...], d_qkv)
    scatter_rows(s.acc, s.offs, grads, blocks)
    lines = diagonal_lines(heads, s.near) + [jnp.zeros((8 - heads, HALF), F32)]
    s.diag[...] = jnp.concatenate(lines, axis=0)


def scatter_rows(acc_ref, offs_ref, outs, blocks):
    k = 0
    for out, count in zip(outs, blocks):
        rows = out.shape[1]
        for b in range(count):
            at = pl.ds(pl.multiple_of(offs_ref[k], rows), rows)
            out[b] = acc_ref[at, :].astype(BF)
            k += 1


def attend_back(d_rows, w, qkv, ctx, lse, first_key, x, table, offs, heads):
    seq, model = x.shape
    width = heads * HD
    vmem = pl.BlockSpec(memory_space=pltpu.VMEM)
    smem = pl.BlockSpec(memory_space=pltpu.SMEM)
    scratch = [
        ("q_t", (width, seq), BF),
        ("k_t", (width, seq), BF),
        ("dc_t", (width, seq), BF),
        ("kn", (heads, seq, HD), BF),
        ("vn", (heads, seq, HD), BF),
        ("qn", (heads, seq, HD), BF),
        ("dcn", (heads, seq, HD), BF),
        ("bias", (heads, 2, HALF, HALF), F32),
        ("far", (8, QT), F32),
        ("dq_t", (width, seq), F32),
        ("dqkv", (seq, 3 * width), BF),
        ("near", (heads, 2, HALF, HALF), F32),
        ("delta", (8, seq), F32),
        ("acc", (model, 4 * width), F32),
    ]
    ins = ["offs", "tab", "d", "w", "qkv", "ctx", "lse", "first", "x"]
    names = ins + ["rows", "diag", "grads"] + [c[0] for c in scratch]

    def kernel(*refs):
        at = len(ins) + 2
        plain = refs[:at] + refs[at + 1 :]
        attend_back_kernel(
            heads, (1,), names[:at] + names[at + 1 :], *plain, refs[at]
        )

    out = pl.pallas_call(
        kernel,
        out_shape=(
            jax.ShapeDtypeStruct((seq, model), BF),
            jax.ShapeDtypeStruct((8, HALF), F32),
            jax.ShapeDtypeStruct((1, model, 4 * width), BF),
        ),
        in_specs=[smem] + [vmem] * 8,
        out_specs=(vmem,) * 3,
        scratch_shapes=[pltpu.VMEM(c[1], c[2]) for c in scratch],
        compiler_params=pltpu.CompilerParams(vmem_limit_bytes=VMEM_MAX),
        cost_estimate=pl.CostEstimate(flops=10**10, bytes_accessed=10**7, transcendentals=2 * 10**6),
        name="attend_back",
    )(offs, table, d_rows, w, qkv, ctx, lse, first_key, x)
    return out[0], out[1], out[2]


def expert_kernel(e, plan_ref, offs_ref, xd_ref, row_ref, col_ref, w_ref, *refs):
    terms_in = refs[0] if e > 0 else None
    terms_ref, grad, acc_ref = refs[-3:]
    model = xd_ref.shape[1] // 2
    hidden = w_ref.shape[1] // 2
    length = xd_ref.shape[0]
    terms_ref[...] = jnp.zeros_like(terms_ref) if terms_in is None else terms_in[...]
    acc_ref[...] = jnp.zeros_like(acc_ref)
    base = plan_ref[E + e]

    @pl.loop(0, plan_ref[e])
    def _(t):
        start = base + t * ROWS
        pick = jnp.where(row_ref[0:1, :] == start + iota((ROWS, length), 0), 1.0, 0.0).astype(BF)
        xd = nn(pick, xd_ref[...]).astype(BF)
        x, d = xd[:, :model], xd[:, model:]
        inner = nn(x, w_ref[:, :hidden])
        cubic = 0.044715 * inner * inner
        tanh = jnp.tanh(math.sqrt(2.0 / math.pi) * inner * (1.0 + cubic))
        half = 0.5 * (1.0 + tanh)
        active = (inner * half).astype(BF)
        slope = half + (0.5 * math.sqrt(2.0 / math.pi)) * inner * (1.0 - tanh * tanh) * (1.0 + 3.0 * cubic)
        out = nt(active, w_ref[:, hidden:]).astype(BF)
        d_inner = (nn(d, w_ref[:, hidden:]) * slope).astype(BF)
        acc_ref[:, :hidden] += tn(x, d_inner)
        acc_ref[:, hidden:] += tn(d, active)
        d_x = nt(d_inner, w_ref[:, :hidden]).astype(BF)
        place = jnp.where(col_ref[:, 0:1] == start + iota((length, ROWS), 1), 1.0, 0.0).astype(BF)
        terms_ref[:, :model] = (terms_ref[:, :model].astype(F32) + nn(place, out)).astype(BF)
        terms_ref[:, model:] = (terms_ref[:, model:].astype(F32) + nn(place, d_x)).astype(BF)

    scatter_rows(acc_ref, offs_ref, [grad], (1,))


def expert(e, plan, offs, xd, slot_row, slot_col, terms, w):
    length, both = xd.shape
    model, hidden2 = w.shape
    vmem = pl.BlockSpec(memory_space=pltpu.VMEM)
    smem = pl.BlockSpec(memory_space=pltpu.SMEM)
    extra = [] if terms is None else [terms]
    return pl.pallas_call(
        functools.partial(expert_kernel, e),
        out_shape=(
            jax.ShapeDtypeStruct((length, both), BF),
            jax.ShapeDtypeStruct((1, model, hidden2), BF),
        ),
        in_specs=[smem] * 2 + [vmem] * (4 + len(extra)),
        out_specs=(vmem,) * 2,
        scratch_shapes=[pltpu.VMEM((model, hidden2), F32)],
        compiler_params=pltpu.CompilerParams(vmem_limit_bytes=VMEM_MAX),
        cost_estimate=pl.CostEstimate(flops=3 * 10**9, bytes_accessed=10**7, transcendentals=10**6),
        name=f"expert_{e}",
    )(plan, offs, xd, slot_row, slot_col, w, *extra)


MESH = pl.DeviceIdType.MESH
PIECES = 2 + 2 * E
LAST = PIECES - 1
T_SEMS = 48
W_SEMS = 9 * PIECES
Y_FIRST = (8, LAST,)
Z_FIRST = {0: 9, 1: 10, 3: 11}
LEGS = 2 * E + 1 + len(Z_FIRST)
G_SEMS = 6 * LEGS


class Here:
    def __init__(self):
        self.d = lax.axis_index("dp")
        self.t = lax.axis_index("tensor")
        self.z, self.y = self.d // 2, self.d % 2
        self.x, self.c = self.t // 2, self.t % 2
        self.core = {"dp": self.d, "tensor": 2 * self.x + 1 - self.c}
        self.side = {"dp": self.d, "tensor": 2 * (1 - self.x) + self.c}
        self.over = {"dp": 2 * self.z + 1 - self.y, "tensor": self.t}

        self.low = self.z // 2
        self.middle = (self.z == 1) | (self.z == 2)
        self.pair_z = self.z + 1 - 2 * (self.z % 2)
        self.mid_z = 2 - self.low
        self.end_z = 3 - 3 * self.low
        self.order = [self.z, self.pair_z, self.mid_z, self.end_z]
        self.pair, self.far_mid, self.far_end = (self.at_z(z) for z in self.order[1:])

    def at_z(self, z):
        return {"dp": 2 * z + self.y, "tensor": self.t}

    def greet(self):
        barrier = pltpu.get_barrier_semaphore()
        peers = [self.core, self.side, self.over, self.pair, self.far_mid, self.far_end]
        for peer in peers:
            pl.semaphore_signal(barrier, inc=1, device_id=peer, device_id_type=MESH)
        pl.semaphore_wait(barrier, len(peers))


class Wire:
    def __init__(self, send, recv):
        self.send, self.recv, self.sent, self.count = send, recv, [], 0

    def take(self, number):
        self.count += number
        return self.count - number

    def plan(self, src, dst, peer, send, recv):
        return pltpu.make_async_remote_copy(
            src_ref=src, dst_ref=dst, send_sem=self.send.at[send], recv_sem=self.recv.at[recv],
            device_id=peer, device_id_type=MESH,
        )

    def __call__(self, src, dst, peer):
        k = self.take(1)
        copy = self.plan(src, dst, peer, k, k)
        copy.start()
        self.sent.append(copy)
        return copy

    def settle(self):
        for copy in self.sent:
            copy.wait_send()
        self.sent = []


class Rows:
    def __init__(self, here, wire, buf, rows, part, parts):
        self.here, self.wire, self.buf = here, wire, buf
        self.rows, self.size = rows, rows // parts
        self.shift = part * self.size

    def at(self, t):
        return self.buf.at[pl.ds(pl.multiple_of(t * self.rows + self.shift, 16), self.size)]

    def start(self):
        mine = self.at(self.here.t)
        self.far = self.wire(mine, mine, self.here.side)
        self.near = self.wire(mine, mine, self.here.core)

    def forward(self):
        self.far.wait_recv()
        theirs = self.at(2 * (1 - self.here.x) + self.here.c)
        self.last = self.wire(theirs, theirs, self.here.core)

    def finish(self):
        self.near.wait_recv()
        self.last.wait_recv()


class Sums:
    def __init__(self, here, wire, src, landed, out, back, rows, part, parts):
        self.here, self.wire, self.src = here, wire, src
        self.landed, self.out, self.back = landed, out, back
        self.rows, self.size = rows, rows // parts
        self.shift = part * self.size
        self.part = part

    def at(self, t):
        return pl.ds(pl.multiple_of(t * self.rows + self.shift, 16), self.size)

    def start(self):
        h = self.here
        self.copies = []
        for slot, x in ((0, 1 - h.x), (1, h.x)):
            src = self.src.at[self.at(2 * x + 1 - h.c)]
            self.copies.append(self.wire(src, self.landed.at[slot, self.part], h.core))

    def cross(self):
        h = self.here
        self.copies[0].wait_recv()
        mine = self.src[self.at(2 * (1 - h.x) + h.c)].astype(F32)
        self.out[self.part] = (mine + self.landed[0, self.part].astype(F32)).astype(BF)
        self.last = self.wire(self.out.at[self.part], self.back.at[self.part], h.side)

    def total(self):
        h = self.here
        self.copies[1].wait_recv()
        near = self.src[self.at(2 * h.x + h.c)].astype(F32) + self.landed[1, self.part].astype(F32)
        self.last.wait_recv()
        return near + self.back[self.part].astype(F32)


class Weights:
    def __init__(self, here, wire, own_sem, sources, target):
        self.here, self.wire, self.own_sem = here, wire, own_sem
        self.sources, self.target = sources, target
        self.over, self.own, self.z, self.far = {}, {}, {}, {}

    def at(self, p, z):
        rows = self.sources[p].shape[0]
        if p in Y_FIRST:
            return self.target(p, pl.ds(pl.multiple_of(2 * z * rows, 16), 2 * rows))
        return self.target(p, pl.ds(pl.multiple_of((2 * z + self.here.y) * rows, 16), rows))

    def start(self, p):
        h, src = self.here, self.sources[p]
        rows = src.shape[0]
        dst = self.target(p, pl.ds(pl.multiple_of(h.d * rows, 16), rows))
        self.own[p] = pltpu.make_async_copy(src, dst, self.own_sem.at[p])
        self.own[p].start()
        if p not in Y_FIRST:
            self.spread(p, src)
        self.over[p] = [self.wire(src, dst, h.over)]

    def pairs(self, p):
        self.over[p][0].wait_recv()
        self.own[p].wait()
        self.spread(p, self.at(p, self.here.z))

    def spread(self, p, src):
        h, wire = self.here, self.wire
        dst = self.at(p, h.z)
        k = wire.take(5)
        end = jnp.where(h.middle, 0, 1)
        near = wire.plan(src, dst, h.pair, k, k)
        far = wire.plan(src, dst, h.far_mid, k + 1, k + 1 + end)
        near.start()
        far.start()
        relays = []
        for j, z in ((1, h.mid_z), (2, h.end_z)):
            block = self.at(p, z)
            relays.append(wire.plan(block, block, h.pair, k + 2 + j, k + j))
        self.z[p] = [near] + relays
        self.far[p] = far

    def forward(self, p):
        h = self.here
        near, *relays = self.z[p]
        for copy, z in zip(self.z[p], h.order[1:]):
            copy.wait_recv()
            if copy is not near:
                pl.when(h.middle)(copy.start)
            if p not in Y_FIRST:
                block = self.at(p, z)
                self.over[p].append(self.wire(block, block, h.over))

    def finish(self, p):
        if p in Y_FIRST:
            return
        for copy in self.over[p]:
            copy.wait_recv()
        self.own[p].wait()

    def release(self, p):
        for copy in [self.z[p][0], self.far[p]] + self.over[p]:
            copy.wait_send()
        for copy in self.z[p][1:]:
            pl.when(self.here.middle)(copy.wait_send)


def normed(values, gain):
    inverse = lax.rsqrt(jnp.mean(values * values, axis=-1, keepdims=True) + EPSILON)
    return values * inverse * gain


class Reduce:
    def __init__(self, here, wire, freed, mine, other, y_land, e_land, z_land):
        self.here, self.wire = here, wire
        self.freed, self.last_mine, self.last_other = freed, mine, other
        self.y_land, self.e_land, self.z_land = y_land, e_land, z_land
        self.y, self.legs = {}, {}

    def mine(self, q, k, count=1):
        return self.part(q, k, count, 0)

    def other(self, q, k, count=1):
        return self.part(q, k, count, 4)

    def part(self, q, k, count, side):
        rows = self.freed.shape[1] // 8
        if q == 2 * E:
            ref = self.last_other if side else self.last_mine
            return ref.at[pl.ds(k * rows, count * rows)]
        return self.freed.at[q, pl.ds((side + k) * rows, count * rows)]

    def store(self, q, acc, shard):
        h = self.here
        for k, z in enumerate(h.order):
            for side, target in ((h.y, self.mine(q, k)), (1 - h.y, self.other(q, k))):
                at = pl.ds(pl.multiple_of((2 * z + side) * shard, 16), shard)
                target[...] = acc[at, : target.shape[1]].astype(BF)

    def start(self, q):
        if q in Z_FIRST:
            self.leg(q, [self.mine(q, k) for k in range(4)])
            self.leg(Z_FIRST[q], [self.other(q, k) for k in range(4)])
        else:
            self.y[q] = self.wire(self.other(q, 0, 4), self.y_land.at[q], self.here.over)

    def y_block(self, q, k):
        rows = self.freed.shape[1] // 8
        return self.y_land.at[q, pl.ds(k * rows, rows)]

    def arrive(self, q):
        self.y[q].wait_recv()
        for k in range(4):
            own = self.mine(q, k)
            own[...] = (own[...].astype(F32) + self.y_block(q, k)[...].astype(F32)).astype(BF)
        self.leg(q, [self.mine(q, k) for k in range(4)])

    def leg(self, j, blocks):
        h, wire = self.here, self.wire
        k = wire.take(5)
        near = wire.plan(blocks[1], self.z_land.at[j, 0], h.pair, k, k)
        hand = [
            wire.plan(blocks[2 + i], self.e_land.at[j, i], h.pair, k + 1 + i, k + 2 + i)
            for i in range(2)
        ]
        on = [
            wire.plan(blocks[2 + i], self.z_land.at[j, 1], peer, k + 3 + i, k + 1)
            for i, peer in enumerate((h.far_mid, h.far_end))
        ]

        @pl.when(jnp.logical_not(h.middle))
        def _():
            for copy in hand:
                copy.start()

        near.start()
        self.legs[j] = (blocks, near, hand, on)

    def relay(self, j):
        blocks, _, hand, on = self.legs[j]

        @pl.when(self.here.middle)
        def _():
            for copy in hand:
                copy.wait_recv()
            for i in range(2):
                both = blocks[2 + i][...].astype(F32) + self.e_land[j, i].astype(F32)
                blocks[2 + i][...] = both.astype(BF)
                on[i].start()

    def along_z(self, j):
        blocks, near, _, on = self.legs[j]
        near.wait_recv()
        on[0].wait_recv()
        both = self.z_land[j, 0].astype(F32) + self.z_land[j, 1].astype(F32)
        return blocks[0][...].astype(F32) + both

    def cross(self, q):
        own = self.other(q, 0)
        own[...] = self.along_z(Z_FIRST[q]).astype(BF)
        self.y[q] = self.wire(own, self.y_block(q, 0), self.here.over)

    def total(self, q):
        result = self.along_z(q)
        if q in Z_FIRST:
            self.y[q].wait_recv()
            result = result + self.y_block(q, 0)[...].astype(F32)
        return result

    def close(self):
        self.wire.settle()
        for _, near, hand, on in self.legs.values():
            near.wait_send()
            for copy in on:
                pl.when(self.here.middle)(copy.wait_send)
            for copy in hand:
                pl.when(jnp.logical_not(self.here.middle))(copy.wait_send)


class SmallSum:
    def __init__(self, here, wire, value, land):
        self.here, self.wire, self.value, self.land = here, wire, value, land

    def start(self, step):
        h, wire, land = self.here, self.wire, self.land
        if step < 3:
            peer = (h.core, h.side, h.over)[step]
            land[2 * step] = self.value[...]
            self.copy = wire(land.at[2 * step], land.at[2 * step + 1], peer)
            return
        land[6 + h.z] = self.value[...]
        self.k = wire.take(3)
        own = land.at[6 + h.z]
        for i, peer in enumerate((h.pair, h.far_mid, h.far_end)):
            back = self.k if i == 0 else self.k + 1 + jnp.where(h.middle, 0, 1)
            copy = wire.plan(own, own, peer, self.k + i, back)
            copy.start()
            wire.sent.append(copy)

    def finish(self, step):
        h, land = self.here, self.land
        if step < 3:
            self.copy.wait_recv()
            self.value[...] += land[2 * step + 1]
            return
        own = land.at[6 + h.z]
        for i, z in enumerate(h.order[1:]):
            self.wire.plan(own, land.at[6 + z], h.pair, self.k + i, self.k + i).wait_recv()
        self.value[...] = (land[6] + land[7]) + (land[8] + land[9])


class Results:
    def __init__(self, s, reduce, width):
        self.s, self.reduce, self.width, self.moves = s, reduce, width, []

    def put(self, q):
        s, width = self.s, self.width
        total = self.reduce.total(q)
        if q == 2 * E:
            s.grad_q[...] = total[:, :width]
            s.grad_k[...] = total[:, width : 2 * width]
            s.grad_v[...] = total[:, 2 * width : 3 * width]
            s.grad_o[...] = jnp.transpose(total[:, 3 * width :])
            return
        slot = len(self.moves) % 2
        if len(self.moves) >= 2:
            self.moves[-2].wait()
        s.held[slot] = total
        target = (s.grad_inner, s.grad_outer)[q % 2].at[q // 2]
        self.moves.append(pltpu.make_async_copy(s.held.at[slot], target, s.local_sem.at[slot]))
        self.moves[-1].start()

    def close(self):
        for move in self.moves[-2:]:
            move.wait()


def norm_back(values, gain, d_normed):
    inverse = lax.rsqrt(jnp.mean(values * values, axis=-1, keepdims=True) + EPSILON)
    scaled = d_normed * gain
    inner = jnp.mean(scaled * values, axis=-1, keepdims=True)
    grad = inverse * scaled - values * (inverse * inverse * inverse * inner)
    return grad, jnp.sum(d_normed * values * inverse, axis=0, keepdims=True)


def gate_parts(normed_rows, router, route):
    logits = nt(normed_rows, router)
    raised = jnp.exp(logits - jnp.max(logits, axis=1, keepdims=True))
    probs = raised / jnp.sum(raised, axis=1, keepdims=True)
    chosen = jnp.where(route == iota(logits.shape, 1), 1.0, 0.0)
    return probs, chosen, jnp.sum(probs * chosen, axis=1, keepdims=True)


def expert_dense(e, w, s, route_ref):
    model = s.x_rows.shape[1]

    @pl.loop(0, s.x_rows.shape[0] // ROWS)
    def _(t):
        at = pl.ds(pl.multiple_of(t * ROWS, ROWS), ROWS)
        here = route_ref[at, 0:1] == e
        inner = nn(s.x_rows[at], w[0][...])
        cubic = 0.044715 * inner * inner
        tanh = jnp.tanh(math.sqrt(2.0 / math.pi) * inner * (1.0 + cubic))
        half = 0.5 * (1.0 + tanh)
        active = jnp.where(here, inner * half, 0.0).astype(BF)
        slope = half + (0.5 * math.sqrt(2.0 / math.pi)) * inner * (1.0 - tanh * tanh) * (
            1.0 + 3.0 * cubic
        )
        d_inner = jnp.where(here, nn(s.d_rows[at], w[1][...]) * slope, 0.0).astype(BF)
        s.active[at] = active
        s.d_inner[at] = d_inner
        out = nt(active, w[1][...]).astype(BF)
        d_x = nt(d_inner, w[0][...]).astype(BF)
        if e == 0:
            s.terms[at, :model] = out
            s.terms[at, model:] = d_x
        else:
            s.terms[at, :model] = jnp.where(here, out, s.terms[at, :model])
            s.terms[at, model:] = jnp.where(here, d_x, s.terms[at, model:])


def layer_kernel(heads, names, *refs):
    s = Names()
    for name, ref in zip(names, refs):
        setattr(s, name, ref)
    h = Here()
    width = heads * HD
    seq, model = s.attn_rows.shape
    rows = s.tokens.shape[0]
    half = rows // 2
    shard = s.wq.shape[0]
    wire = Wire(s.t_send, s.t_recv)
    split = model // 2
    sources = [s.attn_shard.at[0]]
    for e in range(E):
        sources += [s.w_in.at[e], s.w_out.at[e]]
    sources += [s.attn_shard.at[1]]

    def target(p, at):
        if p in (0, LAST):
            return s.w_attn.at[at, pl.ds(split if p else 0, split)]
        return s.experts.at[p - 1, at]

    weights = Weights(h, Wire(s.w_send, s.w_recv), s.own_sem, sources, target)
    reduce = Reduce(
        h, Wire(s.g_send, s.g_recv), s.experts, s.mine, s.other, s.y_land, s.e_land, s.z_land,
    )
    results = Results(s, reduce, width)
    row_id = iota((8, model), 0)

    def block(part):
        return pl.ds(pl.multiple_of(h.t * rows + part * half, 16), half)

    def span(part):
        return slice(part * half, (part + 1) * half)

    def norm_rows(part):
        s.attn_rows[block(part)] = normed(s.tokens[span(part)], gain_a).astype(BF)

    def fill_first():
        segments = s.segments[...]
        first = jnp.zeros(segments.shape, jnp.int32)
        for seg in range(1, 5):
            first = jnp.where(segments >= seg, jnp.sum(jnp.where(segments < seg, 1, 0)), first)
        s.first[...] = jnp.broadcast_to(first, s.first.shape)

    def norm_attended(part, total, gather):
        attended = s.tokens[span(part)] + total.total()
        s.grad_tokens[span(part)] = attended
        s.x_rows[block(part)] = normed(attended, gain_f).astype(BF)
        gather.start()

    def run_expert(e):
        expert_dense(e, (s.experts.at[2 * e], s.experts.at[2 * e + 1]), s, s.route_col)
        weights.release(2 * e + 1)
        weights.release(2 * e + 2)
        s.acc[:, :model] = nn(s.x_t[...], s.d_inner[...])
        reduce.store(2 * e, s.acc, shard)
        s.acc[:, :model] = nn(s.d_t[...], s.active[...])
        reduce.store(2 * e + 1, s.acc, shard)

    def expert_back(part, total, gather):
        router_rows = s.router[...].astype(F32)
        attended, cot = s.grad_tokens[span(part)], s.cot[span(part)]
        expert_out, d_normed = total[:, :model], total[:, model:]
        ffn = normed(attended, gain_f).astype(BF)
        route = s.route_col[block(part), 0:1]
        probs, chosen, gate = gate_parts(ffn, s.router[...], route)
        s.output[span(part)] = attended + gate * expert_out
        d_gate = jnp.sum(cot * expert_out, axis=1, keepdims=True)
        d_logits = d_gate * gate * (chosen - probs)
        small = s.small[...]
        for e in range(E):
            d_normed = d_normed + d_logits[:, e : e + 1] * router_rows[e : e + 1]
            grad = jnp.sum(d_logits[:, e : e + 1] * ffn.astype(F32), axis=0, keepdims=True)
            small = small + jnp.where(row_id == 2 + e, grad, 0.0)
        back, gain_grad = norm_back(attended, gain_f, d_normed)
        s.small[...] = small + jnp.where(row_id == 1, gain_grad, 0.0)
        d_attended = cot + back
        s.grad_tokens[span(part)] = d_attended
        s.x_rows[block(part)] = d_attended.astype(BF)
        gather.start()

    def keep_lines():
        flat = jnp.concatenate(diagonal_lines(heads, s.near), axis=1)
        places = jnp.concatenate([flat, flat], axis=1)
        lane = iota((8, model), 1) // flat.shape[1]
        mine = (row_id == 6 + h.t // 2) & (lane == h.t % 2)
        s.small[...] += jnp.where(mine, places, 0.0)

    def first_norm_back(part, total):
        back, gain_grad = norm_back(s.tokens[span(part)], gain_a, total)
        s.grad_tokens[span(part)] += back
        s.small[...] += jnp.where(row_id == 0, gain_grad, 0.0)

    s.attn_shard[0, :, :width] = s.wq[...]
    s.attn_shard[0, :, width:] = s.wk[...]
    s.attn_shard[1, :, :width] = s.wv[...]
    s.attn_shard[1, :, width:] = jnp.transpose(s.wo[...])
    h.greet()

    gathers = [Rows(h, wire, s.attn_rows, rows, part, 2) for part in range(2)]
    gain_a = s.gain_a[...].astype(F32).reshape(1, model)
    norm_rows(0)
    weights.start(LAST)
    gathers[0].start()
    norm_rows(1)
    weights.start(0)
    gathers[1].start()
    weights.pairs(LAST)
    s.d_rows[pl.ds(pl.multiple_of(h.t * rows, 16), rows)] = s.cot[...].astype(BF)
    s.tab[...] = s.table[...].astype(F32)
    fill_bias(s.bias, s.far, [s.tab[pl.ds(h.t * heads + hd, 1), :] for hd in range(heads)])
    s.route_col[...] = jnp.transpose(
        jnp.broadcast_to(s.routes[...].astype(F32), (8, seq))
    ).astype(jnp.int32)
    fill_first()
    weights.start(8)
    weights.start(2)
    gathers[0].forward()
    gathers[1].forward()
    weights.start(4)
    gathers[0].finish()
    gathers[1].finish()
    weights.start(1)
    cots = Rows(h, wire, s.d_rows, rows, 0, 1)
    cots.start()
    weights.forward(0)
    weights.forward(LAST)
    weights.finish(0)
    weights.finish(LAST)

    project(heads, s.attn_rows[...], s.w_attn, s.qkv, s.q_t, s.v_t, s.kn)
    state = (s.first, s.q_t, s.v_t, s.kn, s.bias, s.far, s.acc, s.ctx_t, s.lse)
    weights.start(3)
    attend_blocks(heads, *state, range(0, 3))
    weights.start(6)
    attend_blocks(heads, *state, range(3, seq // QT))
    s.ctx[...] = jnp.transpose(s.ctx_t[...])
    s.branch[...] = nt(s.ctx[...], s.w_attn[:, 3 * width :]).astype(BF)
    narrow = [s.landed.at[:, :, :, :model], s.out.at[:, :, :model], s.back.at[:, :, :model]]
    sums = [Sums(h, wire, s.branch, *narrow, rows, part, 2) for part in range(2)]
    sums[0].start()
    sums[1].start()
    weights.start(5)
    sums[0].cross()
    sums[1].cross()
    weights.forward(2)
    cots.forward()

    gathers = [Rows(h, wire, s.x_rows, rows, part, 2) for part in range(2)]
    gain_f = s.gain_f[...].astype(F32).reshape(1, model)
    norm_attended(0, sums[0], gathers[0])
    weights.forward(1)
    norm_attended(1, sums[1], gathers[1])
    weights.forward(3)
    gathers[0].forward()
    weights.start(7)
    gathers[1].forward()
    cots.finish()
    gathers[0].finish()
    gathers[1].finish()
    weights.forward(4)
    weights.pairs(8)
    wire.settle()
    gate = gate_parts(s.x_rows[...], s.router[...], s.route_col[:, 0:1])[2]
    s.d_rows[...] = (s.d_rows[...].astype(F32) * gate).astype(BF)
    s.x_t[...] = jnp.transpose(s.x_rows[...])
    s.d_t[...] = jnp.transpose(s.d_rows[...])

    weights.finish(1)
    weights.finish(2)
    weights.forward(5)
    run_expert(0)
    weights.forward(7)
    weights.finish(3)
    reduce.start(0)
    weights.finish(4)
    run_expert(1)
    weights.forward(6)
    reduce.start(2)
    weights.forward(8)
    weights.finish(5)
    weights.finish(6)
    run_expert(2)
    reduce.start(3)
    reduce.start(4)
    weights.finish(7)
    weights.finish(8)
    run_expert(3)

    s.small[...] = jnp.zeros_like(s.small)
    sums = [
        Sums(h, wire, s.terms, s.landed, s.out, s.back, rows, part, 2) for part in range(2)
    ]
    sums[0].start()
    sums[1].start()
    reduce.arrive(2)
    reduce.relay(Z_FIRST[0])
    sums[0].cross()
    sums[1].cross()
    reduce.relay(0)
    reduce.start(5)
    reduce.arrive(4)
    gathers = [Rows(h, wire, s.x_rows, rows, part, 2) for part in range(2)]
    expert_back(0, sums[0].total(), gathers[0])
    reduce.start(1)
    reduce.relay(Z_FIRST[3])
    reduce.relay(2)
    reduce.start(6)
    expert_back(1, sums[1].total(), gathers[1])
    reduce.cross(0)
    gathers[0].forward()
    reduce.relay(4)
    gathers[1].forward()
    reduce.relay(3)
    gathers[0].finish()
    gathers[1].finish()
    reduce.arrive(5)

    scale = jnp.asarray(1.0 / math.sqrt(HD), BF)
    d_ctx = nn(s.x_rows[...], s.w_attn[:, 3 * width :]).astype(BF)
    d_ctx_t = jnp.transpose(d_ctx)
    s.dc_t[...] = d_ctx_t
    s.k_t[...] = jnp.transpose(s.qkv[:, width : 2 * width])
    product = d_ctx_t.astype(F32) * s.ctx_t[...].astype(F32)
    for hd in range(heads):
        band = slice(hd * HD, (hd + 1) * HD)
        s.qn[hd] = s.qkv[:, band] * scale
        s.vn[hd] = s.qkv[:, 2 * width + hd * HD : 2 * width + (hd + 1) * HD]
        s.dcn[hd] = d_ctx[:, band]
        s.delta[hd : hd + 1] = jnp.sum(product[band], axis=0, keepdims=True)
    s.dq_t[...] = jnp.zeros_like(s.dq_t)
    s.near[...] = jnp.zeros_like(s.near)
    attend_back_block(heads, s, 0, seq)
    reduce.start(7)
    for j in range(1, seq // QT):
        attend_back_block(heads, s, j, seq)
    wire.settle()
    s.dqkv[:, :width] = jnp.transpose((s.dq_t[...] * (1.0 / math.sqrt(HD))).astype(BF))
    s.branch[...] = nt(s.dqkv[...], s.w_attn[:, : 3 * width]).astype(BF)
    results.put(0)
    sums = [Sums(h, wire, s.branch, *narrow, rows, part, 2) for part in range(2)]
    sums[0].start()
    sums[1].start()
    reduce.relay(1)
    reduce.relay(Z_FIRST[1])
    reduce.arrive(6)
    s.acc[:, : 3 * width] = tn(s.attn_rows[...], s.dqkv[...])
    s.acc[:, 3 * width : model] = tn(s.x_rows[...], s.ctx[...])
    reduce.store(2 * E, s.acc, shard)
    results.put(2)
    reduce.arrive(7)
    sums[0].cross()
    sums[1].cross()
    reduce.start(8)
    reduce.relay(5)
    reduce.relay(6)
    keep_lines()
    reduce.arrive(8)

    first_norm_back(0, sums[0].total())
    reduce.cross(3)
    first_norm_back(1, sums[1].total())
    everywhere = SmallSum(h, wire, s.small, s.small_land)
    everywhere.start(0)
    reduce.relay(7)
    reduce.cross(1)
    everywhere.finish(0)
    everywhere.start(1)
    everywhere.finish(1)
    results.put(5)
    results.put(3)
    everywhere.start(2)
    everywhere.finish(2)
    results.put(1)
    everywhere.start(3)
    reduce.relay(8)
    results.put(4)
    results.put(7)
    results.put(6)
    everywhere.finish(3)
    results.put(8)
    results.close()
    wire.settle()
    weights.release(0)
    weights.release(LAST)
    reduce.close()


def layer(table, tokens, cot, segments, routes, gain_a, gain_f, router, wq, wk, wv, wo, w_in, w_out):
    rows, model = tokens.shape
    seq = segments.shape[1]
    shard, width = wq.shape
    heads = width // HD
    hidden = w_in.shape[2]
    vmem = pl.BlockSpec(memory_space=pltpu.VMEM)
    hbm = pl.BlockSpec(memory_space=pl.ANY)
    ins = [
        ("table", table, vmem), ("tokens", tokens, vmem), ("cot", cot, vmem),
        ("segments", segments, vmem), ("routes", routes, vmem), ("gain_a", gain_a, vmem),
        ("gain_f", gain_f, vmem), ("router", router, vmem), ("wq", wq, vmem), ("wk", wk, vmem),
        ("wv", wv, vmem), ("wo", wo, vmem), ("w_in", w_in, hbm), ("w_out", w_out, hbm),
    ]
    outs = [
        ("output", (rows, model), F32, vmem),
        ("grad_tokens", (rows, model), F32, vmem),
        ("grad_q", (shard, width), F32, vmem),
        ("grad_k", (shard, width), F32, vmem),
        ("grad_v", (shard, width), F32, vmem),
        ("grad_o", (width, shard), F32, vmem),
        ("small", (8, model), F32, vmem),
        ("grad_inner", (E, shard, hidden), F32, hbm),
        ("grad_outer", (E, shard, hidden), F32, hbm),
    ]
    scratch = [
        ("attn_shard", (2, shard, 2 * width), BF),
        ("attn_rows", (seq, model), BF),
        ("qkv", (seq, 3 * width), BF),
        ("ctx", (seq, width), BF),
        ("lse", (8, seq), F32),
        ("delta", (8, seq), F32),
        ("w_attn", (model, 4 * width), BF),
        ("first", (8, seq), jnp.int32),
        ("x_rows", (seq, model), BF),
        ("d_rows", (seq, model), BF),
        ("x_t", (model, seq), BF),
        ("d_t", (model, seq), BF),
        ("active", (seq, hidden), BF),
        ("d_inner", (seq, hidden), BF),
        ("terms", (seq, 2 * model), BF),
        ("experts", (2 * E, model, hidden), BF),
        ("acc", (heads * QT, seq), F32),
        ("q_t", (width, seq), BF),
        ("k_t", (width, seq), BF),
        ("v_t", (width, seq), BF),
        ("dc_t", (width, seq), BF),
        ("ctx_t", (width, seq), BF),
        ("kn", (heads, seq, HD), BF),
        ("vn", (heads, seq, HD), BF),
        ("qn", (heads, seq, HD), BF),
        ("dcn", (heads, seq, HD), BF),
        ("bias", (heads, 2, HALF, HALF), F32),
        ("far", (8, QT), F32),
        ("tab", table.shape, F32),
        ("route_col", (seq, 8), jnp.int32),
        ("near", (heads, 2, HALF, HALF), F32),
        ("dq_t", (width, seq), F32),
        ("dqkv", (seq, 3 * width), BF),
        ("branch", (seq, model), BF),
        ("landed", (2, 2, rows // 2, 2 * model), BF),
        ("out", (2, rows // 2, 2 * model), BF),
        ("back", (2, rows // 2, 2 * model), BF),
        ("mine", (4 * shard, model), BF),
        ("other", (4 * shard, model), BF),
        ("y_land", (2 * E + 1, 4 * shard, model), BF),
        ("z_land", (LEGS, 2, shard, model), BF),
        ("e_land", (LEGS, 2, shard, model), BF),
        ("held", (2, shard, hidden), F32),
        ("small_land", (10, 8, model), F32),
    ]
    sems = [
        ("t_send", T_SEMS), ("t_recv", T_SEMS), ("w_send", W_SEMS), ("w_recv", W_SEMS),
        ("g_send", G_SEMS), ("g_recv", G_SEMS), ("own_sem", PIECES), ("local_sem", 2),
    ]
    names = [i[0] for i in ins] + [o[0] for o in outs] + [c[0] for c in scratch]
    names += [c[0] for c in sems]
    return pl.pallas_call(
        functools.partial(layer_kernel, heads, names),
        out_shape=tuple(jax.ShapeDtypeStruct(o[1], o[2]) for o in outs),
        in_specs=[i[2] for i in ins],
        out_specs=tuple(o[3] for o in outs),
        scratch_shapes=[pltpu.VMEM(c[1], c[2]) for c in scratch]
        + [pltpu.SemaphoreType.DMA((c[1],)) for c in sems],
        compiler_params=pltpu.CompilerParams(
            vmem_limit_bytes=VMEM_MAX, collective_id=1, has_side_effects=True
        ),
        cost_estimate=pl.CostEstimate(flops=4 * 10**10, bytes_accessed=10**8, transcendentals=10**7),
        name="layer",
    )(*[i[1] for i in ins])


def rms_apply(values, gain_vec):
    inverse = lax.rsqrt(jnp.mean(values * values, axis=-1, keepdims=True) + EPSILON)
    return values * inverse * gain_vec


def finish_kernel(heads_all, copies, *refs):
    small = refs[0]
    srcs, outs = refs[1 : 1 + copies], refs[1 + copies : 1 + 2 * copies]
    gain_a, gain_f, router, table = refs[1 + 2 * copies : 5 + 2 * copies]
    held, sem = refs[5 + 2 * copies : -1], refs[-1]
    loads = [pltpu.make_async_copy(a, v, sem.at[0, k]) for k, (a, v) in enumerate(zip(srcs, held))]
    moves = [pltpu.make_async_copy(v, b, sem.at[1, k]) for k, (v, b) in enumerate(zip(held, outs))]
    for load in loads:
        load.start()
    model = small.shape[1]
    gain_a[...] = small[0:1].reshape(model)
    gain_f[...] = small[1:2].reshape(model)
    router[...] = small[2 : 2 + E]
    per_row = model // HALF
    lines = [
        small[6 + k // per_row : 7 + k // per_row, (k % per_row) * HALF : (k % per_row + 1) * HALF]
        for k in range(heads_all)
    ]
    distance, bucket = iota((HALF, NBKT), 0), iota((HALF, NBKT), 1)
    pick = jnp.zeros((HALF, NBKT), F32)
    for b in range(NBKT - 1):
        inside = (distance >= FIRST[b]) & (distance < FIRST[b + 1]) & (bucket == b)
        pick = jnp.where(inside, 1.0, pick)
    pick = jnp.where((distance < NEAR) & (bucket == NBKT - 1), -1.0, pick)
    table[...] = lax.dot_general(
        jnp.concatenate(lines, axis=0), pick, (((1,), (0,)), ((), ())),
        precision=lax.Precision.HIGHEST, preferred_element_type=F32,
    )
    for load, move in zip(loads, moves):
        load.wait()
        move.start()
    for move in moves:
        move.wait()


def finish(small, arrays, heads_all):
    model = small.shape[1]
    vmem = pl.BlockSpec(memory_space=pltpu.VMEM)
    hbm = pl.BlockSpec(memory_space=pl.ANY)
    n = len(arrays)
    return pl.pallas_call(
        functools.partial(finish_kernel, heads_all, n),
        out_shape=tuple(jax.ShapeDtypeStruct(a.shape, a.dtype) for a in arrays)
        + (
            jax.ShapeDtypeStruct((model,), F32),
            jax.ShapeDtypeStruct((model,), F32),
            jax.ShapeDtypeStruct((E, model), F32),
            jax.ShapeDtypeStruct((heads_all, NBKT), F32),
        ),
        in_specs=[vmem] + [hbm] * n,
        out_specs=(hbm,) * n + (vmem,) * 4,
        scratch_shapes=[pltpu.VMEM(a.shape, a.dtype) for a in arrays]
        + [pltpu.SemaphoreType.DMA((2, n))],
        compiler_params=pltpu.CompilerParams(vmem_limit_bytes=VMEM_MAX),
        cost_estimate=pl.CostEstimate(flops=10**6, bytes_accessed=10**7, transcendentals=0),
        name="finish",
    )(small, *arrays)


def table_grad(diag):
    onehot = jnp.asarray((BUCKETS[:HALF, None] == np.arange(NBKT - 1)[None, :]).astype(np.float32))
    near_sums = jnp.dot(onehot.T, diag.T, precision=lax.Precision.HIGHEST)
    return jnp.concatenate([near_sums, -jnp.sum(near_sums, axis=0, keepdims=True)], axis=0)


def per_device_grid(
    tokens, segments, routes, cotangent, gain_attn, w_query, w_key, w_value, w_output, rel_table,
    gain_ffn, w_router, w_inner, w_outer,
):
    out = layer(
        jnp.transpose(rel_table), tokens, cotangent, segments[None, :], jnp.transpose(routes),
        gain_attn, gain_ffn, jnp.transpose(w_router), w_query, w_key, w_value, w_output, w_inner,
        jnp.transpose(w_outer, (0, 2, 1)),
    )
    small = out[6]
    done = finish(small, [*out[:6], out[7], out[8]], rel_table.shape[1])
    output, grad_tokens, grad_q, grad_k, grad_v, grad_o, grad_inner, grad_outer = done[:8]
    gain_a, gain_f, grad_router, grad_table = done[8:]
    return (
        output, grad_tokens, gain_a, grad_q, grad_k, grad_v, grad_o, jnp.transpose(grad_table),
        gain_f, jnp.transpose(grad_router), grad_inner, jnp.transpose(grad_outer, (0, 2, 1)),
    )


def per_device(
    tokens, segments, routes, cotangent, gain_attn, w_query, w_key, w_value, w_output, rel_table,
    gain_ffn, w_router, w_inner, w_outer,
):
    part_index = lax.axis_index("tensor")
    rows_local, model = tokens.shape
    seq_len = segments.shape[0]
    width = w_query.shape[1]
    heads = width // HD
    all_heads = rel_table.shape[1]
    hidden = w_inner.shape[2]

    attn_shard = jnp.concatenate([w_query, w_key, w_value, jnp.transpose(w_output)], axis=1)
    w_attn = gather_dp(attn_shard)
    both_shard = jnp.concatenate([w_inner, jnp.transpose(w_outer, (0, 2, 1))], axis=2)
    w_experts = [gather_dp(both_shard[e]) for e in range(E)]
    offs = jnp.zeros((1,), jnp.int32)
    slot_row, slot_col, plan = make_plan(jnp.reshape(routes, (1, seq_len)))
    counts = [jnp.sum((segments < s).astype(jnp.int32)) for s in range(1, 5)]
    first_key = jnp.zeros_like(segments)
    for s in range(1, 5):
        first_key = jnp.where(segments >= s, counts[s - 1], first_key)
    first_key = first_key[None, :]
    table = jnp.transpose(
        lax.dynamic_slice_in_dim(rel_table.astype(F32), part_index * heads, heads, 1)
    )

    normed_attn, norm_one_pull = jax.vjp(rms_apply, tokens, gain_attn.astype(F32))
    attn_rows = lax.all_gather(normed_attn.astype(BF), "tensor", axis=0, tiled=True)
    qkv, ctx, lse, branch = attend(attn_rows, w_attn, table, first_key, heads)
    attended = tokens + lax.psum_scatter(
        branch, "tensor", scatter_dimension=0, tiled=True
    ).astype(F32)

    normed_ffn, norm_two_pull = jax.vjp(rms_apply, attended, gain_ffn.astype(F32))
    ffn_in = normed_ffn.astype(BF)
    local_routes = lax.dynamic_slice_in_dim(routes[:, 0], part_index * rows_local, rows_local, 0)
    route_mask = (local_routes[:, None] == jnp.arange(E, dtype=jnp.int32)[None, :]).astype(F32)

    def gate_of(normed_values, router_values):
        logits = jnp.dot(normed_values, router_values, precision=lax.Precision.HIGHEST)
        return jnp.sum(jax.nn.softmax(logits, axis=-1) * route_mask, axis=-1)

    gate_weight, gate_pull = jax.vjp(gate_of, ffn_in.astype(F32), w_router.astype(F32))
    d_expert = (cotangent * gate_weight[:, None]).astype(BF)
    xd = lax.all_gather(jnp.concatenate([ffn_in, d_expert], axis=1), "tensor", axis=0, tiled=True)

    terms = None
    expert_sums = []
    for e in range(E):
        terms, part = expert(e, plan, offs, xd, slot_row, slot_col, terms, w_experts[e])
        expert_sums.append(reduce_dp(part[0]))
    sums = lax.psum_scatter(terms, "tensor", scatter_dimension=0, tiled=True).astype(F32)
    expert_out, d_ffn_local = sums[:, :model], sums[:, model:]
    output = attended + gate_weight[:, None] * expert_out
    d_gate = jnp.sum(cotangent * expert_out, axis=-1)

    d_ffn_router, grad_router_local = gate_pull(d_gate)
    d_attended_norm, grad_gain_two = norm_two_pull(d_ffn_local + d_ffn_router)
    d_attended = cotangent + d_attended_norm
    d_branch_rows = lax.all_gather(d_attended.astype(BF), "tensor", axis=0, tiled=True)

    total_rows, diag, attn_part = attend_back(
        d_branch_rows, w_attn, qkv, ctx, lse, first_key, attn_rows, table, offs, heads
    )
    attn_sum = reduce_dp(attn_part[0])
    d_attn_local = lax.psum_scatter(
        total_rows, "tensor", scatter_dimension=0, tiled=True
    ).astype(F32)
    d_tokens_norm, grad_gain_one = norm_one_pull(d_attn_local)
    grad_tokens = d_attended + d_tokens_norm
    grad_table_full = lax.dynamic_update_slice_in_dim(
        jnp.zeros((NBKT, all_heads), F32), table_grad(diag[:heads]), part_index * heads, 1
    )
    small_sums = lax.psum(
        (grad_gain_one, grad_gain_two, grad_router_local, grad_table_full), ("dp", "tensor")
    )
    return (
        output,
        grad_tokens,
        small_sums[0],
        attn_sum[:, :width],
        attn_sum[:, width : 2 * width],
        attn_sum[:, 2 * width : 3 * width],
        jnp.transpose(attn_sum[:, 3 * width :]),
        small_sums[3],
        small_sums[1],
        small_sums[2],
        jnp.stack([part[:, :hidden] for part in expert_sums]),
        jnp.stack([jnp.transpose(part[:, hidden:]) for part in expert_sums]),
    )


def solution(mesh):
    sizes = dict(mesh.shape)
    in_specs = (
        P(("dp", "tensor"), None),
        P("dp"),
        P("dp", None),
        P(("dp", "tensor"), None),
        P(),
        P("dp", "tensor"),
        P("dp", "tensor"),
        P("dp", "tensor"),
        P("tensor", "dp"),
        P(),
        P(),
        P(),
        P(None, "dp", "tensor"),
        P(None, "tensor", "dp"),
    )
    out_specs = (
        P(("dp", "tensor"), None),
        P(("dp", "tensor"), None),
        P(),
        P("dp", "tensor"),
        P("dp", "tensor"),
        P("dp", "tensor"),
        P("tensor", "dp"),
        P(),
        P(),
        P(),
        P(None, "dp", "tensor"),
        P(None, "tensor", "dp"),
    )
    return jax.shard_map(
        per_device_grid if sizes["dp"] == 8 and sizes["tensor"] == 4 else per_device,
        mesh=mesh,
        in_specs=in_specs,
        out_specs=out_specs,
        check_vma=False,
    )
```

```python
import functools
import math

import jax
import jax.numpy as jnp
import numpy as np
from jax import lax
from jax.experimental import pallas as pl
from jax.experimental.pallas import tpu as pltpu
from jax.sharding import PartitionSpec as P

HD = 64
NBKT = 32
MAXD = 128
E = 4
WIN = 1024
QT = 256
HALF = 128
ROWS = 256

EPSILON = 1e-06
NEG_LARGE = -1e30
BF = jnp.bfloat16
F32 = jnp.float32
VMEM_MAX = 65000 * 1024


def bucket_numbers(window, buckets, far_distance):
    distance = np.arange(window)
    exact_part = buckets // 2
    safe_distance = np.maximum(distance, 1) * 1.0
    log_part = exact_part + np.floor(
        np.log(safe_distance / exact_part)
        / np.log(far_distance / exact_part)
        * (buckets - exact_part)
    ).astype(np.int32)
    log_part = np.minimum(log_part, buckets - 1)
    return np.where(distance < exact_part, distance, log_part).astype(np.int32)


BUCKETS = bucket_numbers(WIN, NBKT, MAXD)
FIRST = [int(np.argmax(BUCKETS == b)) for b in range(NBKT)]
NEAR = FIRST[NBKT - 1]


def nn(a, b):
    return lax.dot_general(a, b, (((1,), (0,)), ((), ())), preferred_element_type=F32)


def nt(a, b):
    return lax.dot_general(a, b, (((1,), (1,)), ((), ())), preferred_element_type=F32)


def tn(a, b):
    return lax.dot_general(a, b, (((0,), (0,)), ((), ())), preferred_element_type=F32)


class Names:
    pass


def iota(shape, dim):
    return lax.broadcasted_iota(jnp.int32, shape, dim)


def gather_dp(shard):
    return lax.all_gather(shard, "dp", axis=0, tiled=True)


def reduce_dp(part):
    return lax.psum_scatter(part, "dp", scatter_dimension=0, tiled=True).astype(F32)


def plan_kernel(route_ref, slot_row_ref, slot_col_ref, plan_ref):
    length = route_ref.shape[1]
    route = route_ref[...]
    chosen = jnp.where(iota((8, length), 0) == route, 1.0, 0.0).astype(F32)
    upper = jnp.where(iota((length, length), 0) < iota((length, length), 1), 1.0, 0.0)
    before = nn(chosen.astype(BF), upper.astype(BF))
    rank = jnp.sum(chosen * before, axis=0, keepdims=True)
    start = jnp.int32(0)
    base = jnp.zeros((1, length), F32)
    for e in range(E):
        here = route == e
        count = jnp.sum(jnp.where(here, 1, 0))
        tiles = (count + (ROWS - 1)) // ROWS
        plan_ref[e] = tiles
        plan_ref[E + e] = start
        base = base + jnp.where(here, start.astype(F32), 0.0)
        start = start + tiles * ROWS
    slots = jnp.broadcast_to(rank + base, (8, length))
    slot_row_ref[...] = slots.astype(jnp.int32)
    slot_col_ref[...] = jnp.transpose(slots).astype(jnp.int32)


def make_plan(route_row):
    length = route_row.shape[1]
    return pl.pallas_call(
        plan_kernel,
        out_shape=(
            jax.ShapeDtypeStruct((8, length), jnp.int32),
            jax.ShapeDtypeStruct((length, 8), jnp.int32),
            jax.ShapeDtypeStruct((2 * E,), jnp.int32),
        ),
        in_specs=[pl.BlockSpec(memory_space=pltpu.VMEM)],
        out_specs=(
            pl.BlockSpec(memory_space=pltpu.VMEM),
            pl.BlockSpec(memory_space=pltpu.VMEM),
            pl.BlockSpec(memory_space=pltpu.SMEM),
        ),
        compiler_params=pltpu.CompilerParams(vmem_limit_bytes=VMEM_MAX),
        name="route_plan",
    )(route_row)


def fill_bias(bias_ref, far_ref, table_rows):
    step = iota((HALF, HALF), 1) - iota((HALF, HALF), 0)
    for h, row in enumerate(table_rows):
        far_ref[h : h + 1] = jnp.broadcast_to(row[:, NBKT - 1 :], (1, far_ref.shape[1]))
    for side in range(2):
        distance = step + side * HALF
        tiles = [jnp.broadcast_to(row[:, NBKT - 1 :], (HALF, HALF)) for row in table_rows]
        for b in reversed(range(NBKT - 1)):
            below = distance < FIRST[b + 1]
            for h, row in enumerate(table_rows):
                tiles[h] = jnp.where(below, row[:, b : b + 1], tiles[h])
        for h, tile in enumerate(tiles):
            bias_ref[h, side] = tile


def biased_scores(raw, gap, h, bias_ref, far_ref, first_key, key_start):
    far = far_ref[h : h + 1]
    keys = key_start + iota((QT, QT), 0)
    if gap >= 2:
        return jnp.where(keys >= first_key, raw + far, NEG_LARGE)
    diag, near = bias_ref[h, 0], bias_ref[h, 1]
    const = jnp.broadcast_to(far[:, :HALF], (HALF, HALF))
    if gap == 1:
        tile = jnp.concatenate(
            [
                jnp.concatenate([const, const], axis=1),
                jnp.concatenate([near, const], axis=1),
            ],
            axis=0,
        )
        return jnp.where(keys >= first_key, raw + tile, NEG_LARGE)
    tile = jnp.concatenate(
        [jnp.concatenate([diag, near], axis=1), jnp.concatenate([const, diag], axis=1)], axis=0
    )
    causal = iota((QT, QT), 0) <= iota((QT, QT), 1)
    return jnp.where((keys >= first_key) & causal, raw + tile, NEG_LARGE)


def attend_blocks(heads, first_ref, q_t, v_t, kn, bias_ref, far_ref, s_ref, ctx_t, lse_ref, blocks):
    for i in blocks:
        cols = slice(i * QT, (i + 1) * QT)
        first_key = first_ref[0:1, cols]
        for h in range(heads):
            band = slice(h * HD, (h + 1) * HD)
            q_blk = q_t[band, cols]
            peak = None
            for j in range(i + 1):
                raw = nn(kn[h, j * QT : (j + 1) * QT], q_blk)
                s = biased_scores(raw, i - j, h, bias_ref, far_ref, first_key, j * QT)
                s_ref[h * QT : (h + 1) * QT, j * QT : (j + 1) * QT] = s
                top = jnp.max(s, axis=0, keepdims=True)
                peak = top if peak is None else jnp.maximum(peak, top)
            total = jnp.zeros((1, QT), F32)
            acc = jnp.zeros((HD, QT), F32)
            for j in range(i + 1):
                p = jnp.exp(s_ref[h * QT : (h + 1) * QT, j * QT : (j + 1) * QT] - peak)
                total = total + jnp.sum(p, axis=0, keepdims=True)
                acc = acc + nn(v_t[band, j * QT : (j + 1) * QT], p.astype(BF))
            ctx_t[band, cols] = (acc / total).astype(BF)
            lse_ref[h : h + 1, cols] = peak + jnp.log(total)


def project(heads, x, w_ref, qkv_ref, q_t, v_t, kn):
    width = heads * HD
    qkv = nn(x, w_ref[:, : 3 * width]).astype(BF)
    qkv_ref[...] = qkv
    q_t[...] = jnp.transpose(qkv[:, :width]) * jnp.asarray(1.0 / math.sqrt(HD), BF)
    v_t[...] = jnp.transpose(qkv[:, 2 * width :])
    for h in range(heads):
        kn[h] = qkv[:, width + h * HD : width + (h + 1) * HD]


def attend_kernel(heads, table_ref, x_ref, first_ref, w_ref, *refs):
    qkv_ref, ctx_ref, lse_ref, branch_ref, q_t, v_t, kn, bias_ref, far_ref, s_ref, ctx_t = refs
    width = heads * HD
    seq = x_ref.shape[0]
    fill_bias(bias_ref, far_ref, [table_ref[hd : hd + 1, :] for hd in range(heads)])
    project(heads, x_ref[...], w_ref, qkv_ref, q_t, v_t, kn)
    blocks = range(seq // QT)
    attend_blocks(
        heads, first_ref, q_t, v_t, kn, bias_ref, far_ref, s_ref, ctx_t, lse_ref, blocks
    )
    ctx = jnp.transpose(ctx_t[...])
    ctx_ref[...] = ctx
    branch_ref[...] = nt(ctx, w_ref[:, 3 * width :]).astype(BF)


def attend(x, w, table, first_key, heads):
    seq, model = x.shape
    width = heads * HD
    vmem = pl.BlockSpec(memory_space=pltpu.VMEM)
    return pl.pallas_call(
        functools.partial(attend_kernel, heads),
        out_shape=(
            jax.ShapeDtypeStruct((seq, 3 * width), BF),
            jax.ShapeDtypeStruct((seq, width), BF),
            jax.ShapeDtypeStruct((8, seq), F32),
            jax.ShapeDtypeStruct((seq, model), BF),
        ),
        in_specs=[vmem] * 4,
        out_specs=(vmem,) * 4,
        scratch_shapes=[
            pltpu.VMEM((width, seq), BF),
            pltpu.VMEM((width, seq), BF),
            pltpu.VMEM((heads, seq, HD), BF),
            pltpu.VMEM((heads, 2, HALF, HALF), F32),
            pltpu.VMEM((8, QT), F32),
            pltpu.VMEM((heads * QT, seq), F32),
            pltpu.VMEM((width, seq), BF),
        ],
        compiler_params=pltpu.CompilerParams(vmem_limit_bytes=VMEM_MAX),
        cost_estimate=pl.CostEstimate(flops=4 * 10**9, bytes_accessed=10**7, transcendentals=2 * 10**6),
        name="attend",
    )(table, x, first_key, w)


def attend_back_block(heads, s, j, seq):
    width = heads * HD
    keys = slice(j * QT, (j + 1) * QT)
    for h in range(heads):
        band = slice(h * HD, (h + 1) * HD)
        dk = jnp.zeros((QT, HD), F32)
        dv = jnp.zeros((QT, HD), F32)
        for i in range(j, seq // QT):
            cols = slice(i * QT, (i + 1) * QT)
            raw = nn(s.kn[h, keys], s.q_t[band, cols])
            scores = biased_scores(raw, i - j, h, s.bias, s.far, s.first[0:1, cols], j * QT)
            p = jnp.exp(scores - s.lse[h : h + 1, cols])
            dp = nn(s.vn[h, keys], s.dc_t[band, cols])
            ds = p * (dp - s.delta[h : h + 1, cols])
            if i == j:
                s.near[h, 0] += ds[:HALF, :HALF] + ds[HALF:, HALF:]
                s.near[h, 1] += ds[:HALF, HALF:]
            elif i == j + 1:
                s.near[h, 1] += ds[HALF:, :HALF]
            ds = ds.astype(BF)
            dv = dv + nn(p.astype(BF), s.dcn[h, cols])
            dk = dk + nn(ds, s.qn[h, cols])
            s.dq_t[band, cols] += nn(s.k_t[band, keys], ds)
        s.dqkv[keys, width + h * HD : width + (h + 1) * HD] = dk.astype(BF)
        s.dqkv[keys, 2 * width + h * HD : 2 * width + (h + 1) * HD] = dv.astype(BF)


def diagonal_lines(heads, near):
    key, query = iota((HALF, HALF), 0), iota((HALF, HALF), 1)
    lines = []
    for h in range(heads):
        both = near[h, 0] + jnp.where(query < key, near[h, 1], 0.0)
        for bit in range(7):
            turned = pltpu.roll(both, HALF - (1 << bit), 1)
            both = jnp.where((key >> bit) & 1 == 1, turned, both)
        lines.append(jnp.sum(both, axis=0, keepdims=True))
    return lines


def attend_back_kernel(heads, blocks, names, *refs):
    s = Names()
    for name, ref in zip(names, refs):
        setattr(s, name, ref)
    grads = refs[len(names) :]
    width = heads * HD
    seq = s.d.shape[0]
    scale = jnp.asarray(1.0 / math.sqrt(HD), BF)
    fill_bias(s.bias, s.far, [s.tab[hd : hd + 1, :] for hd in range(heads)])
    d_rows = s.d[...]
    ctx = s.ctx[...]
    dc = nn(d_rows, s.w[:, 3 * width :]).astype(BF)
    s.acc[:, 3 * width :] = tn(d_rows, ctx)
    dct = jnp.transpose(dc)
    s.dc_t[...] = dct
    qkv = s.qkv[...]
    s.q_t[...] = jnp.transpose(qkv[:, :width]) * scale
    s.k_t[...] = jnp.transpose(qkv[:, width : 2 * width])
    product = dct.astype(F32) * jnp.transpose(ctx).astype(F32)
    for h in range(heads):
        band = slice(h * HD, (h + 1) * HD)
        s.qn[h] = qkv[:, band] * scale
        s.kn[h] = qkv[:, width + h * HD : width + (h + 1) * HD]
        s.vn[h] = qkv[:, 2 * width + h * HD : 2 * width + (h + 1) * HD]
        s.dcn[h] = dc[:, band]
        s.delta[h : h + 1] = jnp.sum(product[band], axis=0, keepdims=True)
    s.dq_t[...] = jnp.zeros_like(s.dq_t)
    s.near[...] = jnp.zeros_like(s.near)
    for j in range(seq // QT):
        attend_back_block(heads, s, j, seq)
    s.dqkv[:, :width] = jnp.transpose((s.dq_t[...] * (1.0 / math.sqrt(HD))).astype(BF))
    d_qkv = s.dqkv[...]
    s.rows[...] = nt(d_qkv, s.w[:, : 3 * width]).astype(BF)
    s.acc[:, : 3 * width] = tn(s.x[...], d_qkv)
    scatter_rows(s.acc, s.offs, grads, blocks)
    lines = diagonal_lines(heads, s.near) + [jnp.zeros((8 - heads, HALF), F32)]
    s.diag[...] = jnp.concatenate(lines, axis=0)


def scatter_rows(acc_ref, offs_ref, outs, blocks):
    k = 0
    for out, count in zip(outs, blocks):
        rows = out.shape[1]
        for b in range(count):
            at = pl.ds(pl.multiple_of(offs_ref[k], rows), rows)
            out[b] = acc_ref[at, :].astype(BF)
            k += 1


def attend_back(d_rows, w, qkv, ctx, lse, first_key, x, table, offs, heads):
    seq, model = x.shape
    width = heads * HD
    vmem = pl.BlockSpec(memory_space=pltpu.VMEM)
    smem = pl.BlockSpec(memory_space=pltpu.SMEM)
    scratch = [
        ("q_t", (width, seq), BF),
        ("k_t", (width, seq), BF),
        ("dc_t", (width, seq), BF),
        ("kn", (heads, seq, HD), BF),
        ("vn", (heads, seq, HD), BF),
        ("qn", (heads, seq, HD), BF),
        ("dcn", (heads, seq, HD), BF),
        ("bias", (heads, 2, HALF, HALF), F32),
        ("far", (8, QT), F32),
        ("dq_t", (width, seq), F32),
        ("dqkv", (seq, 3 * width), BF),
        ("near", (heads, 2, HALF, HALF), F32),
        ("delta", (8, seq), F32),
        ("acc", (model, 4 * width), F32),
    ]
    ins = ["offs", "tab", "d", "w", "qkv", "ctx", "lse", "first", "x"]
    names = ins + ["rows", "diag", "grads"] + [c[0] for c in scratch]

    def kernel(*refs):
        at = len(ins) + 2
        plain = refs[:at] + refs[at + 1 :]
        attend_back_kernel(
            heads, (1,), names[:at] + names[at + 1 :], *plain, refs[at]
        )

    out = pl.pallas_call(
        kernel,
        out_shape=(
            jax.ShapeDtypeStruct((seq, model), BF),
            jax.ShapeDtypeStruct((8, HALF), F32),
            jax.ShapeDtypeStruct((1, model, 4 * width), BF),
        ),
        in_specs=[smem] + [vmem] * 8,
        out_specs=(vmem,) * 3,
        scratch_shapes=[pltpu.VMEM(c[1], c[2]) for c in scratch],
        compiler_params=pltpu.CompilerParams(vmem_limit_bytes=VMEM_MAX),
        cost_estimate=pl.CostEstimate(flops=10**10, bytes_accessed=10**7, transcendentals=2 * 10**6),
        name="attend_back",
    )(offs, table, d_rows, w, qkv, ctx, lse, first_key, x)
    return out[0], out[1], out[2]


def expert_kernel(e, plan_ref, offs_ref, xd_ref, row_ref, col_ref, w_ref, *refs):
    terms_in = refs[0] if e > 0 else None
    terms_ref, grad, acc_ref = refs[-3:]
    model = xd_ref.shape[1] // 2
    hidden = w_ref.shape[1] // 2
    length = xd_ref.shape[0]
    terms_ref[...] = jnp.zeros_like(terms_ref) if terms_in is None else terms_in[...]
    acc_ref[...] = jnp.zeros_like(acc_ref)
    base = plan_ref[E + e]

    @pl.loop(0, plan_ref[e])
    def _(t):
        start = base + t * ROWS
        pick = jnp.where(row_ref[0:1, :] == start + iota((ROWS, length), 0), 1.0, 0.0).astype(BF)
        xd = nn(pick, xd_ref[...]).astype(BF)
        x, d = xd[:, :model], xd[:, model:]
        inner = nn(x, w_ref[:, :hidden])
        cubic = 0.044715 * inner * inner
        tanh = jnp.tanh(math.sqrt(2.0 / math.pi) * inner * (1.0 + cubic))
        half = 0.5 * (1.0 + tanh)
        active = (inner * half).astype(BF)
        slope = half + (0.5 * math.sqrt(2.0 / math.pi)) * inner * (1.0 - tanh * tanh) * (1.0 + 3.0 * cubic)
        out = nt(active, w_ref[:, hidden:]).astype(BF)
        d_inner = (nn(d, w_ref[:, hidden:]) * slope).astype(BF)
        acc_ref[:, :hidden] += tn(x, d_inner)
        acc_ref[:, hidden:] += tn(d, active)
        d_x = nt(d_inner, w_ref[:, :hidden]).astype(BF)
        place = jnp.where(col_ref[:, 0:1] == start + iota((length, ROWS), 1), 1.0, 0.0).astype(BF)
        terms_ref[:, :model] = (terms_ref[:, :model].astype(F32) + nn(place, out)).astype(BF)
        terms_ref[:, model:] = (terms_ref[:, model:].astype(F32) + nn(place, d_x)).astype(BF)

    scatter_rows(acc_ref, offs_ref, [grad], (1,))


def expert(e, plan, offs, xd, slot_row, slot_col, terms, w):
    length, both = xd.shape
    model, hidden2 = w.shape
    vmem = pl.BlockSpec(memory_space=pltpu.VMEM)
    smem = pl.BlockSpec(memory_space=pltpu.SMEM)
    extra = [] if terms is None else [terms]
    return pl.pallas_call(
        functools.partial(expert_kernel, e),
        out_shape=(
            jax.ShapeDtypeStruct((length, both), BF),
            jax.ShapeDtypeStruct((1, model, hidden2), BF),
        ),
        in_specs=[smem] * 2 + [vmem] * (4 + len(extra)),
        out_specs=(vmem,) * 2,
        scratch_shapes=[pltpu.VMEM((model, hidden2), F32)],
        compiler_params=pltpu.CompilerParams(vmem_limit_bytes=VMEM_MAX),
        cost_estimate=pl.CostEstimate(flops=3 * 10**9, bytes_accessed=10**7, transcendentals=10**6),
        name=f"expert_{e}",
    )(plan, offs, xd, slot_row, slot_col, w, *extra)


MESH = pl.DeviceIdType.MESH
PIECES = 2 + 2 * E
LAST = PIECES - 1
T_SEMS = 48
W_SEMS = 9 * PIECES
Y_FIRST = (8, LAST,)
Z_FIRST = {0: 9, 1: 10, 3: 11}
LEGS = 2 * E + 1 + len(Z_FIRST)
G_SEMS = 6 * LEGS


class Here:
    def __init__(self):
        self.d = lax.axis_index("dp")
        self.t = lax.axis_index("tensor")
        self.z, self.y = self.d // 2, self.d % 2
        self.x, self.c = self.t // 2, self.t % 2
        self.core = {"dp": self.d, "tensor": 2 * self.x + 1 - self.c}
        self.side = {"dp": self.d, "tensor": 2 * (1 - self.x) + self.c}
        self.over = {"dp": 2 * self.z + 1 - self.y, "tensor": self.t}

        self.low = self.z // 2
        self.middle = (self.z == 1) | (self.z == 2)
        self.pair_z = self.z + 1 - 2 * (self.z % 2)
        self.mid_z = 2 - self.low
        self.end_z = 3 - 3 * self.low
        self.order = [self.z, self.pair_z, self.mid_z, self.end_z]
        self.pair, self.far_mid, self.far_end = (self.at_z(z) for z in self.order[1:])

    def at_z(self, z):
        return {"dp": 2 * z + self.y, "tensor": self.t}

    def greet(self):
        barrier = pltpu.get_barrier_semaphore()
        peers = [self.core, self.side, self.over, self.pair, self.far_mid, self.far_end]
        for peer in peers:
            pl.semaphore_signal(barrier, inc=1, device_id=peer, device_id_type=MESH)
        pl.semaphore_wait(barrier, len(peers))


class Wire:
    def __init__(self, send, recv):
        self.send, self.recv, self.sent, self.count = send, recv, [], 0

    def take(self, number):
        self.count += number
        return self.count - number

    def plan(self, src, dst, peer, send, recv):
        return pltpu.make_async_remote_copy(
            src_ref=src, dst_ref=dst, send_sem=self.send.at[send], recv_sem=self.recv.at[recv],
            device_id=peer, device_id_type=MESH,
        )

    def __call__(self, src, dst, peer):
        k = self.take(1)
        copy = self.plan(src, dst, peer, k, k)
        copy.start()
        self.sent.append(copy)
        return copy

    def settle(self):
        for copy in self.sent:
            copy.wait_send()
        self.sent = []


class Rows:
    def __init__(self, here, wire, buf, rows, part, parts):
        self.here, self.wire, self.buf = here, wire, buf
        self.rows, self.size = rows, rows // parts
        self.shift = part * self.size

    def at(self, t):
        return self.buf.at[pl.ds(pl.multiple_of(t * self.rows + self.shift, 16), self.size)]

    def start(self):
        mine = self.at(self.here.t)
        self.far = self.wire(mine, mine, self.here.side)
        self.near = self.wire(mine, mine, self.here.core)

    def forward(self):
        self.far.wait_recv()
        theirs = self.at(2 * (1 - self.here.x) + self.here.c)
        self.last = self.wire(theirs, theirs, self.here.core)

    def finish(self):
        self.near.wait_recv()
        self.last.wait_recv()


class Sums:
    def __init__(self, here, wire, src, landed, out, back, rows, part, parts):
        self.here, self.wire, self.src = here, wire, src
        self.landed, self.out, self.back = landed, out, back
        self.rows, self.size = rows, rows // parts
        self.shift = part * self.size
        self.part = part

    def at(self, t):
        return pl.ds(pl.multiple_of(t * self.rows + self.shift, 16), self.size)

    def start(self):
        h = self.here
        self.copies = []
        for slot, x in ((0, 1 - h.x), (1, h.x)):
            src = self.src.at[self.at(2 * x + 1 - h.c)]
            self.copies.append(self.wire(src, self.landed.at[slot, self.part], h.core))

    def cross(self):
        h = self.here
        self.copies[0].wait_recv()
        mine = self.src[self.at(2 * (1 - h.x) + h.c)].astype(F32)
        self.out[self.part] = (mine + self.landed[0, self.part].astype(F32)).astype(BF)
        self.last = self.wire(self.out.at[self.part], self.back.at[self.part], h.side)

    def total(self):
        h = self.here
        self.copies[1].wait_recv()
        near = self.src[self.at(2 * h.x + h.c)].astype(F32) + self.landed[1, self.part].astype(F32)
        self.last.wait_recv()
        return near + self.back[self.part].astype(F32)


class Weights:
    def __init__(self, here, wire, own_sem, sources, target):
        self.here, self.wire, self.own_sem = here, wire, own_sem
        self.sources, self.target = sources, target
        self.over, self.own, self.z, self.far = {}, {}, {}, {}

    def at(self, p, z):
        rows = self.sources[p].shape[0]
        if p in Y_FIRST:
            return self.target(p, pl.ds(pl.multiple_of(2 * z * rows, 16), 2 * rows))
        return self.target(p, pl.ds(pl.multiple_of((2 * z + self.here.y) * rows, 16), rows))

    def start(self, p):
        h, src = self.here, self.sources[p]
        rows = src.shape[0]
        dst = self.target(p, pl.ds(pl.multiple_of(h.d * rows, 16), rows))
        self.own[p] = pltpu.make_async_copy(src, dst, self.own_sem.at[p])
        self.own[p].start()
        if p not in Y_FIRST:
            self.spread(p, src)
        self.over[p] = [self.wire(src, dst, h.over)]

    def pairs(self, p):
        self.over[p][0].wait_recv()
        self.own[p].wait()
        self.spread(p, self.at(p, self.here.z))

    def spread(self, p, src):
        h, wire = self.here, self.wire
        dst = self.at(p, h.z)
        k = wire.take(5)
        end = jnp.where(h.middle, 0, 1)
        near = wire.plan(src, dst, h.pair, k, k)
        far = wire.plan(src, dst, h.far_mid, k + 1, k + 1 + end)
        near.start()
        far.start()
        relays = []
        for j, z in ((1, h.mid_z), (2, h.end_z)):
            block = self.at(p, z)
            relays.append(wire.plan(block, block, h.pair, k + 2 + j, k + j))
        self.z[p] = [near] + relays
        self.far[p] = far

    def forward(self, p):
        h = self.here
        near, *relays = self.z[p]
        for copy, z in zip(self.z[p], h.order[1:]):
            copy.wait_recv()
            if copy is not near:
                pl.when(h.middle)(copy.start)
            if p not in Y_FIRST:
                block = self.at(p, z)
                self.over[p].append(self.wire(block, block, h.over))

    def finish(self, p):
        if p in Y_FIRST:
            return
        for copy in self.over[p]:
            copy.wait_recv()
        self.own[p].wait()

    def release(self, p):
        for copy in [self.z[p][0], self.far[p]] + self.over[p]:
            copy.wait_send()
        for copy in self.z[p][1:]:
            pl.when(self.here.middle)(copy.wait_send)


def normed(values, gain):
    inverse = lax.rsqrt(jnp.mean(values * values, axis=-1, keepdims=True) + EPSILON)
    return values * inverse * gain


class Reduce:
    def __init__(self, here, wire, freed, mine, other, y_land, e_land, z_land):
        self.here, self.wire = here, wire
        self.freed, self.last_mine, self.last_other = freed, mine, other
        self.y_land, self.e_land, self.z_land = y_land, e_land, z_land
        self.y, self.legs = {}, {}

    def mine(self, q, k, count=1):
        return self.part(q, k, count, 0)

    def other(self, q, k, count=1):
        return self.part(q, k, count, 4)

    def part(self, q, k, count, side):
        rows = self.freed.shape[1] // 8
        if q == 2 * E:
            ref = self.last_other if side else self.last_mine
            return ref.at[pl.ds(k * rows, count * rows)]
        return self.freed.at[q, pl.ds((side + k) * rows, count * rows)]

    def store(self, q, acc, shard):
        h = self.here
        for k, z in enumerate(h.order):
            for side, target in ((h.y, self.mine(q, k)), (1 - h.y, self.other(q, k))):
                at = pl.ds(pl.multiple_of((2 * z + side) * shard, 16), shard)
                target[...] = acc[at, : target.shape[1]].astype(BF)

    def start(self, q):
        if q in Z_FIRST:
            self.leg(q, [self.mine(q, k) for k in range(4)])
            self.leg(Z_FIRST[q], [self.other(q, k) for k in range(4)])
        else:
            self.y[q] = self.wire(self.other(q, 0, 4), self.y_land.at[q], self.here.over)

    def y_block(self, q, k):
        rows = self.freed.shape[1] // 8
        return self.y_land.at[q, pl.ds(k * rows, rows)]

    def arrive(self, q):
        self.y[q].wait_recv()
        for k in range(4):
            own = self.mine(q, k)
            own[...] = (own[...].astype(F32) + self.y_block(q, k)[...].astype(F32)).astype(BF)
        self.leg(q, [self.mine(q, k) for k in range(4)])

    def leg(self, j, blocks):
        h, wire = self.here, self.wire
        k = wire.take(5)
        near = wire.plan(blocks[1], self.z_land.at[j, 0], h.pair, k, k)
        hand = [
            wire.plan(blocks[2 + i], self.e_land.at[j, i], h.pair, k + 1 + i, k + 2 + i)
            for i in range(2)
        ]
        on = [
            wire.plan(blocks[2 + i], self.z_land.at[j, 1], peer, k + 3 + i, k + 1)
            for i, peer in enumerate((h.far_mid, h.far_end))
        ]

        @pl.when(jnp.logical_not(h.middle))
        def _():
            for copy in hand:
                copy.start()

        near.start()
        self.legs[j] = (blocks, near, hand, on)

    def relay(self, j):
        blocks, _, hand, on = self.legs[j]

        @pl.when(self.here.middle)
        def _():
            for copy in hand:
                copy.wait_recv()
            for i in range(2):
                both = blocks[2 + i][...].astype(F32) + self.e_land[j, i].astype(F32)
                blocks[2 + i][...] = both.astype(BF)
                on[i].start()

    def along_z(self, j):
        blocks, near, _, on = self.legs[j]
        near.wait_recv()
        on[0].wait_recv()
        both = self.z_land[j, 0].astype(F32) + self.z_land[j, 1].astype(F32)
        return blocks[0][...].astype(F32) + both

    def cross(self, q):
        own = self.other(q, 0)
        own[...] = self.along_z(Z_FIRST[q]).astype(BF)
        self.y[q] = self.wire(own, self.y_block(q, 0), self.here.over)

    def total(self, q):
        result = self.along_z(q)
        if q in Z_FIRST:
            self.y[q].wait_recv()
            result = result + self.y_block(q, 0)[...].astype(F32)
        return result

    def close(self):
        self.wire.settle()
        for _, near, hand, on in self.legs.values():
            near.wait_send()
            for copy in on:
                pl.when(self.here.middle)(copy.wait_send)
            for copy in hand:
                pl.when(jnp.logical_not(self.here.middle))(copy.wait_send)


class SmallSum:
    def __init__(self, here, wire, value, land):
        self.here, self.wire, self.value, self.land = here, wire, value, land

    def start(self, step):
        h, wire, land = self.here, self.wire, self.land
        if step < 3:
            peer = (h.core, h.side, h.over)[step]
            land[2 * step] = self.value[...]
            self.copy = wire(land.at[2 * step], land.at[2 * step + 1], peer)
            return
        land[6 + h.z] = self.value[...]
        self.k = wire.take(3)
        own = land.at[6 + h.z]
        for i, peer in enumerate((h.pair, h.far_mid, h.far_end)):
            back = self.k if i == 0 else self.k + 1 + jnp.where(h.middle, 0, 1)
            copy = wire.plan(own, own, peer, self.k + i, back)
            copy.start()
            wire.sent.append(copy)

    def finish(self, step):
        h, land = self.here, self.land
        if step < 3:
            self.copy.wait_recv()
            self.value[...] += land[2 * step + 1]
            return
        own = land.at[6 + h.z]
        for i, z in enumerate(h.order[1:]):
            self.wire.plan(own, land.at[6 + z], h.pair, self.k + i, self.k + i).wait_recv()
        self.value[...] = (land[6] + land[7]) + (land[8] + land[9])


class Results:
    def __init__(self, s, reduce, width):
        self.s, self.reduce, self.width, self.moves = s, reduce, width, []

    def put(self, q):
        s, width = self.s, self.width
        total = self.reduce.total(q)
        if q == 2 * E:
            s.grad_q[...] = total[:, :width]
            s.grad_k[...] = total[:, width : 2 * width]
            s.grad_v[...] = total[:, 2 * width : 3 * width]
            s.grad_o[...] = jnp.transpose(total[:, 3 * width :])
            return
        slot = len(self.moves) % 2
        if len(self.moves) >= 2:
            self.moves[-2].wait()
        s.held[slot] = total
        target = (s.grad_inner, s.grad_outer)[q % 2].at[q // 2]
        self.moves.append(pltpu.make_async_copy(s.held.at[slot], target, s.local_sem.at[slot]))
        self.moves[-1].start()

    def close(self):
        for move in self.moves[-2:]:
            move.wait()


def norm_back(values, gain, d_normed):
    inverse = lax.rsqrt(jnp.mean(values * values, axis=-1, keepdims=True) + EPSILON)
    scaled = d_normed * gain
    inner = jnp.mean(scaled * values, axis=-1, keepdims=True)
    grad = inverse * scaled - values * (inverse * inverse * inverse * inner)
    return grad, jnp.sum(d_normed * values * inverse, axis=0, keepdims=True)


def gate_parts(normed_rows, router, route):
    logits = nt(normed_rows, router)
    raised = jnp.exp(logits - jnp.max(logits, axis=1, keepdims=True))
    probs = raised / jnp.sum(raised, axis=1, keepdims=True)
    chosen = jnp.where(route == iota(logits.shape, 1), 1.0, 0.0)
    return probs, chosen, jnp.sum(probs * chosen, axis=1, keepdims=True)


def expert_dense(e, w, s, route_ref):
    model = s.x_rows.shape[1]

    @pl.loop(0, s.x_rows.shape[0] // ROWS)
    def _(t):
        at = pl.ds(pl.multiple_of(t * ROWS, ROWS), ROWS)
        here = route_ref[at, 0:1] == e
        inner = nn(s.x_rows[at], w[0][...])
        cubic = 0.044715 * inner * inner
        tanh = jnp.tanh(math.sqrt(2.0 / math.pi) * inner * (1.0 + cubic))
        half = 0.5 * (1.0 + tanh)
        active = jnp.where(here, inner * half, 0.0).astype(BF)
        slope = half + (0.5 * math.sqrt(2.0 / math.pi)) * inner * (1.0 - tanh * tanh) * (
            1.0 + 3.0 * cubic
        )
        d_inner = jnp.where(here, nn(s.d_rows[at], w[1][...]) * slope, 0.0).astype(BF)
        s.active[at] = active
        s.d_inner[at] = d_inner
        out = nt(active, w[1][...]).astype(BF)
        d_x = nt(d_inner, w[0][...]).astype(BF)
        if e == 0:
            s.terms[at, :model] = out
            s.terms[at, model:] = d_x
        else:
            s.terms[at, :model] = jnp.where(here, out, s.terms[at, :model])
            s.terms[at, model:] = jnp.where(here, d_x, s.terms[at, model:])


def layer_kernel(heads, names, *refs):
    s = Names()
    for name, ref in zip(names, refs):
        setattr(s, name, ref)
    h = Here()
    width = heads * HD
    seq, model = s.attn_rows.shape
    rows = s.tokens.shape[0]
    half = rows // 2
    shard = s.wq.shape[0]
    wire = Wire(s.t_send, s.t_recv)
    split = model // 2
    sources = [s.attn_shard.at[0]]
    for e in range(E):
        sources += [s.w_in.at[e], s.w_out.at[e]]
    sources += [s.attn_shard.at[1]]

    def target(p, at):
        if p in (0, LAST):
            return s.w_attn.at[at, pl.ds(split if p else 0, split)]
        return s.experts.at[p - 1, at]

    weights = Weights(h, Wire(s.w_send, s.w_recv), s.own_sem, sources, target)
    reduce = Reduce(
        h, Wire(s.g_send, s.g_recv), s.experts, s.mine, s.other, s.y_land, s.e_land, s.z_land,
    )
    results = Results(s, reduce, width)
    row_id = iota((8, model), 0)

    def block(part):
        return pl.ds(pl.multiple_of(h.t * rows + part * half, 16), half)

    def span(part):
        return slice(part * half, (part + 1) * half)

    def norm_rows(part):
        s.attn_rows[block(part)] = normed(s.tokens[span(part)], gain_a).astype(BF)

    def fill_first():
        segments = s.segments[...]
        first = jnp.zeros(segments.shape, jnp.int32)
        for seg in range(1, 5):
            first = jnp.where(segments >= seg, jnp.sum(jnp.where(segments < seg, 1, 0)), first)
        s.first[...] = jnp.broadcast_to(first, s.first.shape)

    def norm_attended(part, total, gather):
        attended = s.tokens[span(part)] + total.total()
        s.grad_tokens[span(part)] = attended
        s.x_rows[block(part)] = normed(attended, gain_f).astype(BF)
        gather.start()

    def run_expert(e):
        expert_dense(e, (s.experts.at[2 * e], s.experts.at[2 * e + 1]), s, s.route_col)
        weights.release(2 * e + 1)
        weights.release(2 * e + 2)
        s.acc[:, :model] = nn(s.x_t[...], s.d_inner[...])
        reduce.store(2 * e, s.acc, shard)
        s.acc[:, :model] = nn(s.d_t[...], s.active[...])
        reduce.store(2 * e + 1, s.acc, shard)

    def expert_back(part, total, gather):
        router_rows = s.router[...].astype(F32)
        attended, cot = s.grad_tokens[span(part)], s.cot[span(part)]
        expert_out, d_normed = total[:, :model], total[:, model:]
        ffn = normed(attended, gain_f).astype(BF)
        route = s.route_col[block(part), 0:1]
        probs, chosen, gate = gate_parts(ffn, s.router[...], route)
        s.output[span(part)] = attended + gate * expert_out
        d_gate = jnp.sum(cot * expert_out, axis=1, keepdims=True)
        d_logits = d_gate * gate * (chosen - probs)
        small = s.small[...]
        for e in range(E):
            d_normed = d_normed + d_logits[:, e : e + 1] * router_rows[e : e + 1]
            grad = jnp.sum(d_logits[:, e : e + 1] * ffn.astype(F32), axis=0, keepdims=True)
            small = small + jnp.where(row_id == 2 + e, grad, 0.0)
        back, gain_grad = norm_back(attended, gain_f, d_normed)
        s.small[...] = small + jnp.where(row_id == 1, gain_grad, 0.0)
        d_attended = cot + back
        s.grad_tokens[span(part)] = d_attended
        s.x_rows[block(part)] = d_attended.astype(BF)
        gather.start()

    def keep_lines():
        flat = jnp.concatenate(diagonal_lines(heads, s.near), axis=1)
        places = jnp.concatenate([flat, flat], axis=1)
        lane = iota((8, model), 1) // flat.shape[1]
        mine = (row_id == 6 + h.t // 2) & (lane == h.t % 2)
        s.small[...] += jnp.where(mine, places, 0.0)

    def first_norm_back(part, total):
        back, gain_grad = norm_back(s.tokens[span(part)], gain_a, total)
        s.grad_tokens[span(part)] += back
        s.small[...] += jnp.where(row_id == 0, gain_grad, 0.0)

    s.attn_shard[0, :, :width] = s.wq[...]
    s.attn_shard[0, :, width:] = s.wk[...]
    s.attn_shard[1, :, :width] = s.wv[...]
    s.attn_shard[1, :, width:] = jnp.transpose(s.wo[...])
    h.greet()
    weights.start(LAST)

    gathers = [Rows(h, wire, s.attn_rows, rows, part, 2) for part in range(2)]
    gain_a = s.gain_a[...].astype(F32).reshape(1, model)
    norm_rows(0)
    gathers[0].start()
    weights.start(0)
    norm_rows(1)
    gathers[1].start()
    weights.pairs(LAST)
    s.d_rows[pl.ds(pl.multiple_of(h.t * rows, 16), rows)] = s.cot[...].astype(BF)
    s.tab[...] = s.table[...].astype(F32)
    fill_bias(s.bias, s.far, [s.tab[pl.ds(h.t * heads + hd, 1), :] for hd in range(heads)])
    s.route_col[...] = jnp.transpose(
        jnp.broadcast_to(s.routes[...].astype(F32), (8, seq))
    ).astype(jnp.int32)
    fill_first()
    weights.start(1)
    gathers[0].forward()
    weights.forward(0)
    gathers[1].forward()
    gathers[0].finish()
    gathers[1].finish()
    weights.start(2)
    weights.start(6)
    weights.start(8)
    cots = Rows(h, wire, s.d_rows, rows, 0, 1)
    cots.start()
    weights.forward(LAST)
    weights.finish(0)
    weights.finish(LAST)

    project(heads, s.attn_rows[...], s.w_attn, s.qkv, s.q_t, s.v_t, s.kn)
    state = (s.first, s.q_t, s.v_t, s.kn, s.bias, s.far, s.acc, s.ctx_t, s.lse)
    weights.start(3)
    attend_blocks(heads, *state, range(0, 3))
    attend_blocks(heads, *state, range(3, seq // QT))
    s.ctx[...] = jnp.transpose(s.ctx_t[...])
    s.branch[...] = nt(s.ctx[...], s.w_attn[:, 3 * width :]).astype(BF)
    narrow = [s.landed.at[:, :, :, :model], s.out.at[:, :, :model], s.back.at[:, :, :model]]
    sums = [Sums(h, wire, s.branch, *narrow, rows, part, 2) for part in range(2)]
    sums[0].start()
    sums[1].start()
    weights.start(4)
    sums[0].cross()
    sums[1].cross()
    weights.forward(2)
    cots.forward()
    weights.start(5)

    gathers = [Rows(h, wire, s.x_rows, rows, part, 2) for part in range(2)]
    gain_f = s.gain_f[...].astype(F32).reshape(1, model)
    norm_attended(0, sums[0], gathers[0])
    weights.forward(1)
    norm_attended(1, sums[1], gathers[1])
    gathers[0].forward()
    weights.forward(3)
    gathers[1].forward()
    weights.pairs(8)
    cots.finish()
    gathers[0].finish()
    gathers[1].finish()
    weights.forward(4)
    wire.settle()
    gate = gate_parts(s.x_rows[...], s.router[...], s.route_col[:, 0:1])[2]
    s.d_rows[...] = (s.d_rows[...].astype(F32) * gate).astype(BF)
    s.x_t[...] = jnp.transpose(s.x_rows[...])
    s.d_t[...] = jnp.transpose(s.d_rows[...])

    weights.finish(1)
    weights.finish(2)
    run_expert(0)
    weights.start(7)
    weights.forward(5)
    weights.forward(6)
    weights.finish(3)
    reduce.start(0)
    weights.finish(4)
    run_expert(1)
    weights.forward(7)
    weights.forward(8)
    weights.finish(5)
    weights.finish(6)
    reduce.start(3)
    reduce.start(2)
    run_expert(2)
    weights.finish(7)
    weights.finish(8)
    run_expert(3)
    reduce.relay(Z_FIRST[0])

    s.small[...] = jnp.zeros_like(s.small)
    sums = [
        Sums(h, wire, s.terms, s.landed, s.out, s.back, rows, part, 2) for part in range(2)
    ]
    sums[0].start()
    sums[1].start()
    reduce.start(5)
    reduce.arrive(2)
    sums[0].cross()
    reduce.relay(0)
    sums[1].cross()
    reduce.start(1)
    reduce.start(4)
    gathers = [Rows(h, wire, s.x_rows, rows, part, 2) for part in range(2)]
    expert_back(0, sums[0].total(), gathers[0])
    reduce.start(6)
    reduce.relay(3)
    expert_back(1, sums[1].total(), gathers[1])
    reduce.arrive(4)
    reduce.start(7)
    reduce.relay(Z_FIRST[3])
    gathers[0].forward()
    gathers[1].forward()
    gathers[0].finish()
    gathers[1].finish()
    reduce.relay(1)
    reduce.arrive(5)

    scale = jnp.asarray(1.0 / math.sqrt(HD), BF)
    d_ctx = nn(s.x_rows[...], s.w_attn[:, 3 * width :]).astype(BF)
    d_ctx_t = jnp.transpose(d_ctx)
    s.dc_t[...] = d_ctx_t
    s.k_t[...] = jnp.transpose(s.qkv[:, width : 2 * width])
    product = d_ctx_t.astype(F32) * s.ctx_t[...].astype(F32)
    for hd in range(heads):
        band = slice(hd * HD, (hd + 1) * HD)
        s.qn[hd] = s.qkv[:, band] * scale
        s.vn[hd] = s.qkv[:, 2 * width + hd * HD : 2 * width + (hd + 1) * HD]
        s.dcn[hd] = d_ctx[:, band]
        s.delta[hd : hd + 1] = jnp.sum(product[band], axis=0, keepdims=True)
    s.dq_t[...] = jnp.zeros_like(s.dq_t)
    s.near[...] = jnp.zeros_like(s.near)
    attend_back_block(heads, s, 0, seq)
    reduce.relay(2)
    reduce.relay(4)
    for j in range(1, seq // QT):
        attend_back_block(heads, s, j, seq)
    wire.settle()
    s.dqkv[:, :width] = jnp.transpose((s.dq_t[...] * (1.0 / math.sqrt(HD))).astype(BF))
    s.branch[...] = nt(s.dqkv[...], s.w_attn[:, : 3 * width]).astype(BF)
    sums = [Sums(h, wire, s.branch, *narrow, rows, part, 2) for part in range(2)]
    sums[0].start()
    sums[1].start()
    reduce.relay(5)
    reduce.relay(Z_FIRST[1])
    reduce.arrive(6)
    reduce.cross(0)
    s.acc[:, : 3 * width] = tn(s.attn_rows[...], s.dqkv[...])
    s.acc[:, 3 * width : model] = tn(s.x_rows[...], s.ctx[...])
    reduce.store(2 * E, s.acc, shard)
    reduce.start(8)
    sums[0].cross()
    sums[1].cross()
    reduce.relay(6)
    results.put(2)
    results.put(4)
    keep_lines()
    reduce.arrive(7)
    results.put(0)
    reduce.relay(7)

    first_norm_back(0, sums[0].total())
    reduce.arrive(8)
    reduce.cross(1)
    first_norm_back(1, sums[1].total())
    reduce.cross(3)
    everywhere = SmallSum(h, wire, s.small, s.small_land)
    everywhere.start(0)
    results.put(6)
    reduce.relay(8)
    everywhere.finish(0)
    everywhere.start(1)
    results.put(3)
    everywhere.finish(1)
    results.put(1)
    everywhere.start(2)
    everywhere.finish(2)
    results.put(7)
    everywhere.start(3)
    results.put(5)
    results.put(8)
    everywhere.finish(3)
    results.close()
    wire.settle()
    weights.release(0)
    weights.release(LAST)
    reduce.close()


def layer(table, tokens, cot, segments, routes, gain_a, gain_f, router, wq, wk, wv, wo, w_in, w_out):
    rows, model = tokens.shape
    seq = segments.shape[1]
    shard, width = wq.shape
    heads = width // HD
    hidden = w_in.shape[2]
    vmem = pl.BlockSpec(memory_space=pltpu.VMEM)
    hbm = pl.BlockSpec(memory_space=pl.ANY)
    ins = [
        ("table", table, vmem), ("tokens", tokens, vmem), ("cot", cot, vmem),
        ("segments", segments, vmem), ("routes", routes, vmem), ("gain_a", gain_a, vmem),
        ("gain_f", gain_f, vmem), ("router", router, vmem), ("wq", wq, vmem), ("wk", wk, vmem),
        ("wv", wv, vmem), ("wo", wo, vmem), ("w_in", w_in, hbm), ("w_out", w_out, hbm),
    ]
    outs = [
        ("output", (rows, model), F32, vmem),
        ("grad_tokens", (rows, model), F32, vmem),
        ("grad_q", (shard, width), F32, vmem),
        ("grad_k", (shard, width), F32, vmem),
        ("grad_v", (shard, width), F32, vmem),
        ("grad_o", (width, shard), F32, vmem),
        ("small", (8, model), F32, vmem),
        ("grad_inner", (E, shard, hidden), F32, hbm),
        ("grad_outer", (E, shard, hidden), F32, hbm),
    ]
    scratch = [
        ("attn_shard", (2, shard, 2 * width), BF),
        ("attn_rows", (seq, model), BF),
        ("qkv", (seq, 3 * width), BF),
        ("ctx", (seq, width), BF),
        ("lse", (8, seq), F32),
        ("delta", (8, seq), F32),
        ("w_attn", (model, 4 * width), BF),
        ("first", (8, seq), jnp.int32),
        ("x_rows", (seq, model), BF),
        ("d_rows", (seq, model), BF),
        ("x_t", (model, seq), BF),
        ("d_t", (model, seq), BF),
        ("active", (seq, hidden), BF),
        ("d_inner", (seq, hidden), BF),
        ("terms", (seq, 2 * model), BF),
        ("experts", (2 * E, model, hidden), BF),
        ("acc", (heads * QT, seq), F32),
        ("q_t", (width, seq), BF),
        ("k_t", (width, seq), BF),
        ("v_t", (width, seq), BF),
        ("dc_t", (width, seq), BF),
        ("ctx_t", (width, seq), BF),
        ("kn", (heads, seq, HD), BF),
        ("vn", (heads, seq, HD), BF),
        ("qn", (heads, seq, HD), BF),
        ("dcn", (heads, seq, HD), BF),
        ("bias", (heads, 2, HALF, HALF), F32),
        ("far", (8, QT), F32),
        ("tab", table.shape, F32),
        ("route_col", (seq, 8), jnp.int32),
        ("near", (heads, 2, HALF, HALF), F32),
        ("dq_t", (width, seq), F32),
        ("dqkv", (seq, 3 * width), BF),
        ("branch", (seq, model), BF),
        ("landed", (2, 2, rows // 2, 2 * model), BF),
        ("out", (2, rows // 2, 2 * model), BF),
        ("back", (2, rows // 2, 2 * model), BF),
        ("mine", (4 * shard, model), BF),
        ("other", (4 * shard, model), BF),
        ("y_land", (2 * E + 1, 4 * shard, model), BF),
        ("z_land", (LEGS, 2, shard, model), BF),
        ("e_land", (LEGS, 2, shard, model), BF),
        ("held", (2, shard, hidden), F32),
        ("small_land", (10, 8, model), F32),
    ]
    sems = [
        ("t_send", T_SEMS), ("t_recv", T_SEMS), ("w_send", W_SEMS), ("w_recv", W_SEMS),
        ("g_send", G_SEMS), ("g_recv", G_SEMS), ("own_sem", PIECES), ("local_sem", 2),
    ]
    names = [i[0] for i in ins] + [o[0] for o in outs] + [c[0] for c in scratch]
    names += [c[0] for c in sems]
    return pl.pallas_call(
        functools.partial(layer_kernel, heads, names),
        out_shape=tuple(jax.ShapeDtypeStruct(o[1], o[2]) for o in outs),
        in_specs=[i[2] for i in ins],
        out_specs=tuple(o[3] for o in outs),
        scratch_shapes=[pltpu.VMEM(c[1], c[2]) for c in scratch]
        + [pltpu.SemaphoreType.DMA((c[1],)) for c in sems],
        compiler_params=pltpu.CompilerParams(
            vmem_limit_bytes=VMEM_MAX, collective_id=1, has_side_effects=True
        ),
        cost_estimate=pl.CostEstimate(flops=4 * 10**10, bytes_accessed=10**8, transcendentals=10**7),
        name="layer",
    )(*[i[1] for i in ins])


def rms_apply(values, gain_vec):
    inverse = lax.rsqrt(jnp.mean(values * values, axis=-1, keepdims=True) + EPSILON)
    return values * inverse * gain_vec


def finish_kernel(heads_all, copies, *refs):
    small = refs[0]
    srcs, outs = refs[1 : 1 + copies], refs[1 + copies : 1 + 2 * copies]
    gain_a, gain_f, router, table = refs[1 + 2 * copies : 5 + 2 * copies]
    held, sem = refs[5 + 2 * copies : -1], refs[-1]
    loads = [pltpu.make_async_copy(a, v, sem.at[0, k]) for k, (a, v) in enumerate(zip(srcs, held))]
    moves = [pltpu.make_async_copy(v, b, sem.at[1, k]) for k, (v, b) in enumerate(zip(held, outs))]
    for load in loads:
        load.start()
    model = small.shape[1]
    gain_a[...] = small[0:1].reshape(model)
    gain_f[...] = small[1:2].reshape(model)
    router[...] = small[2 : 2 + E]
    per_row = model // HALF
    lines = [
        small[6 + k // per_row : 7 + k // per_row, (k % per_row) * HALF : (k % per_row + 1) * HALF]
        for k in range(heads_all)
    ]
    distance, bucket = iota((HALF, NBKT), 0), iota((HALF, NBKT), 1)
    pick = jnp.zeros((HALF, NBKT), F32)
    for b in range(NBKT - 1):
        inside = (distance >= FIRST[b]) & (distance < FIRST[b + 1]) & (bucket == b)
        pick = jnp.where(inside, 1.0, pick)
    pick = jnp.where((distance < NEAR) & (bucket == NBKT - 1), -1.0, pick)
    table[...] = lax.dot_general(
        jnp.concatenate(lines, axis=0), pick, (((1,), (0,)), ((), ())),
        precision=lax.Precision.HIGHEST, preferred_element_type=F32,
    )
    for load, move in zip(loads, moves):
        load.wait()
        move.start()
    for move in moves:
        move.wait()


def finish(small, arrays, heads_all):
    model = small.shape[1]
    vmem = pl.BlockSpec(memory_space=pltpu.VMEM)
    hbm = pl.BlockSpec(memory_space=pl.ANY)
    n = len(arrays)
    return pl.pallas_call(
        functools.partial(finish_kernel, heads_all, n),
        out_shape=tuple(jax.ShapeDtypeStruct(a.shape, a.dtype) for a in arrays)
        + (
            jax.ShapeDtypeStruct((model,), F32),
            jax.ShapeDtypeStruct((model,), F32),
            jax.ShapeDtypeStruct((E, model), F32),
            jax.ShapeDtypeStruct((heads_all, NBKT), F32),
        ),
        in_specs=[vmem] + [hbm] * n,
        out_specs=(hbm,) * n + (vmem,) * 4,
        scratch_shapes=[pltpu.VMEM(a.shape, a.dtype) for a in arrays]
        + [pltpu.SemaphoreType.DMA((2, n))],
        compiler_params=pltpu.CompilerParams(vmem_limit_bytes=VMEM_MAX),
        cost_estimate=pl.CostEstimate(flops=10**6, bytes_accessed=10**7, transcendentals=0),
        name="finish",
    )(small, *arrays)


def table_grad(diag):
    onehot = jnp.asarray((BUCKETS[:HALF, None] == np.arange(NBKT - 1)[None, :]).astype(np.float32))
    near_sums = jnp.dot(onehot.T, diag.T, precision=lax.Precision.HIGHEST)
    return jnp.concatenate([near_sums, -jnp.sum(near_sums, axis=0, keepdims=True)], axis=0)


def per_device_grid(
    tokens, segments, routes, cotangent, gain_attn, w_query, w_key, w_value, w_output, rel_table,
    gain_ffn, w_router, w_inner, w_outer,
):
    out = layer(
        jnp.transpose(rel_table), tokens, cotangent, segments[None, :], jnp.transpose(routes),
        gain_attn, gain_ffn, jnp.transpose(w_router), w_query, w_key, w_value, w_output, w_inner,
        jnp.transpose(w_outer, (0, 2, 1)),
    )
    small = out[6]
    done = finish(small, [*out[:6], out[7], out[8]], rel_table.shape[1])
    output, grad_tokens, grad_q, grad_k, grad_v, grad_o, grad_inner, grad_outer = done[:8]
    gain_a, gain_f, grad_router, grad_table = done[8:]
    return (
        output, grad_tokens, gain_a, grad_q, grad_k, grad_v, grad_o, jnp.transpose(grad_table),
        gain_f, jnp.transpose(grad_router), grad_inner, jnp.transpose(grad_outer, (0, 2, 1)),
    )


def per_device(
    tokens, segments, routes, cotangent, gain_attn, w_query, w_key, w_value, w_output, rel_table,
    gain_ffn, w_router, w_inner, w_outer,
):
    part_index = lax.axis_index("tensor")
    rows_local, model = tokens.shape
    seq_len = segments.shape[0]
    width = w_query.shape[1]
    heads = width // HD
    all_heads = rel_table.shape[1]
    hidden = w_inner.shape[2]

    attn_shard = jnp.concatenate([w_query, w_key, w_value, jnp.transpose(w_output)], axis=1)
    w_attn = gather_dp(attn_shard)
    both_shard = jnp.concatenate([w_inner, jnp.transpose(w_outer, (0, 2, 1))], axis=2)
    w_experts = [gather_dp(both_shard[e]) for e in range(E)]
    offs = jnp.zeros((1,), jnp.int32)
    slot_row, slot_col, plan = make_plan(jnp.reshape(routes, (1, seq_len)))
    counts = [jnp.sum((segments < s).astype(jnp.int32)) for s in range(1, 5)]
    first_key = jnp.zeros_like(segments)
    for s in range(1, 5):
        first_key = jnp.where(segments >= s, counts[s - 1], first_key)
    first_key = first_key[None, :]
    table = jnp.transpose(
        lax.dynamic_slice_in_dim(rel_table.astype(F32), part_index * heads, heads, 1)
    )

    normed_attn, norm_one_pull = jax.vjp(rms_apply, tokens, gain_attn.astype(F32))
    attn_rows = lax.all_gather(normed_attn.astype(BF), "tensor", axis=0, tiled=True)
    qkv, ctx, lse, branch = attend(attn_rows, w_attn, table, first_key, heads)
    attended = tokens + lax.psum_scatter(
        branch, "tensor", scatter_dimension=0, tiled=True
    ).astype(F32)

    normed_ffn, norm_two_pull = jax.vjp(rms_apply, attended, gain_ffn.astype(F32))
    ffn_in = normed_ffn.astype(BF)
    local_routes = lax.dynamic_slice_in_dim(routes[:, 0], part_index * rows_local, rows_local, 0)
    route_mask = (local_routes[:, None] == jnp.arange(E, dtype=jnp.int32)[None, :]).astype(F32)

    def gate_of(normed_values, router_values):
        logits = jnp.dot(normed_values, router_values, precision=lax.Precision.HIGHEST)
        return jnp.sum(jax.nn.softmax(logits, axis=-1) * route_mask, axis=-1)

    gate_weight, gate_pull = jax.vjp(gate_of, ffn_in.astype(F32), w_router.astype(F32))
    d_expert = (cotangent * gate_weight[:, None]).astype(BF)
    xd = lax.all_gather(jnp.concatenate([ffn_in, d_expert], axis=1), "tensor", axis=0, tiled=True)

    terms = None
    expert_sums = []
    for e in range(E):
        terms, part = expert(e, plan, offs, xd, slot_row, slot_col, terms, w_experts[e])
        expert_sums.append(reduce_dp(part[0]))
    sums = lax.psum_scatter(terms, "tensor", scatter_dimension=0, tiled=True).astype(F32)
    expert_out, d_ffn_local = sums[:, :model], sums[:, model:]
    output = attended + gate_weight[:, None] * expert_out
    d_gate = jnp.sum(cotangent * expert_out, axis=-1)

    d_ffn_router, grad_router_local = gate_pull(d_gate)
    d_attended_norm, grad_gain_two = norm_two_pull(d_ffn_local + d_ffn_router)
    d_attended = cotangent + d_attended_norm
    d_branch_rows = lax.all_gather(d_attended.astype(BF), "tensor", axis=0, tiled=True)

    total_rows, diag, attn_part = attend_back(
        d_branch_rows, w_attn, qkv, ctx, lse, first_key, attn_rows, table, offs, heads
    )
    attn_sum = reduce_dp(attn_part[0])
    d_attn_local = lax.psum_scatter(
        total_rows, "tensor", scatter_dimension=0, tiled=True
    ).astype(F32)
    d_tokens_norm, grad_gain_one = norm_one_pull(d_attn_local)
    grad_tokens = d_attended + d_tokens_norm
    grad_table_full = lax.dynamic_update_slice_in_dim(
        jnp.zeros((NBKT, all_heads), F32), table_grad(diag[:heads]), part_index * heads, 1
    )
    small_sums = lax.psum(
        (grad_gain_one, grad_gain_two, grad_router_local, grad_table_full), ("dp", "tensor")
    )
    return (
        output,
        grad_tokens,
        small_sums[0],
        attn_sum[:, :width],
        attn_sum[:, width : 2 * width],
        attn_sum[:, 2 * width : 3 * width],
        jnp.transpose(attn_sum[:, 3 * width :]),
        small_sums[3],
        small_sums[1],
        small_sums[2],
        jnp.stack([part[:, :hidden] for part in expert_sums]),
        jnp.stack([jnp.transpose(part[:, hidden:]) for part in expert_sums]),
    )


def solution(mesh):
    sizes = dict(mesh.shape)
    in_specs = (
        P(("dp", "tensor"), None),
        P("dp"),
        P("dp", None),
        P(("dp", "tensor"), None),
        P(),
        P("dp", "tensor"),
        P("dp", "tensor"),
        P("dp", "tensor"),
        P("tensor", "dp"),
        P(),
        P(),
        P(),
        P(None, "dp", "tensor"),
        P(None, "tensor", "dp"),
    )
    out_specs = (
        P(("dp", "tensor"), None),
        P(("dp", "tensor"), None),
        P(),
        P("dp", "tensor"),
        P("dp", "tensor"),
        P("dp", "tensor"),
        P("tensor", "dp"),
        P(),
        P(),
        P(),
        P(None, "dp", "tensor"),
        P(None, "tensor", "dp"),
    )
    return jax.shard_map(
        per_device_grid if sizes["dp"] == 8 and sizes["tensor"] == 4 else per_device,
        mesh=mesh,
        in_specs=in_specs,
        out_specs=out_specs,
        check_vma=False,
    )
```
